32 devices in a mesh: gx: 4 (over z), gy: 4 (over y, core), band: 2 (over x).
Axes of the slice: x: 2, y: 2, z: 4, core: 2. Of those that a mesh axis runs over, the one named last changes fastest.
Arguments:
- orbitals: float32 [4, 128, 32, 256], P('band', 'gx', 'gy'), may hold values from -600 to 600
- potential: float32 [128, 32, 256], P('gx', 'gy'), may hold values from -0.5 to 0.5
- order: int32 [4], replicated, may hold values from 0 to 3, as said below
Outputs:
- basis: float32 [4, 128, 32, 256], P('band', 'gx', 'gy')
The draws below stay inside these ranges and needn't reach their ends.
Inputs may be any that keep to these rules, and one draw needn't show every extreme that they name: `order`: each orbital appears once; position p names the orbital orthonormalized p-th.
All inputs are finite; a program needn't handle non-finite values.
Results may differ from the reference program's by a relative error of at most 0.00026.
Values sent between devices are 32-bit elements; how exact they have to be, the bound alone decides.
No kernel may reach another device: no remote copies, remote signals or barrier semaphores. Data moves between devices by JAX's collectives and lax.ppermute only.
A program may use at most 64 MiB of HBM per device.

```python
import jax
import jax.numpy as jnp
from jax import lax

NZ = 256
DEGREE = 8
NX = 128
NY = 32
ORBS = 4


def draw_orbitals(key, part):
    keys = jax.random.split(key, 3)
    along_x = jnp.arange(NX, dtype=jnp.float32) / max(NX - 1, 1)
    along_y = jnp.arange(NY, dtype=jnp.float32) / max(NY - 1, 1)
    cell_scale = 10.0 ** (0.5 * (along_x[:, None] + along_y[None, :]))
    orbital_scale = 10.0 ** jax.random.uniform(keys[1], (ORBS,), jnp.float32)
    noise = jax.random.normal(keys[0], (ORBS, NX, NY, NZ), jnp.float32)
    shared = jax.random.normal(keys[2], (1, NX, NY, NZ), jnp.float32)
    values = jnp.clip(0.8 * noise + 0.6 * shared, -6.0, 6.0)
    return values * orbital_scale[:, None, None, None] * cell_scale[None, :, :, None]


def draw_order(key, part):
    return jax.random.permutation(jax.random.fold_in(key, 17), jnp.arange(ORBS, dtype=jnp.int32)).astype(jnp.int32)


def steps_of(own_key, dims, shards, smallest, high):
    def one(dim, blocks):
        draws = jax.random.uniform(jax.random.fold_in(jax.random.fold_in(own_key, 6), dim), (blocks,), jnp.float32, smallest / len(shards), high / len(shards))
        return jnp.repeat(jnp.exp(draws), dims[dim] // blocks).reshape((-1,) + (1,) * (len(dims) - dim - 1))

    level = one(*shards[0])
    for cut in shards[1:]:
        level = level * one(*cut)
    return level


def setup_inputs(seed: int = 0) -> dict:
    key_list = jax.random.split(jax.random.key(seed), 4)
    orbitals = draw_orbitals(jax.random.fold_in(key_list[3], 71), 0)
    potential = jnp.clip(jax.random.uniform(key_list[1], (NX, NY, NZ), jnp.float32, -0.5, 0.5) * steps_of(key_list[1], (NX, NY, NZ), ((0, 4), (1, 4)), -0.4, 0.0), -0.5, 0.5)
    order = draw_order(jax.random.fold_in(key_list[3], 71), 0)
    return {"orbitals": orbitals, "potential": potential, "order": order}


def apply_operator(extended, potential):
    middle = extended[:, 2:-2, 2:-2, :]
    padded_z = jnp.pad(middle, ((0, 0), (0, 0), (0, 0), (2, 2)))
    nearest = extended[:, 1:-3, 2:-2] + extended[:, 3:-1, 2:-2]
    nearest = nearest + extended[:, 2:-2, 1:-3] + extended[:, 2:-2, 3:-1]
    nearest = nearest + padded_z[..., 1:-3] + padded_z[..., 3:-1]
    distant = extended[:, :-4, 2:-2] + extended[:, 4:, 2:-2]
    distant = distant + extended[:, 2:-2, :-4] + extended[:, 2:-2, 4:]
    distant = distant + padded_z[..., :-4] + padded_z[..., 4:]
    applied = (3.75 + potential) * middle - nearest * (2.0 / 3.0) + distant / 24.0
    return (applied - 4.25 * middle) / 4.25

def widen(field):
    return jnp.pad(field, ((0, 0), (2, 2), (2, 2), (0, 0)))

def filter_one(field, potential):
    previous = field[None]
    current = apply_operator(widen(previous), potential)
    for repeat in range(DEGREE - 1):
        following = 2.0 * apply_operator(widen(current), potential) - previous
        previous, current = (current, following)
    return current[0]

def mixing_matrix(correlation, order):
    orbital_count = correlation.shape[0]
    positions = jnp.arange(orbital_count, dtype=jnp.int32)
    target = order.astype(jnp.int32)
    arrange = (target[:, None] == positions[None, :]).astype(jnp.float32)
    highest = lax.Precision.HIGHEST
    ordered = jnp.dot(jnp.dot(arrange, correlation, precision=highest), arrange.T, precision=highest)
    lower_factor = jnp.linalg.cholesky(ordered)
    inverse = jax.scipy.linalg.solve_triangular(lower_factor, jnp.eye(orbital_count, dtype=jnp.float32), lower=True)
    return jnp.dot(jnp.dot(arrange.T, inverse, precision=highest), arrange, precision=highest)

def reference(orbitals, potential, order):
    filtered = lax.map(lambda field: filter_one(field, potential), orbitals)
    flattened = filtered.reshape(ORBS, -1)
    correlation = jnp.dot(flattened.astype(jnp.float32), flattened.T.astype(jnp.float32), precision=lax.Precision.HIGHEST, preferred_element_type=jnp.float32) / float(NX * NY * NZ)
    mixing = mixing_matrix(correlation, order)
    basis = jnp.dot(mixing.astype(jnp.float32), flattened.astype(jnp.float32), precision=lax.Precision.HIGHEST, preferred_element_type=jnp.float32)
    return basis.reshape(orbitals.shape)
```

```python
import functools

import jax
import jax.numpy as jnp
from jax import lax
from jax.experimental import pallas as pl
from jax.experimental.pallas import tpu as pltpu
from jax.sharding import PartitionSpec as P

STEPS = 4
HALO = 2 * STEPS
PAD = 8
LANES = 128
PLANES = 4
NEAR = -(2.0 / 3.0) / 4.25
FAR = (1.0 / 24.0) / 4.25
VMEM = pl.BlockSpec(memory_space=pltpu.VMEM)
SMEM = pl.BlockSpec(memory_space=pltpu.SMEM)
PARAMS = pltpu.CompilerParams(vmem_limit_bytes=40 * 1024 * 1024)


def struct(*shape):
    return jax.ShapeDtypeStruct(shape, jnp.float32)


def place():
    along_y = lax.axis_index("gy")
    return along_y % 2, along_y // 2, lax.axis_index("gx")


def one_sided():
    return lax.axis_size("gy") == 4


def tile_count():
    return 3 if one_sided() else 4


def own_slots(core, chip):
    first = chip if one_sided() else 1
    return first + core, first + 1 - core


def halo_slots(chip):
    return [2 - 2 * chip] if one_sided() else [0, 3]


def rows_of(slot):
    return pl.ds(pl.multiple_of(PAD + 8 * slot, 8), 8)


def fill(window, tiles, x_left, x_right, y_halos, corners, core, chip, change=lambda a: a):
    width = tiles[0].shape[0]
    for half in range(2):
        lanes = slice(half * LANES, (half + 1) * LANES)
        for index, slot in enumerate(own_slots(core, chip)):
            rows = rows_of(slot)
            window[half, HALO : HALO + width, rows, :] = change(tiles[index][:, :, lanes])
            window[half, :HALO, rows, :] = change(x_left[index, :, :, lanes])
            window[half, HALO + width :, rows, :] = change(x_right[index, :, :, lanes])
        for slot, middle, (left, right) in zip(halo_slots(chip), y_halos, corners):
            rows = rows_of(slot)
            window[half, HALO : HALO + width, rows, :] = change(middle[:, :, lanes])
            window[half, :HALO, rows, :] = change(left[:, :, lanes])
            window[half, HALO + width :, rows, :] = change(right[:, :, lanes])


def z_matrix(depth):
    gap = jnp.abs(
        lax.broadcasted_iota(jnp.int32, (depth, depth), 0)
        - lax.broadcasted_iota(jnp.int32, (depth, depth), 1)
    )
    return jnp.where(gap == 1, -16.0, jnp.where(gap == 2, 1.0, 0.0)).astype(jnp.bfloat16)


def stencil(source, target, local, x, along_z, first):
    height = source.shape[2] - 2 * PAD
    body = slice(PAD, PAD + height)
    now = pl.ds(x, PLANES)
    values = [source[half, now, body, :] for half in range(2)]
    high = [v.astype(jnp.bfloat16) for v in values]
    low = [(v - h.astype(jnp.float32)).astype(jnp.bfloat16) for v, h in zip(values, high)]

    def joined(parts):
        return jnp.concatenate([p.reshape(PLANES * height, LANES) for p in parts], axis=1)

    z_sum = jnp.dot(joined(high), along_z, preferred_element_type=jnp.float32)
    z_sum = z_sum + jnp.dot(joined(low), along_z, preferred_element_type=jnp.float32)
    scale = 1.0 if first else 2.0
    for half in range(2):
        near = source[half, pl.ds(x - 1, PLANES), body, :] + source[half, pl.ds(x + 1, PLANES), body, :]
        near = near + source[half, now, PAD - 1 : PAD - 1 + height, :]
        near = near + source[half, now, PAD + 1 : PAD + 1 + height, :]
        far = source[half, pl.ds(x - 2, PLANES), body, :] + source[half, pl.ds(x + 2, PLANES), body, :]
        far = far + source[half, now, PAD - 2 : PAD - 2 + height, :]
        far = far + source[half, now, PAD + 2 : PAD + 2 + height, :]
        far = far + z_sum[:, half * LANES : (half + 1) * LANES].reshape(PLANES, height, LANES)
        result = local[half, now, body, :] * values[half] * scale
        result = result + near * (NEAR * scale) + far * (FAR * scale)
        if not first:
            result = result - target[half, now, body, :]
        target[half, now, body, :] = result


def four_steps(a, b, local, along_z, chip, along_x):
    extent = a.shape[1]
    height = a.shape[2] - 2 * PAD
    for buffer in (a, b):
        for rows in (slice(0, PAD), slice(PAD + height, PAD + height + PAD)):
            buffer[:, :, rows, :] = jnp.zeros((2, extent, PAD, LANES), jnp.float32)
    buffers = (a, b)
    for step in range(STEPS):
        source, target = buffers[step % 2], buffers[(step + 1) % 2]
        low = 2 * (step + 1)
        blocks = (extent - 2 * low) // PLANES

        def block(index, carry, source=source, target=target, low=low, step=step):
            stencil(source, target, local, low + index * PLANES, along_z, step == 0)
            return carry

        lax.fori_loop(0, blocks, block, 0, unroll=2)
        if step < STEPS - 1:
            @pl.when(along_x == 0)
            def _():
                target[:, :HALO] = jnp.zeros((2, HALO) + target.shape[2:], jnp.float32)

            @pl.when(along_x == lax.axis_size("gx") - 1)
            def _():
                target[:, extent - HALO :] = jnp.zeros((2, HALO) + target.shape[2:], jnp.float32)

            if not one_sided():
                zero = jnp.zeros((2, extent, 8, LANES), jnp.float32)

                @pl.when(chip == 0)
                def _():
                    target[:, :, PAD : PAD + 8, :] = zero

                @pl.when(chip == lax.axis_size("gy") // 2 - 1)
                def _():
                    target[:, :, PAD + 24 : PAD + 32, :] = zero


def edge_flags(core, chip):
    if one_sided():
        return [core == 1 - chip]
    return [core == 1, core == 0]


def pack_kernel(orbitals, received, potential, received_potential, y_out, left_out, right_out, *d_out):
    core, chip, _ = place()
    width = potential.shape[0]
    fields = ((orbitals.at[core], received), (potential, received_potential))
    for f, (own, other) in enumerate(fields):
        for t, tile in enumerate((own, other)):
            left_out[f, t] = tile[:HALO]
            right_out[f, t] = tile[width - HALO :]
        for k, flag in enumerate(edge_flags(core, chip)):
            for chosen, tile in ((flag, own), (jnp.logical_not(flag), other)):

                @pl.when(chosen)
                def _(tile=tile, k=k, f=f):
                    y_out[k, f] = tile[...]
                    d_out[2 * k][f] = tile[:HALO]
                    d_out[2 * k + 1][f] = tile[width - HALO :]


def first_kernel(count, *refs):
    orbitals, received, potential, received_potential, x_left, x_right = refs[:6]
    y_halos = refs[6 : 6 + count]
    corners = refs[6 + count : 6 + 3 * count]
    own_out, other_out, y_out, left_out, right_out = refs[6 + 3 * count : 11 + 3 * count]
    d_out = refs[11 + 3 * count : 11 + 5 * count]
    a, b, local = refs[11 + 5 * count :]
    core, chip, along_x = place()
    width, depth = potential.shape[0], potential.shape[2]

    def pieces(f):
        return (
            x_left.at[f],
            x_right.at[f],
            [y.at[f] for y in y_halos],
            [(corners[2 * k].at[f], corners[2 * k + 1].at[f]) for k in range(count)],
        )

    fill(a, (orbitals.at[core], received), *pieces(0), core, chip)
    fill(local, (potential, received_potential), *pieces(1), core, chip, lambda v: (v - 0.5) / 4.25)
    four_steps(a, b, local, z_matrix(depth), chip, along_x)
    outs = (own_out, other_out)
    for t, slot in enumerate(own_slots(core, chip)):
        for half in range(2):
            lanes = slice(half * LANES, (half + 1) * LANES)
            tile = a[half, HALO : HALO + width, rows_of(slot), :]
            outs[t][:, :, lanes] = tile
            left_out[t, :, :, lanes] = tile[:HALO]
            right_out[t, :, :, lanes] = tile[width - HALO :]
    for k, flag in enumerate(edge_flags(core, chip)):
        own_slot, other_slot = own_slots(core, chip)
        slot = jnp.where(flag, own_slot, other_slot)
        for half in range(2):
            lanes = slice(half * LANES, (half + 1) * LANES)
            tile = a[half, HALO : HALO + width, rows_of(slot), :]
            y_out[k, :, :, lanes] = tile
            d_out[2 * k][:, :, lanes] = tile[:HALO]
            d_out[2 * k + 1][:, :, lanes] = tile[width - HALO :]


def second_kernel(count, *refs):
    orbitals, received, potential, received_potential = refs[:4]
    own, other, x_left, x_right = refs[4:8]
    y_halos = refs[8 : 8 + count]
    corners = refs[8 + count : 8 + 3 * count]
    rest = refs[8 + 3 * count :]
    p_left, p_right = rest[:2]
    p_halos = rest[2 : 2 + count]
    p_corners = rest[2 + count : 2 + 3 * count]
    keep, give, a, b, local = rest[2 + 3 * count :]
    core, chip, along_x = place()
    width, depth = potential.shape[0], potential.shape[2]
    fill(
        a,
        (own, other),
        x_left,
        x_right,
        y_halos,
        [(corners[2 * k], corners[2 * k + 1]) for k in range(count)],
        core,
        chip,
    )
    fill(
        local,
        (potential, received_potential),
        p_left.at[1],
        p_right.at[1],
        [y.at[1] for y in p_halos],
        [(p_corners[2 * k].at[1], p_corners[2 * k + 1].at[1]) for k in range(count)],
        core,
        chip,
        lambda v: (v - 0.5) / 4.25,
    )
    four_steps(a, b, local, z_matrix(depth), chip, along_x)
    start = (orbitals.at[core], received)
    outs = (keep, give)
    for t, slot in enumerate(own_slots(core, chip)):
        for half in range(2):
            lanes = slice(half * LANES, (half + 1) * LANES)
            tile = a[half, HALO : HALO + width, rows_of(slot), :]
            outs[t][:, :, lanes] = 2.0 * tile - start[t][:, :, lanes]


def slot_orbitals(bands):
    core, _, _ = place()
    band = lax.axis_index("band")
    names = []
    for d in range(bands):
        group = lax.rem(band + bands - d, bands)
        names += [2 * group + core, 2 * group + 1 - core]
    return names


def correlation_kernel(bands, *refs):
    slots, out = refs[:-1], refs[-1]
    names = slot_orbitals(bands)
    row = lax.broadcasted_iota(jnp.int32, (8, LANES), 0)
    column = lax.broadcasted_iota(jnp.int32, (8, LANES), 1)
    count = len(slots)
    pairs = [(i, j) for i in range(count) for j in range(i, count)]
    width, height, depth = slots[0].shape

    def body(index, totals):
        planes = [s[pl.ds(index * PLANES, PLANES)] for s in slots]
        found = []
        for (i, j), total in zip(pairs, totals):
            product = jnp.sum(planes[i] * planes[j], axis=0)
            for half in range(depth // LANES):
                total = total + product[:, half * LANES : (half + 1) * LANES]
            found.append(total)
        return tuple(found)

    zero = jnp.zeros((height, LANES), jnp.float32)
    totals = lax.fori_loop(0, width // PLANES, body, (zero,) * len(pairs))
    result = jnp.zeros((8, LANES), jnp.float32)
    for (i, j), total in zip(pairs, totals):
        here = ((row == names[i]) & (column == names[j])) | ((row == names[j]) & (column == names[i]))
        result = jnp.where(here, jnp.sum(total), result)
    out[...] = result


def basis_kernel(bands, cells, *refs):
    correlation, order = refs[:2]
    slots = refs[2 : 2 + 2 * bands]
    out, mixing = refs[2 + 2 * bands :]
    names = slot_orbitals(bands)
    count = 2 * bands
    band = lax.axis_index("band")

    def splat(value):
        return jnp.full((8, LANES), value, jnp.float32)

    at = [order[p] for p in range(count)]
    mixing[...] = jnp.zeros_like(mixing)
    lower = {}
    inverse_diagonal = []
    for j in range(count):
        for i in range(j, count):
            total = splat(correlation[at[i], at[j]]) * (1.0 / cells)
            for k in range(j):
                total = total - lower[i, k] * lower[j, k]
            if i == j:
                diagonal = jnp.sqrt(total)
                inverse_diagonal.append(1.0 / diagonal)
            else:
                lower[i, j] = total * inverse_diagonal[j]
    inverse = {}
    for j in range(count):
        inverse[j, j] = inverse_diagonal[j]
        for i in range(j + 1, count):
            total = lower[i, j] * inverse[j, j]
            for k in range(j + 1, i):
                total = total + lower[i, k] * inverse[k, j]
            inverse[i, j] = -total * inverse_diagonal[i]
    for (i, j), value in inverse.items():
        mixing[at[i], at[j]] = value
    width, _, depth = slots[0].shape
    for r in range(2):
        factors = [mixing[2 * band + r, name] for name in names]

        def body(x, carry, r=r, factors=factors):
            for half in range(depth // LANES):
                lanes = slice(half * LANES, (half + 1) * LANES)
                total = factors[0] * slots[0][x, :, lanes]
                for factor, slot in zip(factors[1:], slots[1:]):
                    total = total + factor * slot[x, :, lanes]
                out[r, x, :, lanes] = total
            return carry

        lax.fori_loop(0, width, body, 0, unroll=4)


def moves(dx, dy_chip, swap=False):
    nx, ny = lax.axis_size("gx"), lax.axis_size("gy")
    pairs = []
    for x in range(nx):
        for y in range(ny):
            chip, core = y // 2, y % 2
            to_x = x + dx
            to_chip = 1 - chip if dy_chip == "flip" else chip + dy_chip
            to_core = 1 - core if swap else core
            if 0 <= to_x < nx and 0 <= to_chip < ny // 2:
                pairs.append((x * ny + y, to_x * ny + to_chip * 2 + to_core))
    return pairs


def send(value, dx, dy_chip, swap=False):
    return lax.ppermute(value, ("gx", "gy"), moves(dx, dy_chip, swap))


def y_steps():
    return ["flip"] if one_sided() else [1, -1]


def exchange(y_out, left_out, right_out, d_out):
    y_halos = [send(y_out[k], 0, step) for k, step in enumerate(y_steps())]
    corners = []
    for k, step in enumerate(y_steps()):
        corners += [send(d_out[2 * k + 1], 1, step), send(d_out[2 * k], -1, step)]
    x_left = send(right_out, 1, 0)
    x_right = send(left_out, -1, 0)
    return x_left, x_right, *y_halos, *corners


def summed(value, axis):
    count = lax.axis_size(axis)
    if count & (count - 1):
        return lax.psum(value, axis)
    step = 1
    while step < count:
        value = value + lax.ppermute(value, axis, [(i, i ^ step) for i in range(count)])
        step *= 2
    return value


def per_device(orbitals, potential, order):
    group, width, height, depth = orbitals.shape
    bands = lax.axis_size("band")
    cells = float(width * lax.axis_size("gx") * height * lax.axis_size("gy") * depth)
    count = len(y_steps())
    core, chip, _ = place()
    extent = width + 2 * HALO
    window = (2, extent, 8 * tile_count() + 2 * PAD, LANES)
    scratch = [pltpu.VMEM(window, jnp.float32)] * 3

    other = lax.dynamic_index_in_dim(orbitals, 1 - core, 0, keepdims=False)
    received = send(other, 0, 0, True)
    received_potential = send(potential, 0, 0, True)
    tile = (width, height, depth)
    ends = (2, HALO, height, depth)
    corner = (HALO, height, depth)
    packed = pl.pallas_call(
        pack_kernel,
        out_shape=[struct(count, 2, *tile), struct(2, *ends), struct(2, *ends)]
        + [struct(2, *corner)] * (2 * count),
        in_specs=[VMEM] * 4,
        out_specs=[VMEM] * (3 + 2 * count),
        compiler_params=PARAMS,
        name="pack",
    )(orbitals, received, potential, received_potential)
    halos = exchange(*packed[:3], packed[3:])
    first = pl.pallas_call(
        functools.partial(first_kernel, count),
        out_shape=[struct(*tile)] * 2
        + [struct(count, *tile), struct(*ends), struct(*ends)]
        + [struct(*corner)] * (2 * count),
        in_specs=[VMEM] * (6 + 3 * count),
        out_specs=[VMEM] * (5 + 2 * count),
        scratch_shapes=scratch,
        compiler_params=PARAMS,
        name="first_round",
    )(orbitals, received, potential, received_potential, *halos)
    own, sibling = first[:2]
    second_halos = exchange(*first[2:5], first[5:])
    keep, give = pl.pallas_call(
        functools.partial(second_kernel, count),
        out_shape=[struct(*tile)] * 2,
        in_specs=[VMEM] * (10 + 6 * count),
        out_specs=[VMEM] * 2,
        scratch_shapes=scratch,
        compiler_params=PARAMS,
        name="second_round",
    )(orbitals, received, potential, received_potential, own, sibling, *second_halos, *halos)

    slots = [keep, send(give, 0, 0, True)]
    for d in range(1, bands):
        same, crossed = [], []
        for y in range(lax.axis_size("gy")):
            for b in range(bands):
                to = (b + d) % bands
                same.append((y * bands + b, y * bands + to))
                crossed.append((y * bands + b, (y ^ 1) * bands + to))
        slots.append(lax.ppermute(keep, ("gy", "band"), same))
        slots.append(lax.ppermute(give, ("gy", "band"), crossed))
    partial_value = pl.pallas_call(
        functools.partial(correlation_kernel, bands),
        out_shape=struct(8, LANES),
        in_specs=[VMEM] * len(slots),
        out_specs=VMEM,
        compiler_params=PARAMS,
        name="correlation",
    )(*slots)
    correlation = summed(summed(partial_value, "gy"), "gx")
    return pl.pallas_call(
        functools.partial(basis_kernel, bands, cells),
        out_shape=struct(*orbitals.shape),
        in_specs=[SMEM, SMEM] + [VMEM] * len(slots),
        out_specs=VMEM,
        scratch_shapes=[pltpu.VMEM((2 * bands, 2 * bands, 8, LANES), jnp.float32)],
        compiler_params=PARAMS,
        name="basis",
    )(correlation, order, *slots)


def solution(mesh):
    in_specs = (P("band", "gx", "gy", None), P("gx", "gy", None), P())
    out_specs = P("band", "gx", "gy", None)
    return jax.shard_map(
        per_device, mesh=mesh, in_specs=in_specs, out_specs=out_specs, check_vma=False
    )
```

```python
import functools

import jax
import jax.numpy as jnp
from jax import lax
from jax.experimental import pallas as pl
from jax.experimental.pallas import tpu as pltpu
from jax.sharding import PartitionSpec as P

STEPS = 4
HALO = 2 * STEPS
PAD = 8
LANES = 128
PLANES = 4
NEAR = -(2.0 / 3.0) / 4.25
FAR = (1.0 / 24.0) / 4.25
VMEM = pl.BlockSpec(memory_space=pltpu.VMEM)
SMEM = pl.BlockSpec(memory_space=pltpu.SMEM)
PARAMS = pltpu.CompilerParams(vmem_limit_bytes=40 * 1024 * 1024)


def struct(*shape):
    return jax.ShapeDtypeStruct(shape, jnp.float32)


def place():
    along_y = lax.axis_index("gy")
    return along_y % 2, along_y // 2, lax.axis_index("gx")


def one_sided():
    return lax.axis_size("gy") == 4


def tile_count():
    return 3 if one_sided() else 4


def y_phases():
    return range(1 if one_sided() else 2)


def upward(position, phase):
    return (position % 2) == phase


def own_slots(core, chip):
    first = chip if one_sided() else 1
    return first + core, first + 1 - core


def halo_slot(chip, up):
    first = chip if one_sided() else 1
    return jnp.where(up, first + 2, first - 1)


def rows_of(slot):
    return pl.ds(pl.multiple_of(PAD + 8 * slot, 8), 8)


def put(window, first_plane, rows, planes, change=lambda a: a):
    count = planes.shape[0]
    for half in range(2):
        lanes = slice(half * LANES, (half + 1) * LANES)
        window[half, pl.ds(first_plane, count), rows, :] = change(planes[:, :, lanes])


def halo_start(right, width, count):
    return jnp.where(right, HALO + width, HALO - count)


def fill(window, tiles, x_halos, y_halos, corners, change=lambda a: a):
    core, chip, along_x = place()
    width = tiles[0].shape[0]
    slots = own_slots(core, chip)
    for index, slot in enumerate(slots):
        put(window, HALO, rows_of(slot), tiles[index], change)
        for phase in range(2):
            halo = x_halos[phase].at[index]
            start = halo_start(upward(along_x, phase), width, halo.shape[0])
            put(window, start, rows_of(slot), halo, change)
    for phase in y_phases():
        rows = rows_of(halo_slot(chip, upward(chip, phase)))
        put(window, HALO, rows, y_halos[phase], change)
        for x_phase in range(2):
            corner = corners[2 * phase + x_phase]
            start = halo_start(upward(along_x, x_phase), width, corner.shape[0])
            put(window, start, rows, corner, change)


def near_planes(right, width, count):
    return pl.ds(jnp.where(right, width - count, 0), count)


def z_matrix(depth):
    gap = jnp.abs(
        lax.broadcasted_iota(jnp.int32, (depth, depth), 0)
        - lax.broadcasted_iota(jnp.int32, (depth, depth), 1)
    )
    return jnp.where(gap == 1, -16.0, jnp.where(gap == 2, 1.0, 0.0)).astype(jnp.bfloat16)


def stencil(source, target, local, x, along_z, first):
    height = source.shape[2] - 2 * PAD
    body = slice(PAD, PAD + height)
    now = pl.ds(x, PLANES)
    values = [source[half, now, body, :] for half in range(2)]
    high = [v.astype(jnp.bfloat16) for v in values]
    low = [(v - h.astype(jnp.float32)).astype(jnp.bfloat16) for v, h in zip(values, high)]

    def joined(parts):
        return jnp.concatenate([p.reshape(PLANES * height, LANES) for p in parts], axis=1)

    z_sum = jnp.dot(joined(high), along_z, preferred_element_type=jnp.float32)
    z_sum = z_sum + jnp.dot(joined(low), along_z, preferred_element_type=jnp.float32)
    scale = 1.0 if first else 2.0
    for half in range(2):
        near = source[half, pl.ds(x - 1, PLANES), body, :] + source[half, pl.ds(x + 1, PLANES), body, :]
        near = near + source[half, now, PAD - 1 : PAD - 1 + height, :]
        near = near + source[half, now, PAD + 1 : PAD + 1 + height, :]
        far = source[half, pl.ds(x - 2, PLANES), body, :] + source[half, pl.ds(x + 2, PLANES), body, :]
        far = far + source[half, now, PAD - 2 : PAD - 2 + height, :]
        far = far + source[half, now, PAD + 2 : PAD + 2 + height, :]
        far = far + z_sum[:, half * LANES : (half + 1) * LANES].reshape(PLANES, height, LANES)
        result = local[half, now, body, :] * values[half] * scale
        result = result + near * (NEAR * scale) + far * (FAR * scale)
        if not first:
            result = result - target[half, now, body, :]
        target[half, now, body, :] = result


def four_steps(a, b, local, along_z, chip, along_x):
    extent = a.shape[1]
    height = a.shape[2] - 2 * PAD
    for buffer in (a, b):
        for rows in (slice(0, PAD), slice(PAD + height, PAD + height + PAD)):
            buffer[:, :, rows, :] = jnp.zeros((2, extent, PAD, LANES), jnp.float32)
    buffers = (a, b)
    for step in range(STEPS):
        source, target = buffers[step % 2], buffers[(step + 1) % 2]
        low = 2 * (step + 1)
        blocks = (extent - 2 * low) // PLANES

        def block(index, carry, source=source, target=target, low=low, step=step):
            stencil(source, target, local, low + index * PLANES, along_z, step == 0)
            return carry

        lax.fori_loop(0, blocks, block, 0, unroll=2)
        if step < STEPS - 1:
            @pl.when(along_x == 0)
            def _():
                target[:, :HALO] = jnp.zeros((2, HALO) + target.shape[2:], jnp.float32)

            @pl.when(along_x == lax.axis_size("gx") - 1)
            def _():
                target[:, extent - HALO :] = jnp.zeros((2, HALO) + target.shape[2:], jnp.float32)

            if not one_sided():
                zero = jnp.zeros((2, extent, 8, LANES), jnp.float32)

                @pl.when(chip == 0)
                def _():
                    target[:, :, PAD : PAD + 8, :] = zero

                @pl.when(chip == lax.axis_size("gy") // 2 - 1)
                def _():
                    target[:, :, PAD + 24 : PAD + 32, :] = zero


def edge_is_own(core, chip, phase):
    return core == jnp.where(upward(chip, phase), 1, 0)


def pack_kernel(orbitals, received, potential, received_potential, *outs):
    core, chip, along_x = place()
    width = potential.shape[0]
    y_out = outs[: len(y_phases())]
    x_out = outs[len(y_phases()) : len(y_phases()) + 2]
    d_out = outs[len(y_phases()) + 2 :]
    tiles = (orbitals.at[core], received)
    local = (potential, received_potential)
    for x_phase in range(2):
        right = upward(along_x, x_phase)
        for t in range(2):
            x_out[x_phase][t, :HALO] = tiles[t][near_planes(right, width, HALO)]
            x_out[x_phase][t, HALO:] = local[t][near_planes(right, width, HALO - 2)]
    for phase in y_phases():
        own = edge_is_own(core, chip, phase)
        for t, chosen in enumerate((own, jnp.logical_not(own))):

            @pl.when(chosen)
            def _(t=t, phase=phase):
                y_out[phase][...] = tiles[t][...]
                for x_phase in range(2):
                    right = upward(along_x, x_phase)
                    out = d_out[2 * phase + x_phase]
                    out[: HALO - 1] = tiles[t][near_planes(right, width, HALO - 1)]
                    out[HALO - 1 :] = local[t][near_planes(right, width, HALO - 3)]


def fill_local(window, potential, received_potential, edge, passed, x_halos, corners):
    core, chip, _ = place()
    fill(
        window,
        (potential, received_potential),
        [x.at[:, HALO:] for x in x_halos],
        [edge] * len(y_phases()),
        [c.at[HALO - 1 :] for c in corners],
        lambda v: (v - 0.5) / 4.25,
    )
    for phase in y_phases():
        up = upward(chip, phase)

        @pl.when(core != jnp.where(up, 1, 0))
        def _(up=up):
            put(window, HALO, rows_of(halo_slot(chip, up)), passed, lambda v: (v - 0.5) / 4.25)


def first_kernel(*refs):
    count = len(y_phases())
    orbitals, received, potential, received_potential, edge, passed = refs[:6]
    y_halos, x_halos, corners = refs[6 : 6 + count], refs[6 + count : 8 + count], refs[8 + count : 8 + 3 * count]
    own_out, other_out = refs[8 + 3 * count : 10 + 3 * count]
    outs = refs[10 + 3 * count : 12 + 6 * count]
    a, b, local = refs[12 + 6 * count :]
    core, chip, along_x = place()
    width, depth = potential.shape[0], potential.shape[2]
    fill(
        a,
        (orbitals.at[core], received),
        [x.at[:, :HALO] for x in x_halos],
        y_halos,
        [c.at[: HALO - 1] for c in corners],
    )
    fill_local(local, potential, received_potential, edge, passed, x_halos, corners)
    four_steps(a, b, local, z_matrix(depth), chip, along_x)
    y_out, x_out, d_out = outs[:count], outs[count : count + 2], outs[count + 2 :]
    slots = own_slots(core, chip)
    for half in range(2):
        lanes = slice(half * LANES, (half + 1) * LANES)

        def planes(slot, start, size, half=half):
            return a[half, pl.ds(HALO + start, size), rows_of(slot), :]

        def ends(right, size):
            return jnp.where(right, width - size, 0)

        for t, out in enumerate((own_out, other_out)):
            out[:, :, lanes] = planes(slots[t], 0, width)
            for x_phase in range(2):
                start = ends(upward(along_x, x_phase), HALO)
                x_out[x_phase][t, :, :, lanes] = planes(slots[t], start, HALO)
        for phase in y_phases():
            slot = jnp.where(edge_is_own(core, chip, phase), *slots)
            y_out[phase][:, :, lanes] = planes(slot, 0, width)
            for x_phase in range(2):
                start = ends(upward(along_x, x_phase), HALO - 1)
                d_out[2 * phase + x_phase][:, :, lanes] = planes(slot, start, HALO - 1)


def second_kernel(*refs):
    count = len(y_phases())
    orbitals, received, potential, received_potential, edge, passed, own, other = refs[:8]
    halos = refs[8 : 10 + 3 * count]
    y_halos, x_halos, corners = halos[:count], halos[count : count + 2], halos[count + 2 :]
    p_x_halos = refs[10 + 3 * count : 12 + 3 * count]
    p_corners = refs[12 + 3 * count : 12 + 5 * count]
    keep, give, a, b, local = refs[12 + 5 * count :]
    core, chip, along_x = place()
    width, depth = potential.shape[0], potential.shape[2]
    fill(a, (own, other), x_halos, y_halos, corners)
    fill_local(local, potential, received_potential, edge, passed, p_x_halos, p_corners)
    four_steps(a, b, local, z_matrix(depth), chip, along_x)
    start = (orbitals.at[core], received)
    outs = (keep, give)
    for t, slot in enumerate(own_slots(core, chip)):
        for half in range(2):
            lanes = slice(half * LANES, (half + 1) * LANES)
            tile = a[half, HALO : HALO + width, rows_of(slot), :]
            outs[t][:, :, lanes] = 2.0 * tile - start[t][:, :, lanes]


def slot_orbitals(bands):
    core, _, _ = place()
    band = lax.axis_index("band")
    names = []
    for d in range(bands):
        group = lax.rem(band + bands - d, bands)
        names += [2 * group + core, 2 * group + 1 - core]
    return names


def correlation_kernel(bands, *refs):
    slots, out = refs[:-1], refs[-1]
    names = slot_orbitals(bands)
    row = lax.broadcasted_iota(jnp.int32, (8, LANES), 0)
    column = lax.broadcasted_iota(jnp.int32, (8, LANES), 1)
    count = len(slots)
    pairs = [(i, j) for i in range(count) for j in range(i, count)]
    width, height, depth = slots[0].shape

    def body(index, totals):
        planes = [s[pl.ds(index * PLANES, PLANES)] for s in slots]
        found = []
        for (i, j), total in zip(pairs, totals):
            product = jnp.sum(planes[i] * planes[j], axis=0)
            for half in range(depth // LANES):
                total = total + product[:, half * LANES : (half + 1) * LANES]
            found.append(total)
        return tuple(found)

    zero = jnp.zeros((height, LANES), jnp.float32)
    totals = lax.fori_loop(0, width // PLANES, body, (zero,) * len(pairs))
    result = jnp.zeros((8, LANES), jnp.float32)
    for (i, j), total in zip(pairs, totals):
        here = ((row == names[i]) & (column == names[j])) | ((row == names[j]) & (column == names[i]))
        result = jnp.where(here, jnp.sum(total), result)
    out[...] = result


def basis_kernel(bands, cells, *refs):
    correlation, order = refs[:2]
    slots = refs[2 : 2 + 2 * bands]
    out, mixing = refs[2 + 2 * bands :]
    names = slot_orbitals(bands)
    count = 2 * bands
    band = lax.axis_index("band")

    def splat(value):
        return jnp.full((8, LANES), value, jnp.float32)

    at = [order[p] for p in range(count)]
    mixing[...] = jnp.zeros_like(mixing)
    lower = {}
    inverse_diagonal = []
    for j in range(count):
        for i in range(j, count):
            total = splat(correlation[at[i], at[j]]) * (1.0 / cells)
            for k in range(j):
                total = total - lower[i, k] * lower[j, k]
            if i == j:
                diagonal = jnp.sqrt(total)
                inverse_diagonal.append(1.0 / diagonal)
            else:
                lower[i, j] = total * inverse_diagonal[j]
    inverse = {}
    for j in range(count):
        inverse[j, j] = inverse_diagonal[j]
        for i in range(j + 1, count):
            total = lower[i, j] * inverse[j, j]
            for k in range(j + 1, i):
                total = total + lower[i, k] * inverse[k, j]
            inverse[i, j] = -total * inverse_diagonal[i]
    for (i, j), value in inverse.items():
        mixing[at[i], at[j]] = value
    width, _, depth = slots[0].shape
    for r in range(2):
        factors = [mixing[2 * band + r, name] for name in names]

        def body(x, carry, r=r, factors=factors):
            for half in range(depth // LANES):
                lanes = slice(half * LANES, (half + 1) * LANES)
                total = factors[0] * slots[0][x, :, lanes]
                for factor, slot in zip(factors[1:], slots[1:]):
                    total = total + factor * slot[x, :, lanes]
                out[r, x, :, lanes] = total
            return carry

        lax.fori_loop(0, width, body, 0, unroll=4)


def partner(position, phase, count):
    other = position + 1 if position % 2 == phase else position - 1
    return other if 0 <= other < count else None


def meet(value, x_phase=None, y_phase=None):
    nx, ny = lax.axis_size("gx"), lax.axis_size("gy")
    pairs = []
    for x in range(nx):
        for y in range(ny):
            to_x = x if x_phase is None else partner(x, x_phase, nx)
            chip = y // 2 if y_phase is None else partner(y // 2, y_phase, ny // 2)
            if to_x is not None and chip is not None:
                pairs.append((x * ny + y, to_x * ny + chip * 2 + y % 2))
    return lax.ppermute(value, ("gx", "gy"), pairs)


def swap(value):
    count = lax.axis_size("gy")
    return lax.ppermute(value, "gy", [(y, y ^ 1) for y in range(count)])


def face(value):
    count = lax.axis_size("gy")
    pairs = [(y, partner(y, 1, count)) for y in range(count)]
    return lax.ppermute(value, "gy", [p for p in pairs if p[1] is not None])


def exchange(payloads):
    count = len(y_phases())
    halos = [meet(payloads[phase], y_phase=phase) for phase in y_phases()]
    halos += [meet(payloads[count + phase], x_phase=phase) for phase in range(2)]
    for y_phase in y_phases():
        for x_phase in range(2):
            halos.append(meet(payloads[count + 2 + 2 * y_phase + x_phase], x_phase, y_phase))
    return halos


def summed(value, axis):
    count = lax.axis_size(axis)
    if count & (count - 1):
        return lax.psum(value, axis)

    def of(step):
        return lax.ppermute(value, axis, [(i, i ^ step) for i in range(count)])

    if count == 4:
        return (value + of(1)) + (of(2) + of(3))
    step = 1
    while step < count:
        value = value + of(step)
        step *= 2
    return value


def per_device(orbitals, potential, order):
    group, width, height, depth = orbitals.shape
    bands = lax.axis_size("band")
    cells = float(width * lax.axis_size("gx") * height * lax.axis_size("gy") * depth)
    count = len(y_phases())
    core, chip, _ = place()
    window = (2, width + 2 * HALO, 8 * tile_count() + 2 * PAD, LANES)
    scratch = [pltpu.VMEM(window, jnp.float32)] * 3

    edge = face(potential)
    other = lax.dynamic_index_in_dim(orbitals, 1 - core, 0, keepdims=False)
    received = swap(other)
    received_potential = swap(potential)
    tile = (width, height, depth)

    def payloads(in_x, in_corner):
        return (
            [struct(*tile)] * count
            + [struct(2, in_x, height, depth)] * 2
            + [struct(in_corner, height, depth)] * (2 * count)
        )

    packed = pl.pallas_call(
        pack_kernel,
        out_shape=payloads(2 * HALO - 2, 2 * HALO - 4),
        in_specs=[VMEM] * 4,
        out_specs=[VMEM] * (2 + 3 * count),
        compiler_params=PARAMS,
        name="pack",
    )(orbitals, received, potential, received_potential)
    halos = exchange(packed)
    passed = swap(edge)
    local = (potential, received_potential, edge, passed)
    own, sibling, *packed = pl.pallas_call(
        first_kernel,
        out_shape=[struct(*tile)] * 2 + payloads(HALO, HALO - 1),
        in_specs=[VMEM] * (8 + 3 * count),
        out_specs=[VMEM] * (4 + 3 * count),
        scratch_shapes=scratch,
        compiler_params=PARAMS,
        name="first_round",
    )(orbitals, received, *local, *halos)
    second_halos = exchange(packed)
    keep, give = pl.pallas_call(
        second_kernel,
        out_shape=[struct(*tile)] * 2,
        in_specs=[VMEM] * (12 + 5 * count),
        out_specs=[VMEM] * 2,
        scratch_shapes=scratch,
        compiler_params=PARAMS,
        name="second_round",
    )(orbitals, received, *local, own, sibling, *second_halos, *halos[count:])

    slots = [keep, swap(give)]
    for d in range(1, bands):
        same, crossed = [], []
        for y in range(lax.axis_size("gy")):
            for b in range(bands):
                to = (b + d) % bands
                same.append((y * bands + b, y * bands + to))
                crossed.append((y * bands + b, (y ^ 1) * bands + to))
        slots.append(lax.ppermute(keep, ("gy", "band"), same))
        slots.append(lax.ppermute(give, ("gy", "band"), crossed))
    partial_value = pl.pallas_call(
        functools.partial(correlation_kernel, bands),
        out_shape=struct(8, LANES),
        in_specs=[VMEM] * len(slots),
        out_specs=VMEM,
        compiler_params=PARAMS,
        name="correlation",
    )(*slots)
    correlation = summed(summed(partial_value, "gy"), "gx")
    return pl.pallas_call(
        functools.partial(basis_kernel, bands, cells),
        out_shape=struct(*orbitals.shape),
        in_specs=[SMEM, SMEM] + [VMEM] * len(slots),
        out_specs=VMEM,
        scratch_shapes=[pltpu.VMEM((2 * bands, 2 * bands, 8, LANES), jnp.float32)],
        compiler_params=PARAMS,
        name="basis",
    )(correlation, order, *slots)


def solution(mesh):
    in_specs = (P("band", "gx", "gy", None), P("gx", "gy", None), P())
    out_specs = P("band", "gx", "gy", None)
    return jax.shard_map(
        per_device, mesh=mesh, in_specs=in_specs, out_specs=out_specs, check_vma=False
    )
```

```python
import functools

import jax
import jax.numpy as jnp
from jax import lax
from jax.experimental import pallas as pl
from jax.experimental.pallas import tpu as pltpu
from jax.sharding import PartitionSpec as P

STEPS = 4
HALO = 2 * STEPS
PAD = 8
LANES = 128
PLANES = 4
NEAR = -(2.0 / 3.0) / 4.25
FAR = (1.0 / 24.0) / 4.25
VMEM = pl.BlockSpec(memory_space=pltpu.VMEM)
SMEM = pl.BlockSpec(memory_space=pltpu.SMEM)
PARAMS = pltpu.CompilerParams(vmem_limit_bytes=40 * 1024 * 1024)


def struct(*shape):
    return jax.ShapeDtypeStruct(shape, jnp.float32)


def place():
    along_y = lax.axis_index("gy")
    return along_y % 2, along_y // 2, lax.axis_index("gx")


def one_sided():
    return lax.axis_size("gy") == 4


def tile_count():
    return 3 if one_sided() else 4


def y_phases():
    return range(1 if one_sided() else 2)


def upward(position, phase):
    return (position % 2) == phase


def own_slots(core, chip):
    first = chip if one_sided() else 1
    return first + core, first + 1 - core


def halo_slot(chip, up):
    first = chip if one_sided() else 1
    return jnp.where(up, first + 2, first - 1)


def rows_of(slot):
    return pl.ds(pl.multiple_of(PAD + 8 * slot, 8), 8)


def put(window, first_plane, rows, planes, change=lambda a: a):
    count = planes.shape[0]
    for half in range(2):
        lanes = slice(half * LANES, (half + 1) * LANES)
        window[half, pl.ds(first_plane, count), rows, :] = change(planes[:, :, lanes])


def halo_start(right, width, count):
    return jnp.where(right, HALO + width, HALO - count)


def fill(window, tiles, x_halos, y_halos, corners, change=lambda a: a):
    core, chip, along_x = place()
    width = tiles[0].shape[0]
    slots = own_slots(core, chip)
    for index, slot in enumerate(slots):
        put(window, HALO, rows_of(slot), tiles[index], change)
        for phase in range(2):
            halo = x_halos[phase].at[index]
            start = halo_start(upward(along_x, phase), width, halo.shape[0])
            put(window, start, rows_of(slot), halo, change)
    for phase in y_phases():
        rows = rows_of(halo_slot(chip, upward(chip, phase)))
        put(window, HALO, rows, y_halos[phase], change)
        for x_phase in range(2):
            corner = corners[2 * phase + x_phase]
            start = halo_start(upward(along_x, x_phase), width, corner.shape[0])
            put(window, start, rows, corner, change)


def near_planes(right, width, count):
    return pl.ds(jnp.where(right, width - count, 0), count)


def z_matrix(depth):
    gap = jnp.abs(
        lax.broadcasted_iota(jnp.int32, (depth, depth), 0)
        - lax.broadcasted_iota(jnp.int32, (depth, depth), 1)
    )
    return jnp.where(gap == 1, -16.0, jnp.where(gap == 2, 1.0, 0.0)).astype(jnp.bfloat16)


def stencil(source, target, local, x, along_z, first):
    height = source.shape[2] - 2 * PAD
    body = slice(PAD, PAD + height)
    now = pl.ds(x, PLANES)
    values = [source[half, now, body, :] for half in range(2)]
    high = [v.astype(jnp.bfloat16) for v in values]
    low = [(v - h.astype(jnp.float32)).astype(jnp.bfloat16) for v, h in zip(values, high)]

    def joined(parts):
        return jnp.concatenate([p.reshape(PLANES * height, LANES) for p in parts], axis=1)

    z_sum = jnp.dot(joined(high), along_z, preferred_element_type=jnp.float32)
    z_sum = z_sum + jnp.dot(joined(low), along_z, preferred_element_type=jnp.float32)
    scale = 1.0 if first else 2.0
    for half in range(2):
        near = source[half, pl.ds(x - 1, PLANES), body, :] + source[half, pl.ds(x + 1, PLANES), body, :]
        near = near + source[half, now, PAD - 1 : PAD - 1 + height, :]
        near = near + source[half, now, PAD + 1 : PAD + 1 + height, :]
        far = source[half, pl.ds(x - 2, PLANES), body, :] + source[half, pl.ds(x + 2, PLANES), body, :]
        far = far + source[half, now, PAD - 2 : PAD - 2 + height, :]
        far = far + source[half, now, PAD + 2 : PAD + 2 + height, :]
        far = far + z_sum[:, half * LANES : (half + 1) * LANES].reshape(PLANES, height, LANES)
        result = local[half, now, body, :] * values[half] * scale
        result = result + near * (NEAR * scale) + far * (FAR * scale)
        if not first:
            result = result - target[half, now, body, :]
        target[half, now, body, :] = result


def four_steps(a, b, local, along_z):
    extent = a.shape[1]
    height = a.shape[2] - 2 * PAD
    for buffer in (a, b):
        for rows in (slice(0, PAD), slice(PAD + height, PAD + height + PAD)):
            buffer[:, :, rows, :] = jnp.zeros((2, extent, PAD, LANES), jnp.float32)
    outside_is_zero(a)
    buffers = (a, b)
    for step in range(STEPS):
        source, target = buffers[step % 2], buffers[(step + 1) % 2]
        low = 2 * (step + 1)
        blocks = (extent - 2 * low) // PLANES

        def block(index, carry, source=source, target=target, low=low, step=step):
            stencil(source, target, local, low + index * PLANES, along_z, step == 0)
            return carry

        lax.fori_loop(0, blocks, block, 0, unroll=2)
        if step < STEPS - 1:
            outside_is_zero(target)


def outside_is_zero(window):
    _, chip, along_x = place()
    extent = window.shape[1]

    def clear(where, planes, rows=slice(None)):
        @pl.when(where)
        def _():
            region = window[:, planes, rows, :]
            window[:, planes, rows, :] = jnp.zeros_like(region)

    clear(along_x == 0, slice(0, HALO))
    clear(along_x == lax.axis_size("gx") - 1, slice(extent - HALO, extent))
    if not one_sided():
        clear(chip == 0, slice(None), slice(PAD, PAD + 8))
        clear(chip == lax.axis_size("gy") // 2 - 1, slice(None), slice(PAD + 24, PAD + 32))


def edge_is_own(core, chip, phase):
    return core == jnp.where(upward(chip, phase), 1, 0)


def pack_kernel(orbitals, received, potential, received_potential, *outs):
    core, chip, along_x = place()
    width = potential.shape[0]
    y_out = outs[: len(y_phases())]
    x_out = outs[len(y_phases()) : len(y_phases()) + 2]
    d_out = outs[len(y_phases()) + 2 :]
    tiles = (orbitals.at[core], received)
    local = (potential, received_potential)
    for x_phase in range(2):
        right = upward(along_x, x_phase)
        for t in range(2):
            x_out[x_phase][t, :HALO] = tiles[t][near_planes(right, width, HALO)]
            x_out[x_phase][t, HALO:] = local[t][near_planes(right, width, HALO - 2)]
    for phase in y_phases():
        own = edge_is_own(core, chip, phase)
        for t, chosen in enumerate((own, jnp.logical_not(own))):

            @pl.when(chosen)
            def _(t=t, phase=phase):
                y_out[phase][...] = tiles[t][...]
                for x_phase in range(2):
                    right = upward(along_x, x_phase)
                    out = d_out[2 * phase + x_phase]
                    out[: HALO - 1] = tiles[t][near_planes(right, width, HALO - 1)]
                    out[HALO - 1 :] = local[t][near_planes(right, width, HALO - 3)]


def fill_local(window, potential, received_potential, edge, passed, x_halos, corners):
    core, chip, _ = place()
    fill(
        window,
        (potential, received_potential),
        [x.at[:, HALO:] for x in x_halos],
        [edge] * len(y_phases()),
        [c.at[HALO - 1 :] for c in corners],
        lambda v: (v - 0.5) / 4.25,
    )
    for phase in y_phases():
        up = upward(chip, phase)

        @pl.when(core != jnp.where(up, 1, 0))
        def _(up=up):
            put(window, HALO, rows_of(halo_slot(chip, up)), passed, lambda v: (v - 0.5) / 4.25)


def first_kernel(*refs):
    count = len(y_phases())
    orbitals, received, potential, received_potential, edge, passed = refs[:6]
    y_halos, x_halos, corners = refs[6 : 6 + count], refs[6 + count : 8 + count], refs[8 + count : 8 + 3 * count]
    own_out, other_out = refs[8 + 3 * count : 10 + 3 * count]
    outs = refs[10 + 3 * count : 12 + 6 * count]
    a, b, local = refs[12 + 6 * count :]
    core, chip, along_x = place()
    width, depth = potential.shape[0], potential.shape[2]
    fill(
        a,
        (orbitals.at[core], received),
        [x.at[:, :HALO] for x in x_halos],
        y_halos,
        [c.at[: HALO - 1] for c in corners],
    )
    fill_local(local, potential, received_potential, edge, passed, x_halos, corners)
    four_steps(a, b, local, z_matrix(depth))
    y_out, x_out, d_out = outs[:count], outs[count : count + 2], outs[count + 2 :]
    slots = own_slots(core, chip)
    for half in range(2):
        lanes = slice(half * LANES, (half + 1) * LANES)

        def planes(slot, start, size, half=half):
            return a[half, pl.ds(HALO + start, size), rows_of(slot), :]

        def ends(right, size):
            return jnp.where(right, width - size, 0)

        for t, out in enumerate((own_out, other_out)):
            out[:, :, lanes] = planes(slots[t], 0, width)
            for x_phase in range(2):
                start = ends(upward(along_x, x_phase), HALO)
                x_out[x_phase][t, :, :, lanes] = planes(slots[t], start, HALO)
        for phase in y_phases():
            slot = jnp.where(edge_is_own(core, chip, phase), *slots)
            y_out[phase][:, :, lanes] = planes(slot, 0, width)
            for x_phase in range(2):
                start = ends(upward(along_x, x_phase), HALO - 1)
                d_out[2 * phase + x_phase][:, :, lanes] = planes(slot, start, HALO - 1)


def second_kernel(*refs):
    count = len(y_phases())
    orbitals, received, potential, received_potential, edge, passed, own, other = refs[:8]
    halos = refs[8 : 10 + 3 * count]
    y_halos, x_halos, corners = halos[:count], halos[count : count + 2], halos[count + 2 :]
    p_x_halos = refs[10 + 3 * count : 12 + 3 * count]
    p_corners = refs[12 + 3 * count : 12 + 5 * count]
    keep, give, a, b, local = refs[12 + 5 * count :]
    core, chip, along_x = place()
    width, depth = potential.shape[0], potential.shape[2]
    fill(a, (own, other), x_halos, y_halos, corners)
    fill_local(local, potential, received_potential, edge, passed, p_x_halos, p_corners)
    four_steps(a, b, local, z_matrix(depth))
    start = (orbitals.at[core], received)
    outs = (keep, give)
    for t, slot in enumerate(own_slots(core, chip)):
        for half in range(2):
            lanes = slice(half * LANES, (half + 1) * LANES)
            tile = a[half, HALO : HALO + width, rows_of(slot), :]
            outs[t][:, :, lanes] = 2.0 * tile - start[t][:, :, lanes]


def slot_orbitals(bands):
    core, _, _ = place()
    band = lax.axis_index("band")
    names = []
    for d in range(bands):
        group = lax.rem(band + bands - d, bands)
        names += [2 * group + core, 2 * group + 1 - core]
    return names


def correlation_kernel(bands, *refs):
    slots, out = refs[:-1], refs[-1]
    names = slot_orbitals(bands)
    row = lax.broadcasted_iota(jnp.int32, (8, LANES), 0)
    column = lax.broadcasted_iota(jnp.int32, (8, LANES), 1)
    count = len(slots)
    pairs = [(i, j) for i in range(count) for j in range(i, count)]
    width, height, depth = slots[0].shape

    def body(index, totals):
        planes = [s[pl.ds(index * PLANES, PLANES)] for s in slots]
        found = []
        for (i, j), total in zip(pairs, totals):
            product = jnp.sum(planes[i] * planes[j], axis=0)
            for half in range(depth // LANES):
                total = total + product[:, half * LANES : (half + 1) * LANES]
            found.append(total)
        return tuple(found)

    zero = jnp.zeros((height, LANES), jnp.float32)
    totals = lax.fori_loop(0, width // PLANES, body, (zero,) * len(pairs))
    result = jnp.zeros((8, LANES), jnp.float32)
    for (i, j), total in zip(pairs, totals):
        here = ((row == names[i]) & (column == names[j])) | ((row == names[j]) & (column == names[i]))
        result = jnp.where(here, jnp.sum(total), result)
    out[...] = result


def basis_kernel(bands, cells, *refs):
    correlation, order = refs[:2]
    slots = refs[2 : 2 + 2 * bands]
    out, mixing = refs[2 + 2 * bands :]
    names = slot_orbitals(bands)
    count = 2 * bands
    band = lax.axis_index("band")

    def splat(value):
        return jnp.full((8, LANES), value, jnp.float32)

    at = [order[p] for p in range(count)]
    mixing[...] = jnp.zeros_like(mixing)
    lower = {}
    inverse_diagonal = []
    for j in range(count):
        for i in range(j, count):
            total = splat(correlation[at[i], at[j]]) * (1.0 / cells)
            for k in range(j):
                total = total - lower[i, k] * lower[j, k]
            if i == j:
                diagonal = jnp.sqrt(total)
                inverse_diagonal.append(1.0 / diagonal)
            else:
                lower[i, j] = total * inverse_diagonal[j]
    inverse = {}
    for j in range(count):
        inverse[j, j] = inverse_diagonal[j]
        for i in range(j + 1, count):
            total = lower[i, j] * inverse[j, j]
            for k in range(j + 1, i):
                total = total + lower[i, k] * inverse[k, j]
            inverse[i, j] = -total * inverse_diagonal[i]
    for (i, j), value in inverse.items():
        mixing[at[i], at[j]] = value
    width, _, depth = slots[0].shape
    for r in range(2):
        factors = [mixing[2 * band + r, name] for name in names]

        def body(x, carry, r=r, factors=factors):
            for half in range(depth // LANES):
                lanes = slice(half * LANES, (half + 1) * LANES)
                total = factors[0] * slots[0][x, :, lanes]
                for factor, slot in zip(factors[1:], slots[1:]):
                    total = total + factor * slot[x, :, lanes]
                out[r, x, :, lanes] = total
            return carry

        lax.fori_loop(0, width, body, 0, unroll=4)


def partner(position, phase, count):
    other = position + 1 if position % 2 == phase else position - 1
    return other if 0 <= other < count else None


def meet(value, x_phase=None, y_phase=None):
    nx, ny = lax.axis_size("gx"), lax.axis_size("gy")
    pairs = []
    for x in range(nx):
        for y in range(ny):
            to_x = x if x_phase is None else partner(x, x_phase, nx)
            chip = y // 2 if y_phase is None else partner(y // 2, y_phase, ny // 2)
            if to_x is None or chip is None:
                pairs.append((x * ny + y, x * ny + (y ^ 1)))
            else:
                pairs.append((x * ny + y, to_x * ny + chip * 2 + y % 2))
    return lax.ppermute(value, ("gx", "gy"), pairs)


def swap(value):
    count = lax.axis_size("gy")
    return lax.ppermute(value, "gy", [(y, y ^ 1) for y in range(count)])


def face(value):
    count, bands = lax.axis_size("gy"), lax.axis_size("band")
    pairs = []
    for y in range(count):
        for band in range(bands):
            to = partner(y, 1, count)
            if to is not None:
                pairs.append((y * bands + band, to * bands + band))
            elif bands % 2 == 0:
                pairs.append((y * bands + band, y * bands + (band ^ 1)))
    return lax.ppermute(value, ("gy", "band"), pairs)


def exchange(payloads):
    count = len(y_phases())
    halos = [meet(payloads[phase], y_phase=phase) for phase in y_phases()]
    halos += [meet(payloads[count + phase], x_phase=phase) for phase in range(2)]
    for y_phase in y_phases():
        for x_phase in range(2):
            halos.append(meet(payloads[count + 2 + 2 * y_phase + x_phase], x_phase, y_phase))
    return halos


def summed(value, axis):
    count = lax.axis_size(axis)
    if count & (count - 1):
        return lax.psum(value, axis)

    def of(step):
        return lax.ppermute(value, axis, [(i, i ^ step) for i in range(count)])

    if count == 4:
        return (value + of(1)) + (of(2) + of(3))
    step = 1
    while step < count:
        value = value + of(step)
        step *= 2
    return value


def per_device(orbitals, potential, order):
    group, width, height, depth = orbitals.shape
    bands = lax.axis_size("band")
    cells = float(width * lax.axis_size("gx") * height * lax.axis_size("gy") * depth)
    count = len(y_phases())
    core, chip, _ = place()
    window = (2, width + 2 * HALO, 8 * tile_count() + 2 * PAD, LANES)
    scratch = [pltpu.VMEM(window, jnp.float32)] * 3

    edge = face(potential)
    other = lax.dynamic_index_in_dim(orbitals, 1 - core, 0, keepdims=False)
    received = swap(other)
    received_potential = swap(potential)
    tile = (width, height, depth)

    def payloads(in_x, in_corner):
        return (
            [struct(*tile)] * count
            + [struct(2, in_x, height, depth)] * 2
            + [struct(in_corner, height, depth)] * (2 * count)
        )

    packed = pl.pallas_call(
        pack_kernel,
        out_shape=payloads(2 * HALO - 2, 2 * HALO - 4),
        in_specs=[VMEM] * 4,
        out_specs=[VMEM] * (2 + 3 * count),
        compiler_params=PARAMS,
        name="pack",
    )(orbitals, received, potential, received_potential)
    halos = exchange(packed)
    passed = swap(edge)
    local = (potential, received_potential, edge, passed)
    own, sibling, *packed = pl.pallas_call(
        first_kernel,
        out_shape=[struct(*tile)] * 2 + payloads(HALO, HALO - 1),
        in_specs=[VMEM] * (8 + 3 * count),
        out_specs=[VMEM] * (4 + 3 * count),
        scratch_shapes=scratch,
        compiler_params=PARAMS,
        name="first_round",
    )(orbitals, received, *local, *halos)
    second_halos = exchange(packed)
    keep, give = pl.pallas_call(
        second_kernel,
        out_shape=[struct(*tile)] * 2,
        in_specs=[VMEM] * (12 + 5 * count),
        out_specs=[VMEM] * 2,
        scratch_shapes=scratch,
        compiler_params=PARAMS,
        name="second_round",
    )(orbitals, received, *local, own, sibling, *second_halos, *halos[count:])

    slots = [keep, swap(give)]
    for d in range(1, bands):
        same, crossed = [], []
        for y in range(lax.axis_size("gy")):
            for b in range(bands):
                to = (b + d) % bands
                same.append((y * bands + b, y * bands + to))
                crossed.append((y * bands + b, (y ^ 1) * bands + to))
        slots.append(lax.ppermute(keep, ("gy", "band"), same))
        slots.append(lax.ppermute(give, ("gy", "band"), crossed))
    partial_value = pl.pallas_call(
        functools.partial(correlation_kernel, bands),
        out_shape=struct(8, LANES),
        in_specs=[VMEM] * len(slots),
        out_specs=VMEM,
        compiler_params=PARAMS,
        name="correlation",
    )(*slots)
    correlation = summed(summed(partial_value, "gy"), "gx")
    return pl.pallas_call(
        functools.partial(basis_kernel, bands, cells),
        out_shape=struct(*orbitals.shape),
        in_specs=[SMEM, SMEM] + [VMEM] * len(slots),
        out_specs=VMEM,
        scratch_shapes=[pltpu.VMEM((2 * bands, 2 * bands, 8, LANES), jnp.float32)],
        compiler_params=PARAMS,
        name="basis",
    )(correlation, order, *slots)


def solution(mesh):
    in_specs = (P("band", "gx", "gy", None), P("gx", "gy", None), P())
    out_specs = P("band", "gx", "gy", None)
    return jax.shard_map(
        per_device, mesh=mesh, in_specs=in_specs, out_specs=out_specs, check_vma=False
    )
```

```python
import functools

import jax
import jax.numpy as jnp
from jax import lax
from jax.experimental import pallas as pl
from jax.experimental.pallas import tpu as pltpu
from jax.sharding import PartitionSpec as P

STEPS = 4
HALO = 2 * STEPS
PAD = 8
LANES = 128
PLANES = 4
NEAR = -(2.0 / 3.0) / 4.25
FAR = (1.0 / 24.0) / 4.25
VMEM = pl.BlockSpec(memory_space=pltpu.VMEM)
SMEM = pl.BlockSpec(memory_space=pltpu.SMEM)
PARAMS = pltpu.CompilerParams(vmem_limit_bytes=40 * 1024 * 1024)


def struct(*shape):
    return jax.ShapeDtypeStruct(shape, jnp.float32)


def place():
    along_y = lax.axis_index("gy")
    return along_y % 2, along_y // 2, lax.axis_index("gx")


def one_sided():
    return lax.axis_size("gy") == 4


def tile_count():
    return 3 if one_sided() else 4


def y_phases():
    return range(1 if one_sided() else 2)


def upward(position, phase):
    return (position % 2) == phase


def own_slots(core, chip):
    first = chip if one_sided() else 1
    return first + core, first + 1 - core


def halo_slot(chip, up):
    first = chip if one_sided() else 1
    return jnp.where(up, first + 2, first - 1)


def rows_of(slot):
    return pl.ds(pl.multiple_of(PAD + 8 * slot, 8), 8)


def put(window, first_plane, rows, planes, change=lambda a: a):
    count = planes.shape[0]
    for half in range(2):
        lanes = slice(half * LANES, (half + 1) * LANES)
        window[half, pl.ds(first_plane, count), rows, :] = change(planes[:, :, lanes])


def halo_start(right, width, count):
    return jnp.where(right, HALO + width, HALO - count)


def fill(window, tiles, x_halos, y_halos, corners, change=lambda a: a):
    core, chip, along_x = place()
    width = tiles[0].shape[0]
    slots = own_slots(core, chip)
    for index, slot in enumerate(slots):
        put(window, HALO, rows_of(slot), tiles[index], change)
        for phase in range(2):
            halo = x_halos[phase].at[index]
            start = halo_start(upward(along_x, phase), width, halo.shape[0])
            put(window, start, rows_of(slot), halo, change)
    for phase in y_phases():
        rows = rows_of(halo_slot(chip, upward(chip, phase)))
        put(window, HALO, rows, y_halos[phase], change)
        for x_phase in range(2):
            corner = corners[2 * phase + x_phase]
            start = halo_start(upward(along_x, x_phase), width, corner.shape[0])
            put(window, start, rows, corner, change)


def near_planes(right, width, count):
    return pl.ds(jnp.where(right, width - count, 0), count)


def z_matrix(depth):
    gap = jnp.abs(
        lax.broadcasted_iota(jnp.int32, (depth, depth), 0)
        - lax.broadcasted_iota(jnp.int32, (depth, depth), 1)
    )
    return jnp.where(gap == 1, -16.0, jnp.where(gap == 2, 1.0, 0.0)).astype(jnp.bfloat16)


def stencil(source, target, local, x, along_z, first):
    height = source.shape[2] - 2 * PAD
    body = slice(PAD, PAD + height)
    now = pl.ds(x, PLANES)
    values = [source[half, now, body, :] for half in range(2)]
    high = [v.astype(jnp.bfloat16) for v in values]
    low = [(v - h.astype(jnp.float32)).astype(jnp.bfloat16) for v, h in zip(values, high)]

    def joined(parts):
        return jnp.concatenate([p.reshape(PLANES * height, LANES) for p in parts], axis=1)

    z_sum = jnp.dot(joined(high), along_z, preferred_element_type=jnp.float32)
    z_sum = z_sum + jnp.dot(joined(low), along_z, preferred_element_type=jnp.float32)
    scale = 1.0 if first else 2.0
    for half in range(2):
        near = source[half, pl.ds(x - 1, PLANES), body, :] + source[half, pl.ds(x + 1, PLANES), body, :]
        near = near + source[half, now, PAD - 1 : PAD - 1 + height, :]
        near = near + source[half, now, PAD + 1 : PAD + 1 + height, :]
        far = source[half, pl.ds(x - 2, PLANES), body, :] + source[half, pl.ds(x + 2, PLANES), body, :]
        far = far + source[half, now, PAD - 2 : PAD - 2 + height, :]
        far = far + source[half, now, PAD + 2 : PAD + 2 + height, :]
        far = far + z_sum[:, half * LANES : (half + 1) * LANES].reshape(PLANES, height, LANES)
        result = local[half, now, body, :] * values[half] * scale
        result = result + near * (NEAR * scale) + far * (FAR * scale)
        if not first:
            result = result - target[half, now, body, :]
        target[half, now, body, :] = result


def four_steps(a, b, local, along_z):
    extent = a.shape[1]
    height = a.shape[2] - 2 * PAD
    for buffer in (a, b):
        for rows in (slice(0, PAD), slice(PAD + height, PAD + height + PAD)):
            buffer[:, :, rows, :] = jnp.zeros((2, extent, PAD, LANES), jnp.float32)
    outside_is_zero(a)
    buffers = (a, b)
    for step in range(STEPS):
        source, target = buffers[step % 2], buffers[(step + 1) % 2]
        low = 2 * (step + 1)
        blocks = (extent - 2 * low) // PLANES

        def block(index, carry, source=source, target=target, low=low, step=step):
            stencil(source, target, local, low + index * PLANES, along_z, step == 0)
            return carry

        lax.fori_loop(0, blocks, block, 0, unroll=2)
        if step < STEPS - 1:
            outside_is_zero(target)


def outside_is_zero(window):
    _, chip, along_x = place()
    extent = window.shape[1]

    def clear(where, planes, rows=slice(None)):
        @pl.when(where)
        def _():
            region = window[:, planes, rows, :]
            window[:, planes, rows, :] = jnp.zeros_like(region)

    clear(along_x == 0, slice(0, HALO))
    clear(along_x == lax.axis_size("gx") - 1, slice(extent - HALO, extent))
    if not one_sided():
        clear(chip == 0, slice(None), slice(PAD, PAD + 8))
        clear(chip == lax.axis_size("gy") // 2 - 1, slice(None), slice(PAD + 24, PAD + 32))


def edge_is_own(core, chip, phase):
    return core == jnp.where(upward(chip, phase), 1, 0)


def pack_kernel(orbitals, received, potential, received_potential, *outs):
    core, chip, along_x = place()
    width = potential.shape[0]
    y_out = outs[: len(y_phases())]
    x_out = outs[len(y_phases()) : len(y_phases()) + 2]
    d_out = outs[len(y_phases()) + 2 :]
    tiles = (orbitals.at[core], received.at[core])
    local = (potential, received_potential)
    for x_phase in range(2):
        right = upward(along_x, x_phase)
        for t in range(2):
            x_out[x_phase][t, :HALO] = tiles[t][near_planes(right, width, HALO)]
            x_out[x_phase][t, HALO:] = local[t][near_planes(right, width, HALO - 2)]
    for phase in y_phases():
        own = edge_is_own(core, chip, phase)
        for t, chosen in enumerate((own, jnp.logical_not(own))):

            @pl.when(chosen)
            def _(t=t, phase=phase):
                y_out[phase][...] = tiles[t][...]
                for x_phase in range(2):
                    right = upward(along_x, x_phase)
                    out = d_out[2 * phase + x_phase]
                    out[: HALO - 1] = tiles[t][near_planes(right, width, HALO - 1)]
                    out[HALO - 1 :] = local[t][near_planes(right, width, HALO - 3)]


def fill_local(window, potential, received_potential, edge, passed, x_halos, corners):
    core, chip, _ = place()
    fill(
        window,
        (potential, received_potential),
        [x.at[:, HALO:] for x in x_halos],
        [edge] * len(y_phases()),
        [c.at[HALO - 1 :] for c in corners],
        lambda v: (v - 0.5) / 4.25,
    )
    for phase in y_phases():
        up = upward(chip, phase)

        @pl.when(core != jnp.where(up, 1, 0))
        def _(up=up):
            put(window, HALO, rows_of(halo_slot(chip, up)), passed, lambda v: (v - 0.5) / 4.25)


def first_kernel(*refs):
    count = len(y_phases())
    orbitals, received, potential, received_potential, edge, passed = refs[:6]
    y_halos, x_halos, corners = refs[6 : 6 + count], refs[6 + count : 8 + count], refs[8 + count : 8 + 3 * count]
    own_out, other_out = refs[8 + 3 * count : 10 + 3 * count]
    outs = refs[10 + 3 * count : 12 + 6 * count]
    a, b, local = refs[12 + 6 * count :]
    core, chip, along_x = place()
    width, depth = potential.shape[0], potential.shape[2]
    fill(
        a,
        (orbitals.at[core], received.at[core]),
        [x.at[:, :HALO] for x in x_halos],
        y_halos,
        [c.at[: HALO - 1] for c in corners],
    )
    fill_local(local, potential, received_potential, edge, passed, x_halos, corners)
    four_steps(a, b, local, z_matrix(depth))
    y_out, x_out, d_out = outs[:count], outs[count : count + 2], outs[count + 2 :]
    slots = own_slots(core, chip)
    for half in range(2):
        lanes = slice(half * LANES, (half + 1) * LANES)

        def planes(slot, start, size, half=half):
            return a[half, pl.ds(HALO + start, size), rows_of(slot), :]

        def ends(right, size):
            return jnp.where(right, width - size, 0)

        for t, out in enumerate((own_out, other_out)):
            out[:, :, lanes] = planes(slots[t], 0, width)
            for x_phase in range(2):
                start = ends(upward(along_x, x_phase), HALO)
                x_out[x_phase][t, :, :, lanes] = planes(slots[t], start, HALO)
        for phase in y_phases():
            slot = jnp.where(edge_is_own(core, chip, phase), *slots)
            y_out[phase][:, :, lanes] = planes(slot, 0, width)
            for x_phase in range(2):
                start = ends(upward(along_x, x_phase), HALO - 1)
                d_out[2 * phase + x_phase][:, :, lanes] = planes(slot, start, HALO - 1)


def second_kernel(*refs):
    count = len(y_phases())
    orbitals, received, potential, received_potential, edge, passed, own, other = refs[:8]
    halos = refs[8 : 10 + 3 * count]
    y_halos, x_halos, corners = halos[:count], halos[count : count + 2], halos[count + 2 :]
    p_x_halos = refs[10 + 3 * count : 12 + 3 * count]
    p_corners = refs[12 + 3 * count : 12 + 5 * count]
    keep, give, a, b, local = refs[12 + 5 * count :]
    core, chip, along_x = place()
    width, depth = potential.shape[0], potential.shape[2]
    fill(a, (own, other), x_halos, y_halos, corners)
    fill_local(local, potential, received_potential, edge, passed, p_x_halos, p_corners)
    four_steps(a, b, local, z_matrix(depth))
    start = (orbitals.at[core], received.at[core])
    outs = (keep, give)
    for t, slot in enumerate(own_slots(core, chip)):
        for half in range(2):
            lanes = slice(half * LANES, (half + 1) * LANES)
            tile = a[half, HALO : HALO + width, rows_of(slot), :]
            outs[t][:, :, lanes] = 2.0 * tile - start[t][:, :, lanes]


def slot_orbitals(bands):
    core, _, _ = place()
    band = lax.axis_index("band")
    names = []
    for d in range(bands):
        group = lax.rem(band + bands - d, bands)
        names += [2 * group + core, 2 * group + 1 - core]
    return names


def correlation_kernel(bands, *refs):
    slots, out = refs[:-1], refs[-1]
    names = slot_orbitals(bands)
    row = lax.broadcasted_iota(jnp.int32, (8, LANES), 0)
    column = lax.broadcasted_iota(jnp.int32, (8, LANES), 1)
    count = len(slots)
    pairs = [(i, j) for i in range(count) for j in range(i, count)]
    width, height, depth = slots[0].shape

    def body(index, totals):
        planes = [s[pl.ds(index * PLANES, PLANES)] for s in slots]
        found = []
        for (i, j), total in zip(pairs, totals):
            product = jnp.sum(planes[i] * planes[j], axis=0)
            for half in range(depth // LANES):
                total = total + product[:, half * LANES : (half + 1) * LANES]
            found.append(total)
        return tuple(found)

    zero = jnp.zeros((height, LANES), jnp.float32)
    totals = lax.fori_loop(0, width // PLANES, body, (zero,) * len(pairs))
    result = jnp.zeros((8, LANES), jnp.float32)
    for (i, j), total in zip(pairs, totals):
        here = ((row == names[i]) & (column == names[j])) | ((row == names[j]) & (column == names[i]))
        result = jnp.where(here, jnp.sum(total), result)
    out[...] = result


def basis_kernel(bands, cells, *refs):
    correlation, order = refs[:2]
    slots = refs[2 : 2 + 2 * bands]
    out, mixing = refs[2 + 2 * bands :]
    names = slot_orbitals(bands)
    count = 2 * bands
    band = lax.axis_index("band")

    def splat(value):
        return jnp.full((8, LANES), value, jnp.float32)

    at = [order[p] for p in range(count)]
    mixing[...] = jnp.zeros_like(mixing)
    lower = {}
    inverse_diagonal = []
    for j in range(count):
        for i in range(j, count):
            total = splat(correlation[at[i], at[j]]) * (1.0 / cells)
            for k in range(j):
                total = total - lower[i, k] * lower[j, k]
            if i == j:
                diagonal = jnp.sqrt(total)
                inverse_diagonal.append(1.0 / diagonal)
            else:
                lower[i, j] = total * inverse_diagonal[j]
    inverse = {}
    for j in range(count):
        inverse[j, j] = inverse_diagonal[j]
        for i in range(j + 1, count):
            total = lower[i, j] * inverse[j, j]
            for k in range(j + 1, i):
                total = total + lower[i, k] * inverse[k, j]
            inverse[i, j] = -total * inverse_diagonal[i]
    for (i, j), value in inverse.items():
        mixing[at[i], at[j]] = value
    width, _, depth = slots[0].shape
    for r in range(2):
        factors = [mixing[2 * band + r, name] for name in names]

        def body(x, carry, r=r, factors=factors):
            for half in range(depth // LANES):
                lanes = slice(half * LANES, (half + 1) * LANES)
                total = factors[0] * slots[0][x, :, lanes]
                for factor, slot in zip(factors[1:], slots[1:]):
                    total = total + factor * slot[x, :, lanes]
                out[r, x, :, lanes] = total
            return carry

        lax.fori_loop(0, width, body, 0, unroll=4)


def partner(position, phase, count):
    other = position + 1 if position % 2 == phase else position - 1
    return other if 0 <= other < count else None


def meet(value, x_phase=None, y_phase=None):
    nx, ny = lax.axis_size("gx"), lax.axis_size("gy")
    pairs = []
    for x in range(nx):
        for y in range(ny):
            to_x = x if x_phase is None else partner(x, x_phase, nx)
            chip = y // 2 if y_phase is None else partner(y // 2, y_phase, ny // 2)
            if to_x is None or chip is None:
                pairs.append((x * ny + y, x * ny + (y ^ 1)))
            else:
                pairs.append((x * ny + y, to_x * ny + chip * 2 + y % 2))
    return lax.ppermute(value, ("gx", "gy"), pairs)


def swap(value):
    count = lax.axis_size("gy")
    return lax.ppermute(value, "gy", [(y, y ^ 1) for y in range(count)])


def face(value):
    count, bands = lax.axis_size("gy"), lax.axis_size("band")
    pairs = []
    for y in range(count):
        for band in range(bands):
            to = partner(y, 1, count)
            if to is not None:
                pairs.append((y * bands + band, to * bands + band))
            elif bands % 2 == 0:
                pairs.append((y * bands + band, y * bands + (band ^ 1)))
    return lax.ppermute(value, ("gy", "band"), pairs)


def exchange(payloads):
    count = len(y_phases())
    halos = [meet(payloads[phase], y_phase=phase) for phase in y_phases()]
    halos += [meet(payloads[count + phase], x_phase=phase) for phase in range(2)]
    for y_phase in y_phases():
        for x_phase in range(2):
            halos.append(meet(payloads[count + 2 + 2 * y_phase + x_phase], x_phase, y_phase))
    return halos


def summed(value, axis):
    count = lax.axis_size(axis)
    if count & (count - 1):
        return lax.psum(value, axis)

    def of(step):
        return lax.ppermute(value, axis, [(i, i ^ step) for i in range(count)])

    if count == 4:
        return (value + of(1)) + (of(2) + of(3))
    step = 1
    while step < count:
        value = value + of(step)
        step *= 2
    return value


def per_device(orbitals, potential, order):
    group, width, height, depth = orbitals.shape
    bands = lax.axis_size("band")
    cells = float(width * lax.axis_size("gx") * height * lax.axis_size("gy") * depth)
    count = len(y_phases())
    window = (2, width + 2 * HALO, 8 * tile_count() + 2 * PAD, LANES)
    scratch = [pltpu.VMEM(window, jnp.float32)] * 3

    edge = face(potential)
    received = swap(orbitals)
    received_potential = swap(potential)
    tile = (width, height, depth)

    def payloads(in_x, in_corner):
        return (
            [struct(*tile)] * count
            + [struct(2, in_x, height, depth)] * 2
            + [struct(in_corner, height, depth)] * (2 * count)
        )

    packed = pl.pallas_call(
        pack_kernel,
        out_shape=payloads(2 * HALO - 2, 2 * HALO - 4),
        in_specs=[VMEM] * 4,
        out_specs=[VMEM] * (2 + 3 * count),
        compiler_params=PARAMS,
        name="pack",
    )(orbitals, received, potential, received_potential)
    halos = exchange(packed)
    edge, _ = lax.optimization_barrier((edge, halos[count]))
    passed = swap(edge)
    local = (potential, received_potential, edge, passed)
    own, sibling, *packed = pl.pallas_call(
        first_kernel,
        out_shape=[struct(*tile)] * 2 + payloads(HALO, HALO - 1),
        in_specs=[VMEM] * (8 + 3 * count),
        out_specs=[VMEM] * (4 + 3 * count),
        scratch_shapes=scratch,
        compiler_params=PARAMS,
        name="first_round",
    )(orbitals, received, *local, *halos)
    second_halos = exchange(packed)
    keep, give = pl.pallas_call(
        second_kernel,
        out_shape=[struct(*tile)] * 2,
        in_specs=[VMEM] * (12 + 5 * count),
        out_specs=[VMEM] * 2,
        scratch_shapes=scratch,
        compiler_params=PARAMS,
        name="second_round",
    )(orbitals, received, *local, own, sibling, *second_halos, *halos[count:])

    slots = [keep, swap(give)]
    for d in range(1, bands):
        same, crossed = [], []
        for y in range(lax.axis_size("gy")):
            for b in range(bands):
                to = (b + d) % bands
                same.append((y * bands + b, y * bands + to))
                crossed.append((y * bands + b, (y ^ 1) * bands + to))
        slots.append(lax.ppermute(keep, ("gy", "band"), same))
        slots.append(lax.ppermute(give, ("gy", "band"), crossed))
    partial_value = pl.pallas_call(
        functools.partial(correlation_kernel, bands),
        out_shape=struct(8, LANES),
        in_specs=[VMEM] * len(slots),
        out_specs=VMEM,
        compiler_params=PARAMS,
        name="correlation",
    )(*slots)
    correlation = summed(summed(partial_value, "gy"), "gx")
    return pl.pallas_call(
        functools.partial(basis_kernel, bands, cells),
        out_shape=struct(*orbitals.shape),
        in_specs=[SMEM, SMEM] + [VMEM] * len(slots),
        out_specs=VMEM,
        scratch_shapes=[pltpu.VMEM((2 * bands, 2 * bands, 8, LANES), jnp.float32)],
        compiler_params=PARAMS,
        name="basis",
    )(correlation, order, *slots)


def solution(mesh):
    in_specs = (P("band", "gx", "gy", None), P("gx", "gy", None), P())
    out_specs = P("band", "gx", "gy", None)
    return jax.shard_map(
        per_device, mesh=mesh, in_specs=in_specs, out_specs=out_specs, check_vma=False
    )
```

```python
import functools

import jax
import jax.numpy as jnp
from jax import lax
from jax.experimental import pallas as pl
from jax.experimental.pallas import tpu as pltpu
from jax.sharding import PartitionSpec as P

STEPS = 4
HALO = 2 * STEPS
PAD = 8
LANES = 128
PLANES = 4
NEAR = -(2.0 / 3.0) / 4.25
FAR = (1.0 / 24.0) / 4.25
VMEM = pl.BlockSpec(memory_space=pltpu.VMEM)
SMEM = pl.BlockSpec(memory_space=pltpu.SMEM)
PARAMS = pltpu.CompilerParams(vmem_limit_bytes=40 * 1024 * 1024)


def struct(*shape):
    return jax.ShapeDtypeStruct(shape, jnp.float32)


def place():
    along_y = lax.axis_index("gy")
    return along_y % 2, along_y // 2, lax.axis_index("gx")


def one_sided():
    return lax.axis_size("gy") == 4


def tile_count():
    return 3 if one_sided() else 4


def y_phases():
    return range(1 if one_sided() else 2)


def upward(position, phase):
    return (position % 2) == phase


def own_slots(core, chip):
    first = chip if one_sided() else 1
    return first + core, first + 1 - core


def halo_slot(chip, up):
    first = chip if one_sided() else 1
    return jnp.where(up, first + 2, first - 1)


def rows_of(slot):
    return pl.ds(pl.multiple_of(PAD + 8 * slot, 8), 8)


def put(window, first_plane, rows, planes, change=lambda a: a):
    count = planes.shape[0]
    for half in range(2):
        lanes = slice(half * LANES, (half + 1) * LANES)
        window[half, pl.ds(first_plane, count), rows, :] = change(planes[:, :, lanes])


def halo_start(right, width, count):
    return jnp.where(right, HALO + width, HALO - count)


def fill(window, tiles, x_halos, y_halos, corners, change=lambda a: a):
    core, chip, along_x = place()
    width = tiles[0].shape[0]
    slots = own_slots(core, chip)
    for index, slot in enumerate(slots):
        put(window, HALO, rows_of(slot), tiles[index], change)
        for phase in range(2):
            halo = x_halos[phase].at[index]
            start = halo_start(upward(along_x, phase), width, halo.shape[0])
            put(window, start, rows_of(slot), halo, change)
    for phase in y_phases():
        rows = rows_of(halo_slot(chip, upward(chip, phase)))
        if y_halos is not None:
            put(window, HALO, rows, y_halos[phase], change)
        for x_phase in range(2):
            corner = corners[2 * phase + x_phase]
            start = halo_start(upward(along_x, x_phase), width, corner.shape[0])
            put(window, start, rows, corner, change)


def near_planes(right, width, count):
    return pl.ds(jnp.where(right, width - count, 0), count)


def z_matrix(depth):
    gap = jnp.abs(
        lax.broadcasted_iota(jnp.int32, (depth, depth), 0)
        - lax.broadcasted_iota(jnp.int32, (depth, depth), 1)
    )
    return jnp.where(gap == 1, -16.0, jnp.where(gap == 2, 1.0, 0.0)).astype(jnp.bfloat16)


def stencil(source, target, local, x, along_z, first):
    height = source.shape[2] - 2 * PAD
    body = slice(PAD, PAD + height)
    now = pl.ds(x, PLANES)
    values = [source[half, now, body, :] for half in range(2)]
    high = [v.astype(jnp.bfloat16) for v in values]
    low = [(v - h.astype(jnp.float32)).astype(jnp.bfloat16) for v, h in zip(values, high)]

    def joined(parts):
        return jnp.concatenate([p.reshape(PLANES * height, LANES) for p in parts], axis=1)

    z_sum = jnp.dot(joined(high), along_z, preferred_element_type=jnp.float32)
    z_sum = z_sum + jnp.dot(joined(low), along_z, preferred_element_type=jnp.float32)
    scale = 1.0 if first else 2.0
    for half in range(2):
        near = source[half, pl.ds(x - 1, PLANES), body, :] + source[half, pl.ds(x + 1, PLANES), body, :]
        near = near + source[half, now, PAD - 1 : PAD - 1 + height, :]
        near = near + source[half, now, PAD + 1 : PAD + 1 + height, :]
        far = source[half, pl.ds(x - 2, PLANES), body, :] + source[half, pl.ds(x + 2, PLANES), body, :]
        far = far + source[half, now, PAD - 2 : PAD - 2 + height, :]
        far = far + source[half, now, PAD + 2 : PAD + 2 + height, :]
        far = far + z_sum[:, half * LANES : (half + 1) * LANES].reshape(PLANES, height, LANES)
        result = local[half, now, body, :] * values[half] * scale
        result = result + near * (NEAR * scale) + far * (FAR * scale)
        if not first:
            result = result - target[half, now, body, :]
        target[half, now, body, :] = result


def four_steps(a, b, local, along_z):
    extent = a.shape[1]
    height = a.shape[2] - 2 * PAD
    for buffer in (a, b):
        for rows in (slice(0, PAD), slice(PAD + height, PAD + height + PAD)):
            buffer[:, :, rows, :] = jnp.zeros((2, extent, PAD, LANES), jnp.float32)
    outside_is_zero(a)
    buffers = (a, b)
    for step in range(STEPS):
        source, target = buffers[step % 2], buffers[(step + 1) % 2]
        low = 2 * (step + 1)
        blocks = (extent - 2 * low) // PLANES

        def block(index, carry, source=source, target=target, low=low, step=step):
            stencil(source, target, local, low + index * PLANES, along_z, step == 0)
            return carry

        lax.fori_loop(0, blocks, block, 0, unroll=2)
        if step < STEPS - 1:
            outside_is_zero(target)


def outside_is_zero(window):
    _, chip, along_x = place()
    extent = window.shape[1]

    def clear(where, planes, rows=slice(None)):
        @pl.when(where)
        def _():
            region = window[:, planes, rows, :]
            window[:, planes, rows, :] = jnp.zeros_like(region)

    clear(along_x == 0, slice(0, HALO))
    clear(along_x == lax.axis_size("gx") - 1, slice(extent - HALO, extent))
    if not one_sided():
        clear(chip == 0, slice(None), slice(PAD, PAD + 8))
        clear(chip == lax.axis_size("gy") // 2 - 1, slice(None), slice(PAD + 24, PAD + 32))


def edge_is_own(core, chip, phase):
    return core == jnp.where(upward(chip, phase), 1, 0)


def load_kernel(orbitals, potential, orbitals_out, potential_out, arrived):
    copies = [
        pltpu.make_async_copy(orbitals, orbitals_out, arrived.at[0]),
        pltpu.make_async_copy(potential, potential_out, arrived.at[1]),
    ]
    for copy in copies:
        copy.start()
    for copy in copies:
        copy.wait()


def pack_kernel(orbitals, received, potential, received_potential, *outs):
    core, chip, along_x = place()
    width = potential.shape[0]
    y_out = outs[: len(y_phases())]
    x_out = outs[len(y_phases()) : len(y_phases()) + 2]
    d_out = outs[len(y_phases()) + 2 :]
    tiles = (orbitals.at[core], received.at[core])
    local = (potential, received_potential)
    for x_phase in range(2):
        right = upward(along_x, x_phase)
        for t in range(2):
            x_out[x_phase][t, :HALO] = tiles[t][near_planes(right, width, HALO)]
            x_out[x_phase][t, HALO:] = local[t][near_planes(right, width, HALO - 2)]
    for phase in y_phases():
        own = edge_is_own(core, chip, phase)
        for t, chosen in enumerate((own, jnp.logical_not(own))):

            @pl.when(chosen)
            def _(t=t, phase=phase):
                y_out[phase][:width] = tiles[t][...]
                half = width // 2
                y_out[phase][width:] = local[t][pl.ds(core * half, half)]
                for x_phase in range(2):
                    right = upward(along_x, x_phase)
                    out = d_out[2 * phase + x_phase]
                    out[: HALO - 1] = tiles[t][near_planes(right, width, HALO - 1)]
                    out[HALO - 1 :] = local[t][near_planes(right, width, HALO - 3)]


def fill_local(window, potential, received_potential, passed, y_halos, x_halos, corners):
    core, chip, _ = place()
    width = potential.shape[0]
    half = width // 2

    def change(v):
        return (v - 0.5) / 4.25

    fill(
        window,
        (potential, received_potential),
        [x.at[:, HALO:] for x in x_halos],
        None,
        [c.at[HALO - 1 :] for c in corners],
        change,
    )
    for phase in y_phases():
        rows = rows_of(halo_slot(chip, upward(chip, phase)))
        put(window, HALO + core * half, rows, y_halos[phase].at[width:], change)
        put(window, HALO + (1 - core) * half, rows, passed[phase], change)


def first_kernel(*refs):
    count = len(y_phases())
    orbitals, received, potential, received_potential = refs[:4]
    passed, halos = refs[4 : 4 + count], refs[4 + count : 6 + 4 * count]
    y_halos, x_halos, corners = halos_of(halos)
    own_out, other_out = refs[6 + 4 * count : 8 + 4 * count]
    outs = refs[8 + 4 * count : 10 + 7 * count]
    a, b, local = refs[10 + 7 * count :]
    core, chip, along_x = place()
    width, depth = potential.shape[0], potential.shape[2]
    fill(
        a,
        (orbitals.at[core], received.at[core]),
        [x.at[:, :HALO] for x in x_halos],
        [y.at[:width] for y in y_halos],
        [c.at[: HALO - 1] for c in corners],
    )
    fill_local(local, potential, received_potential, passed, *halos_of(halos))
    four_steps(a, b, local, z_matrix(depth))
    y_out, x_out, d_out = outs[:count], outs[count : count + 2], outs[count + 2 :]
    slots = own_slots(core, chip)
    for half in range(2):
        lanes = slice(half * LANES, (half + 1) * LANES)

        def planes(slot, start, size, half=half):
            return a[half, pl.ds(HALO + start, size), rows_of(slot), :]

        def ends(right, size):
            return jnp.where(right, width - size, 0)

        for t, out in enumerate((own_out, other_out)):
            out[:, :, lanes] = planes(slots[t], 0, width)
            for x_phase in range(2):
                start = ends(upward(along_x, x_phase), HALO)
                x_out[x_phase][t, :, :, lanes] = planes(slots[t], start, HALO)
        for phase in y_phases():
            slot = jnp.where(edge_is_own(core, chip, phase), *slots)
            y_out[phase][:, :, lanes] = planes(slot, 0, width)
            for x_phase in range(2):
                start = ends(upward(along_x, x_phase), HALO - 1)
                d_out[2 * phase + x_phase][:, :, lanes] = planes(slot, start, HALO - 1)


def halos_of(refs):
    count = len(y_phases())
    return refs[:count], refs[count : count + 2], refs[count + 2 :]


def second_kernel(*refs):
    count = len(y_phases())
    orbitals, received, potential, received_potential = refs[:4]
    passed, local_halos = refs[4 : 4 + count], refs[4 + count : 6 + 4 * count]
    own, other = refs[6 + 4 * count : 8 + 4 * count]
    halos = refs[8 + 4 * count : 10 + 7 * count]
    keep, give, a, b, local = refs[10 + 7 * count :]
    core, chip, _ = place()
    width, depth = potential.shape[0], potential.shape[2]
    y_halos, x_halos, corners = halos_of(halos)
    fill(a, (own, other), x_halos, y_halos, corners)
    fill_local(local, potential, received_potential, passed, *halos_of(local_halos))
    four_steps(a, b, local, z_matrix(depth))
    start = (orbitals.at[core], received.at[core])
    outs = (keep, give)
    for t, slot in enumerate(own_slots(core, chip)):
        for half in range(2):
            lanes = slice(half * LANES, (half + 1) * LANES)
            tile = a[half, HALO : HALO + width, rows_of(slot), :]
            outs[t][:, :, lanes] = 2.0 * tile - start[t][:, :, lanes]


def slot_orbitals(bands):
    core, _, _ = place()
    band = lax.axis_index("band")
    names = []
    for d in range(bands):
        group = lax.rem(band + bands - d, bands)
        names += [2 * group + core, 2 * group + 1 - core]
    return names


def correlation_kernel(bands, *refs):
    slots, out = refs[:-1], refs[-1]
    names = slot_orbitals(bands)
    row = lax.broadcasted_iota(jnp.int32, (8, LANES), 0)
    column = lax.broadcasted_iota(jnp.int32, (8, LANES), 1)
    count = len(slots)
    pairs = [(i, j) for i in range(count) for j in range(i, count)]
    width, height, depth = slots[0].shape

    def body(index, totals):
        planes = [s[pl.ds(index * PLANES, PLANES)] for s in slots]
        found = []
        for (i, j), total in zip(pairs, totals):
            product = jnp.sum(planes[i] * planes[j], axis=0)
            for half in range(depth // LANES):
                total = total + product[:, half * LANES : (half + 1) * LANES]
            found.append(total)
        return tuple(found)

    zero = jnp.zeros((height, LANES), jnp.float32)
    totals = lax.fori_loop(0, width // PLANES, body, (zero,) * len(pairs))
    result = jnp.zeros((8, LANES), jnp.float32)
    for (i, j), total in zip(pairs, totals):
        here = ((row == names[i]) & (column == names[j])) | ((row == names[j]) & (column == names[i]))
        result = jnp.where(here, jnp.sum(total), result)
    out[...] = result


def basis_kernel(bands, cells, *refs):
    correlation, order = refs[:2]
    slots = refs[2 : 2 + 2 * bands]
    out, mixing = refs[2 + 2 * bands :]
    names = slot_orbitals(bands)
    count = 2 * bands
    band = lax.axis_index("band")

    def splat(value):
        return jnp.full((8, LANES), value, jnp.float32)

    at = [order[p] for p in range(count)]
    mixing[...] = jnp.zeros_like(mixing)
    lower = {}
    inverse_diagonal = []
    for j in range(count):
        for i in range(j, count):
            total = splat(correlation[at[i], at[j]]) * (1.0 / cells)
            for k in range(j):
                total = total - lower[i, k] * lower[j, k]
            if i == j:
                diagonal = jnp.sqrt(total)
                inverse_diagonal.append(1.0 / diagonal)
            else:
                lower[i, j] = total * inverse_diagonal[j]
    inverse = {}
    for j in range(count):
        inverse[j, j] = inverse_diagonal[j]
        for i in range(j + 1, count):
            total = lower[i, j] * inverse[j, j]
            for k in range(j + 1, i):
                total = total + lower[i, k] * inverse[k, j]
            inverse[i, j] = -total * inverse_diagonal[i]
    for (i, j), value in inverse.items():
        mixing[at[i], at[j]] = value
    width, _, depth = slots[0].shape
    for r in range(2):
        factors = [mixing[2 * band + r, name] for name in names]

        def body(x, carry, r=r, factors=factors):
            for half in range(depth // LANES):
                lanes = slice(half * LANES, (half + 1) * LANES)
                total = factors[0] * slots[0][x, :, lanes]
                for factor, slot in zip(factors[1:], slots[1:]):
                    total = total + factor * slot[x, :, lanes]
                out[r, x, :, lanes] = total
            return carry

        lax.fori_loop(0, width, body, 0, unroll=4)


def partner(position, phase, count):
    other = position + 1 if position % 2 == phase else position - 1
    return other if 0 <= other < count else None


def meet(value, x_phase=None, y_phase=None):
    nx, ny = lax.axis_size("gx"), lax.axis_size("gy")
    pairs = []
    for x in range(nx):
        for y in range(ny):
            to_x = x if x_phase is None else partner(x, x_phase, nx)
            chip = y // 2 if y_phase is None else partner(y // 2, y_phase, ny // 2)
            if to_x is None or chip is None:
                pairs.append((x * ny + y, x * ny + (y ^ 1)))
            else:
                pairs.append((x * ny + y, to_x * ny + chip * 2 + y % 2))
    return lax.ppermute(value, ("gx", "gy"), pairs)


def swap(value):
    count = lax.axis_size("gy")
    return lax.ppermute(value, "gy", [(y, y ^ 1) for y in range(count)])


def exchange(payloads):
    count = len(y_phases())
    halos = [meet(payloads[phase], y_phase=phase) for phase in y_phases()]
    halos += [meet(payloads[count + phase], x_phase=phase) for phase in range(2)]
    for y_phase in y_phases():
        for x_phase in range(2):
            halos.append(meet(payloads[count + 2 + 2 * y_phase + x_phase], x_phase, y_phase))
    return halos


def summed(value, axis):
    count = lax.axis_size(axis)
    if count & (count - 1):
        return lax.psum(value, axis)

    def of(step):
        return lax.ppermute(value, axis, [(i, i ^ step) for i in range(count)])

    if count == 4:
        return (value + of(1)) + (of(2) + of(3))
    step = 1
    while step < count:
        value = value + of(step)
        step *= 2
    return value


def per_device(orbitals, potential, order):
    group, width, height, depth = orbitals.shape
    bands = lax.axis_size("band")
    cells = float(width * lax.axis_size("gx") * height * lax.axis_size("gy") * depth)
    count = len(y_phases())
    window = (2, width + 2 * HALO, 8 * tile_count() + 2 * PAD, LANES)
    scratch = [pltpu.VMEM(window, jnp.float32)] * 3

    received = swap(orbitals)
    received_potential = swap(potential)
    tile = (width, height, depth)
    orbitals, potential = pl.pallas_call(
        load_kernel,
        out_shape=[struct(*orbitals.shape), struct(*tile)],
        in_specs=[pl.BlockSpec(memory_space=pl.ANY)] * 2,
        out_specs=[VMEM] * 2,
        scratch_shapes=[pltpu.SemaphoreType.DMA((2,))],
        compiler_params=PARAMS,
        name="load",
    )(orbitals, potential)

    def payloads(in_y, in_x, in_corner):
        return (
            [struct(in_y, height, depth)] * count
            + [struct(2, in_x, height, depth)] * 2
            + [struct(in_corner, height, depth)] * (2 * count)
        )

    packed = pl.pallas_call(
        pack_kernel,
        out_shape=payloads(width + width // 2, 2 * HALO - 2, 2 * HALO - 4),
        in_specs=[VMEM] * 4,
        out_specs=[VMEM] * (2 + 3 * count),
        compiler_params=PARAMS,
        name="pack",
    )(orbitals, received, potential, received_potential)
    halos = exchange(packed)
    passed = []
    for phase in y_phases():
        half, *_ = lax.optimization_barrier((halos[phase][width:], *halos[count:]))
        passed.append(swap(half))
    local = (potential, received_potential, *passed, *halos)
    own, sibling, *packed = pl.pallas_call(
        first_kernel,
        out_shape=[struct(*tile)] * 2 + payloads(width, HALO, HALO - 1),
        in_specs=[VMEM] * (6 + 4 * count),
        out_specs=[VMEM] * (4 + 3 * count),
        scratch_shapes=scratch,
        compiler_params=PARAMS,
        name="first_round",
    )(orbitals, received, *local)
    keep, give = pl.pallas_call(
        second_kernel,
        out_shape=[struct(*tile)] * 2,
        in_specs=[VMEM] * (10 + 7 * count),
        out_specs=[VMEM] * 2,
        scratch_shapes=scratch,
        compiler_params=PARAMS,
        name="second_round",
    )(orbitals, received, *local, own, sibling, *exchange(packed))

    slots = [keep, swap(give)]
    for d in range(1, bands):
        same, crossed = [], []
        for y in range(lax.axis_size("gy")):
            for b in range(bands):
                to = (b + d) % bands
                same.append((y * bands + b, y * bands + to))
                crossed.append((y * bands + b, (y ^ 1) * bands + to))
        slots.append(lax.ppermute(keep, ("gy", "band"), same))
        slots.append(lax.ppermute(give, ("gy", "band"), crossed))
    partial_value = pl.pallas_call(
        functools.partial(correlation_kernel, bands),
        out_shape=struct(8, LANES),
        in_specs=[VMEM] * len(slots),
        out_specs=VMEM,
        compiler_params=PARAMS,
        name="correlation",
    )(*slots)
    correlation = summed(summed(partial_value, "gy"), "gx")
    return pl.pallas_call(
        functools.partial(basis_kernel, bands, cells),
        out_shape=struct(*orbitals.shape),
        in_specs=[SMEM, SMEM] + [VMEM] * len(slots),
        out_specs=VMEM,
        scratch_shapes=[pltpu.VMEM((2 * bands, 2 * bands, 8, LANES), jnp.float32)],
        compiler_params=PARAMS,
        name="basis",
    )(correlation, order, *slots)


def solution(mesh):
    in_specs = (P("band", "gx", "gy", None), P("gx", "gy", None), P())
    out_specs = P("band", "gx", "gy", None)
    return jax.shard_map(
        per_device, mesh=mesh, in_specs=in_specs, out_specs=out_specs, check_vma=False
    )
```

```python
import functools

import jax
import jax.numpy as jnp
from jax import lax
from jax.experimental import pallas as pl
from jax.experimental.pallas import tpu as pltpu
from jax.sharding import PartitionSpec as P

STEPS = 4
HALO = 2 * STEPS
PAD = 8
LANES = 128
PLANES = 4
NEAR = -(2.0 / 3.0) / 4.25
FAR = (1.0 / 24.0) / 4.25
VMEM = pl.BlockSpec(memory_space=pltpu.VMEM)
SMEM = pl.BlockSpec(memory_space=pltpu.SMEM)
PARAMS = pltpu.CompilerParams(vmem_limit_bytes=40 * 1024 * 1024)


def struct(*shape):
    return jax.ShapeDtypeStruct(shape, jnp.float32)


def place():
    along_y = lax.axis_index("gy")
    return along_y % 2, along_y // 2, lax.axis_index("gx")


def one_sided():
    return lax.axis_size("gy") == 4


def tile_count():
    return 3 if one_sided() else 4


def y_phases():
    return range(1 if one_sided() else 2)


def upward(position, phase):
    return (position % 2) == phase


def own_slots(core, chip):
    first = chip if one_sided() else 1
    return first + core, first + 1 - core


def halo_slot(chip, up):
    first = chip if one_sided() else 1
    return jnp.where(up, first + 2, first - 1)


def rows_of(slot):
    return pl.ds(pl.multiple_of(PAD + 8 * slot, 8), 8)


def put(window, first_plane, rows, planes, change=lambda a: a):
    count = planes.shape[0]
    for half in range(2):
        lanes = slice(half * LANES, (half + 1) * LANES)
        window[half, pl.ds(first_plane, count), rows, :] = change(planes[:, :, lanes])


def halo_start(right, width, count):
    return jnp.where(right, HALO + width, HALO - count)


def fill(window, tiles, x_halos, y_halos, corners, change=lambda a: a):
    core, chip, along_x = place()
    width = tiles[0].shape[0]
    slots = own_slots(core, chip)
    for index, slot in enumerate(slots):
        put(window, HALO, rows_of(slot), tiles[index], change)
        for phase in range(2):
            halo = x_halos[phase].at[index]
            start = halo_start(upward(along_x, phase), width, halo.shape[0])
            put(window, start, rows_of(slot), halo, change)
    for phase in y_phases():
        rows = rows_of(halo_slot(chip, upward(chip, phase)))
        if y_halos is not None:
            put(window, HALO, rows, y_halos[phase], change)
        for x_phase in range(2):
            corner = corners[2 * phase + x_phase]
            start = halo_start(upward(along_x, x_phase), width, corner.shape[0])
            put(window, start, rows, corner, change)


def near_planes(right, width, count):
    return pl.ds(jnp.where(right, width - count, 0), count)


def z_matrix(depth):
    gap = jnp.abs(
        lax.broadcasted_iota(jnp.int32, (depth, depth), 0)
        - lax.broadcasted_iota(jnp.int32, (depth, depth), 1)
    )
    return jnp.where(gap == 1, -16.0, jnp.where(gap == 2, 1.0, 0.0)).astype(jnp.bfloat16)


def stencil(source, target, local, x, along_z, first):
    height = source.shape[2] - 2 * PAD
    body = slice(PAD, PAD + height)
    now = pl.ds(x, PLANES)
    values = [source[half, now, body, :] for half in range(2)]
    high = [v.astype(jnp.bfloat16) for v in values]
    low = [(v - h.astype(jnp.float32)).astype(jnp.bfloat16) for v, h in zip(values, high)]

    def joined(parts):
        return jnp.concatenate([p.reshape(PLANES * height, LANES) for p in parts], axis=1)

    z_sum = jnp.dot(joined(high), along_z, preferred_element_type=jnp.float32)
    z_sum = z_sum + jnp.dot(joined(low), along_z, preferred_element_type=jnp.float32)
    scale = 1.0 if first else 2.0
    for half in range(2):
        near = source[half, pl.ds(x - 1, PLANES), body, :] + source[half, pl.ds(x + 1, PLANES), body, :]
        near = near + source[half, now, PAD - 1 : PAD - 1 + height, :]
        near = near + source[half, now, PAD + 1 : PAD + 1 + height, :]
        far = source[half, pl.ds(x - 2, PLANES), body, :] + source[half, pl.ds(x + 2, PLANES), body, :]
        far = far + source[half, now, PAD - 2 : PAD - 2 + height, :]
        far = far + source[half, now, PAD + 2 : PAD + 2 + height, :]
        far = far + z_sum[:, half * LANES : (half + 1) * LANES].reshape(PLANES, height, LANES)
        result = local[half, now, body, :] * values[half] * scale
        result = result + near * (NEAR * scale) + far * (FAR * scale)
        if not first:
            result = result - target[half, now, body, :]
        target[half, now, body, :] = result


def four_steps(a, b, local, along_z):
    extent = a.shape[1]
    height = a.shape[2] - 2 * PAD
    for buffer in (a, b):
        for rows in (slice(0, PAD), slice(PAD + height, PAD + height + PAD)):
            buffer[:, :, rows, :] = jnp.zeros((2, extent, PAD, LANES), jnp.float32)
    outside_is_zero(a)
    buffers = (a, b)
    for step in range(STEPS):
        source, target = buffers[step % 2], buffers[(step + 1) % 2]
        low = 2 * (step + 1)
        blocks = (extent - 2 * low) // PLANES

        def block(index, carry, source=source, target=target, low=low, step=step):
            stencil(source, target, local, low + index * PLANES, along_z, step == 0)
            return carry

        lax.fori_loop(0, blocks, block, 0, unroll=2)
        if step < STEPS - 1:
            outside_is_zero(target)


def outside_is_zero(window):
    _, chip, along_x = place()
    extent = window.shape[1]

    def clear(where, planes, rows=slice(None)):
        @pl.when(where)
        def _():
            region = window[:, planes, rows, :]
            window[:, planes, rows, :] = jnp.zeros_like(region)

    clear(along_x == 0, slice(0, HALO))
    clear(along_x == lax.axis_size("gx") - 1, slice(extent - HALO, extent))
    if not one_sided():
        clear(chip == 0, slice(None), slice(PAD, PAD + 8))
        clear(chip == lax.axis_size("gy") // 2 - 1, slice(None), slice(PAD + 24, PAD + 32))


def edge_is_own(core, chip, phase):
    return core == jnp.where(upward(chip, phase), 1, 0)


def load_kernel(orbitals, potential, orbitals_out, potential_out, arrived):
    copies = [
        pltpu.make_async_copy(orbitals, orbitals_out, arrived.at[0]),
        pltpu.make_async_copy(potential, potential_out, arrived.at[1]),
    ]
    for copy in copies:
        copy.start()
    for copy in copies:
        copy.wait()


def pack_kernel(orbitals, received, potential, received_potential, *outs):
    core, chip, along_x = place()
    width = potential.shape[0]
    y_out = outs[: len(y_phases())]
    x_out = outs[len(y_phases()) : len(y_phases()) + 2]
    d_out = outs[len(y_phases()) + 2 :]
    tiles = (orbitals.at[core], received.at[core])
    local = (potential, received_potential)
    for x_phase in range(2):
        right = upward(along_x, x_phase)
        for t in range(2):
            x_out[x_phase][t, :HALO] = tiles[t][near_planes(right, width, HALO)]
            x_out[x_phase][t, HALO:] = local[t][near_planes(right, width, HALO - 2)]
    for phase in y_phases():
        own = edge_is_own(core, chip, phase)
        for t, chosen in enumerate((own, jnp.logical_not(own))):

            @pl.when(chosen)
            def _(t=t, phase=phase):
                y_out[phase][:width] = tiles[t][...]
                half = width // 2
                y_out[phase][width:] = local[t][pl.ds(core * half, half)]
                for x_phase in range(2):
                    right = upward(along_x, x_phase)
                    out = d_out[2 * phase + x_phase]
                    out[: HALO - 1] = tiles[t][near_planes(right, width, HALO - 1)]
                    out[HALO - 1 :] = local[t][near_planes(right, width, HALO - 3)]


def fill_local(window, potential, received_potential, passed, y_halos, x_halos, corners):
    core, chip, _ = place()
    width = potential.shape[0]
    half = width // 2

    def change(v):
        return (v - 0.5) / 4.25

    fill(
        window,
        (potential, received_potential),
        [x.at[:, HALO:] for x in x_halos],
        None,
        [c.at[HALO - 1 :] for c in corners],
        change,
    )
    for phase in y_phases():
        rows = rows_of(halo_slot(chip, upward(chip, phase)))
        put(window, HALO + core * half, rows, y_halos[phase].at[width:], change)
        put(window, HALO + (1 - core) * half, rows, passed[phase], change)


def first_kernel(*refs):
    count = len(y_phases())
    orbitals, received, potential, received_potential = refs[:4]
    passed, halos = refs[4 : 4 + count], refs[4 + count : 6 + 4 * count]
    y_halos, x_halos, corners = halos_of(halos)
    own_out, other_out = refs[6 + 4 * count : 8 + 4 * count]
    outs = refs[8 + 4 * count : 10 + 7 * count]
    a, b, local = refs[10 + 7 * count :]
    core, chip, along_x = place()
    width, depth = potential.shape[0], potential.shape[2]
    fill(
        a,
        (orbitals.at[core], received.at[core]),
        [x.at[:, :HALO] for x in x_halos],
        [y.at[:width] for y in y_halos],
        [c.at[: HALO - 1] for c in corners],
    )
    fill_local(local, potential, received_potential, passed, *halos_of(halos))
    four_steps(a, b, local, z_matrix(depth))
    y_out, x_out, d_out = outs[:count], outs[count : count + 2], outs[count + 2 :]
    slots = own_slots(core, chip)
    for half in range(2):
        lanes = slice(half * LANES, (half + 1) * LANES)

        def planes(slot, start, size, half=half):
            return a[half, pl.ds(HALO + start, size), rows_of(slot), :]

        def ends(right, size):
            return jnp.where(right, width - size, 0)

        for t, out in enumerate((own_out, other_out)):
            out[:, :, lanes] = planes(slots[t], 0, width)
            for x_phase in range(2):
                start = ends(upward(along_x, x_phase), HALO)
                x_out[x_phase][t, :, :, lanes] = planes(slots[t], start, HALO)
        for phase in y_phases():
            slot = jnp.where(edge_is_own(core, chip, phase), *slots)
            y_out[phase][:, :, lanes] = planes(slot, 0, width)
            for x_phase in range(2):
                start = ends(upward(along_x, x_phase), HALO - 1)
                d_out[2 * phase + x_phase][:, :, lanes] = planes(slot, start, HALO - 1)


def halos_of(refs):
    count = len(y_phases())
    return refs[:count], refs[count : count + 2], refs[count + 2 :]


def second_kernel(*refs):
    count = len(y_phases())
    orbitals, received, potential, received_potential = refs[:4]
    passed, local_halos = refs[4 : 4 + count], refs[4 + count : 6 + 4 * count]
    own, other = refs[6 + 4 * count : 8 + 4 * count]
    halos = refs[8 + 4 * count : 10 + 7 * count]
    keep, give = refs[10 + 7 * count : 12 + 7 * count]
    early = refs[12 + 7 * count : -3]
    a, b, local = refs[-3:]
    core, chip, _ = place()
    width, depth = potential.shape[0], potential.shape[2]
    y_halos, x_halos, corners = halos_of(halos)
    fill(a, (own, other), x_halos, y_halos, corners)
    fill_local(local, potential, received_potential, passed, *halos_of(local_halos))
    four_steps(a, b, local, z_matrix(depth))
    start = (orbitals.at[core], received.at[core])
    outs = (keep, give)
    for t, slot in enumerate(own_slots(core, chip)):
        for half in range(2):
            lanes = slice(half * LANES, (half + 1) * LANES)
            tile = a[half, HALO : HALO + width, rows_of(slot), :]
            outs[t][:, :, lanes] = 2.0 * tile - start[t][:, :, lanes]
    half = width // 2
    for d in range(1, lax.axis_size("band")):
        upper, _ = halves_met(d)
        for out, whole in zip(early[2 * d - 2 : 2 * d], outs):
            out[...] = whole[pl.ds(upper * half, half)]


def halves_met(d):
    bands, band = lax.axis_size("band"), lax.axis_index("band")
    to, source = lax.rem(band + d, bands), lax.rem(band + bands - d, bands)
    return jnp.where(band < to, 1, 0), jnp.where(source < band, 1, 0)


def late_kernel(keep, sibling, *outs):
    half = keep.shape[0] // 2
    for d, out in enumerate(outs, 1):
        upper, _ = halves_met(d)
        for t, whole in enumerate((keep, sibling)):
            out[t] = whole[pl.ds((1 - upper) * half, half)]


def slot_orbitals(bands):
    core, _, _ = place()
    band = lax.axis_index("band")
    names = []
    for d in range(bands):
        group = lax.rem(band + bands - d, bands)
        names += [2 * group + core, 2 * group + 1 - core]
    return names


def correlation_kernel(*refs):
    bands = lax.axis_size("band")
    own, early, out = refs[:2], refs[2:-1], refs[-1]
    names = slot_orbitals(bands)
    row = lax.broadcasted_iota(jnp.int32, (8, LANES), 0)
    column = lax.broadcasted_iota(jnp.int32, (8, LANES), 1)
    pairs = [(0, 0), (0, 1), (1, 1)] + [(i, 2 * d + j) for d in range(1, bands) for i in range(2) for j in range(2)]
    width, height, depth = own[0].shape
    half = width // 2

    def summed_up(value):
        total = jnp.sum(value, axis=0)
        return sum(total[:, k * LANES : (k + 1) * LANES] for k in range(depth // LANES))

    def body(index, totals):
        def planes(ref, upper):
            return ref[pl.ds(upper * half + index * PLANES, PLANES)]

        halves = [[planes(ref, upper) for ref in own] for upper in range(2)]
        found = []
        for (i, j), total in zip(pairs, totals):
            if j < 2:
                total = total + summed_up(halves[0][i] * halves[0][j] + halves[1][i] * halves[1][j])
            else:
                _, upper = halves_met(j // 2)
                total = total + summed_up(planes(own[i], upper) * planes(early[j - 2], 0))
            found.append(total)
        return tuple(found)

    zero = jnp.zeros((height, LANES), jnp.float32)
    totals = lax.fori_loop(0, half // PLANES, body, (zero,) * len(pairs))
    result = jnp.zeros((8, LANES), jnp.float32)
    for (i, j), total in zip(pairs, totals):
        here = ((row == names[i]) & (column == names[j])) | ((row == names[j]) & (column == names[i]))
        result = jnp.where(here, jnp.sum(total), result)
    out[...] = result


def basis_kernel(bands, cells, *refs):
    correlation, order = refs[:2]
    early, late = refs[4 : 2 + 2 * bands], refs[2 + 2 * bands : 1 + 3 * bands]
    out, mixing = refs[1 + 3 * bands : 3 + 3 * bands]
    joined = refs[3 + 3 * bands :]
    slots = list(refs[2:4]) + list(joined)
    for d in range(1, bands):
        _, upper = halves_met(d)
        for t in range(2):
            whole = joined[2 * d - 2 + t]
            half = whole.shape[0] // 2
            whole[pl.ds(upper * half, half)] = early[2 * d - 2 + t][...]
            whole[pl.ds((1 - upper) * half, half)] = late[d - 1][t]
    names = slot_orbitals(bands)
    count = 2 * bands
    band = lax.axis_index("band")

    def splat(value):
        return jnp.full((8, LANES), value, jnp.float32)

    at = [order[p] for p in range(count)]
    mixing[...] = jnp.zeros_like(mixing)
    lower = {}
    inverse_diagonal = []
    for j in range(count):
        for i in range(j, count):
            total = splat(correlation[at[i], at[j]]) * (1.0 / cells)
            for k in range(j):
                total = total - lower[i, k] * lower[j, k]
            if i == j:
                diagonal = jnp.sqrt(total)
                inverse_diagonal.append(1.0 / diagonal)
            else:
                lower[i, j] = total * inverse_diagonal[j]
    inverse = {}
    for j in range(count):
        inverse[j, j] = inverse_diagonal[j]
        for i in range(j + 1, count):
            total = lower[i, j] * inverse[j, j]
            for k in range(j + 1, i):
                total = total + lower[i, k] * inverse[k, j]
            inverse[i, j] = -total * inverse_diagonal[i]
    for (i, j), value in inverse.items():
        mixing[at[i], at[j]] = value
    width, _, depth = slots[0].shape
    for r in range(2):
        factors = [mixing[2 * band + r, name] for name in names]

        def body(x, carry, r=r, factors=factors):
            for half in range(depth // LANES):
                lanes = slice(half * LANES, (half + 1) * LANES)
                total = factors[0] * slots[0][x, :, lanes]
                for factor, slot in zip(factors[1:], slots[1:]):
                    total = total + factor * slot[x, :, lanes]
                out[r, x, :, lanes] = total
            return carry

        lax.fori_loop(0, width, body, 0, unroll=4)


def partner(position, phase, count):
    other = position + 1 if position % 2 == phase else position - 1
    return other if 0 <= other < count else None


def meet(value, x_phase=None, y_phase=None):
    nx, ny = lax.axis_size("gx"), lax.axis_size("gy")
    pairs = []
    for x in range(nx):
        for y in range(ny):
            to_x = x if x_phase is None else partner(x, x_phase, nx)
            chip = y // 2 if y_phase is None else partner(y // 2, y_phase, ny // 2)
            if to_x is None or chip is None:
                pairs.append((x * ny + y, x * ny + (y ^ 1)))
            else:
                pairs.append((x * ny + y, to_x * ny + chip * 2 + y % 2))
    return lax.ppermute(value, ("gx", "gy"), pairs)


def swap(value):
    count = lax.axis_size("gy")
    return lax.ppermute(value, "gy", [(y, y ^ 1) for y in range(count)])


def to_band(value, d, crossed=False):
    bands = lax.axis_size("band")
    pairs = []
    for y in range(lax.axis_size("gy")):
        for band in range(bands):
            pairs.append((y * bands + band, (y ^ crossed) * bands + (band + d) % bands))
    return lax.ppermute(value, ("gy", "band"), pairs)


def exchange(payloads):
    count = len(y_phases())
    halos = [meet(payloads[phase], y_phase=phase) for phase in y_phases()]
    halos += [meet(payloads[count + phase], x_phase=phase) for phase in range(2)]
    for y_phase in y_phases():
        for x_phase in range(2):
            halos.append(meet(payloads[count + 2 + 2 * y_phase + x_phase], x_phase, y_phase))
    return halos


def summed(value, axis):
    count = lax.axis_size(axis)
    if count & (count - 1):
        return lax.psum(value, axis)

    def of(step):
        return lax.ppermute(value, axis, [(i, i ^ step) for i in range(count)])

    if count == 4:
        return (value + of(1)) + (of(2) + of(3))
    step = 1
    while step < count:
        value = value + of(step)
        step *= 2
    return value


def per_device(orbitals, potential, order):
    group, width, height, depth = orbitals.shape
    bands = lax.axis_size("band")
    cells = float(width * lax.axis_size("gx") * height * lax.axis_size("gy") * depth)
    count = len(y_phases())
    window = (2, width + 2 * HALO, 8 * tile_count() + 2 * PAD, LANES)
    scratch = [pltpu.VMEM(window, jnp.float32)] * 3

    received = swap(orbitals)
    received_potential = swap(potential)
    tile = (width, height, depth)
    orbitals, potential = pl.pallas_call(
        load_kernel,
        out_shape=[struct(*orbitals.shape), struct(*tile)],
        in_specs=[pl.BlockSpec(memory_space=pl.ANY)] * 2,
        out_specs=[VMEM] * 2,
        scratch_shapes=[pltpu.SemaphoreType.DMA((2,))],
        compiler_params=PARAMS,
        name="load",
    )(orbitals, potential)

    def payloads(in_y, in_x, in_corner):
        return (
            [struct(in_y, height, depth)] * count
            + [struct(2, in_x, height, depth)] * 2
            + [struct(in_corner, height, depth)] * (2 * count)
        )

    packed = pl.pallas_call(
        pack_kernel,
        out_shape=payloads(width + width // 2, 2 * HALO - 2, 2 * HALO - 4),
        in_specs=[VMEM] * 4,
        out_specs=[VMEM] * (2 + 3 * count),
        compiler_params=PARAMS,
        name="pack",
    )(orbitals, received, potential, received_potential)
    halos = exchange(packed)
    passed = []
    for phase in y_phases():
        half, *_ = lax.optimization_barrier((halos[phase][width:], *halos[count:]))
        passed.append(swap(half))
    local = (potential, received_potential, *passed, *halos)
    own, sibling, *packed = pl.pallas_call(
        first_kernel,
        out_shape=[struct(*tile)] * 2 + payloads(width, HALO, HALO - 1),
        in_specs=[VMEM] * (6 + 4 * count),
        out_specs=[VMEM] * (4 + 3 * count),
        scratch_shapes=scratch,
        compiler_params=PARAMS,
        name="first_round",
    )(orbitals, received, *local)
    half = (width // 2, height, depth)
    keep, give, *early = pl.pallas_call(
        second_kernel,
        out_shape=[struct(*tile)] * 2 + [struct(*half)] * (2 * bands - 2),
        in_specs=[VMEM] * (10 + 7 * count),
        out_specs=[VMEM] * (2 * bands),
        scratch_shapes=scratch,
        compiler_params=PARAMS,
        name="second_round",
    )(orbitals, received, *local, own, sibling, *exchange(packed))

    early = [to_band(value, 1 + k // 2, crossed=k % 2 == 1) for k, value in enumerate(early)]
    sibling = swap(give)
    late = pl.pallas_call(
        late_kernel,
        out_shape=[struct(2, *half)] * (bands - 1),
        in_specs=[VMEM] * 2,
        out_specs=[VMEM] * (bands - 1),
        compiler_params=PARAMS,
        name="late",
    )(keep, sibling)
    late = [to_band(value, d) for d, value in enumerate(late, 1)]
    partial_value = pl.pallas_call(
        correlation_kernel,
        out_shape=struct(8, LANES),
        in_specs=[VMEM] * (2 * bands),
        out_specs=VMEM,
        compiler_params=PARAMS,
        name="correlation",
    )(keep, sibling, *early)
    correlation = summed(summed(summed(partial_value, "band"), "gy"), "gx")
    return pl.pallas_call(
        functools.partial(basis_kernel, bands, cells),
        out_shape=struct(*orbitals.shape),
        in_specs=[SMEM, SMEM] + [VMEM] * (3 * bands - 1),
        out_specs=VMEM,
        scratch_shapes=[pltpu.VMEM((2 * bands, 2 * bands, 8, LANES), jnp.float32)]
        + [pltpu.VMEM(tile, jnp.float32)] * (2 * bands - 2),
        compiler_params=PARAMS,
        name="basis",
    )(correlation, order, keep, sibling, *early, *late)


def solution(mesh):
    in_specs = (P("band", "gx", "gy", None), P("gx", "gy", None), P())
    out_specs = P("band", "gx", "gy", None)
    return jax.shard_map(
        per_device, mesh=mesh, in_specs=in_specs, out_specs=out_specs, check_vma=False
    )
```

```python
import functools

import jax
import jax.numpy as jnp
from jax import lax
from jax.experimental import pallas as pl
from jax.experimental.pallas import tpu as pltpu
from jax.sharding import PartitionSpec as P

STEPS = 4
HALO = 2 * STEPS
PAD = 8
LANES = 128
PLANES = 4
BY_PRODUCT, BY_ROLLS, UNROLL = 8, 4, 2
NEAR = -(2.0 / 3.0) / 4.25
FAR = (1.0 / 24.0) / 4.25
VMEM = pl.BlockSpec(memory_space=pltpu.VMEM)
SMEM = pl.BlockSpec(memory_space=pltpu.SMEM)
PARAMS = pltpu.CompilerParams(vmem_limit_bytes=40 * 1024 * 1024)


def struct(*shape):
    return jax.ShapeDtypeStruct(shape, jnp.float32)


def place():
    along_y = lax.axis_index("gy")
    return along_y % 2, along_y // 2, lax.axis_index("gx")


def one_sided():
    return lax.axis_size("gy") == 4


def tile_count():
    return 3 if one_sided() else 4


def y_phases():
    return range(1 if one_sided() else 2)


def upward(position, phase):
    return (position % 2) == phase


def own_slots(core, chip):
    first = chip if one_sided() else 1
    return first + core, first + 1 - core


def halo_slot(chip, up):
    first = chip if one_sided() else 1
    return jnp.where(up, first + 2, first - 1)


def rows_of(slot):
    return pl.ds(pl.multiple_of(PAD + 8 * slot, 8), 8)


def put(window, first_plane, rows, planes, change=lambda a: a):
    count = planes.shape[0]
    for half in range(2):
        lanes = slice(half * LANES, (half + 1) * LANES)
        window[half, pl.ds(first_plane, count), rows, :] = change(planes[:, :, lanes])


def halo_start(right, width, count):
    return jnp.where(right, HALO + width, HALO - count)


def corner_plane(right, width, distance):
    return jnp.where(right, HALO + width + distance - 1, HALO - distance)


def put_corner(window, corner, reach, right, up, rows, width, change=lambda a: a):
    for k in range(1, reach // 2 + 1):
        tile = corner[k - 1]
        put(window, corner_plane(right, width, k), rows, tile[None], change)
        if k != reach - k:
            other = jnp.where(up, pltpu.roll(tile, k, 0), pltpu.roll(tile, 8 - k, 0))
            put(window, corner_plane(right, width, reach - k), rows, other[None], change)


def pack_corner(out, plane, reach, up):
    for k in range(1, reach // 2 + 1):
        tile = plane(k)
        if k != reach - k:
            other = plane(reach - k)
            other = jnp.where(up, pltpu.roll(other, k, 0), pltpu.roll(other, 8 - k, 0))
            row = lax.broadcasted_iota(jnp.int32, tile.shape, 0)
            mine = jnp.where(up, row - k, 7 - k - row) >= 0
            tile = jnp.where(mine, tile, other)
        out[k - 1] = tile


def fill(window, tiles, x_halos, y_halos, corners, reach, change=lambda a: a):
    core, chip, along_x = place()
    width = tiles[0].shape[0]
    slots = own_slots(core, chip)
    for index, slot in enumerate(slots):
        put(window, HALO, rows_of(slot), tiles[index], change)
        for phase in range(2):
            halo = x_halos[phase].at[index]
            start = halo_start(upward(along_x, phase), width, halo.shape[0])
            put(window, start, rows_of(slot), halo, change)
    for phase in y_phases():
        up = upward(chip, phase)
        rows = rows_of(halo_slot(chip, up))
        put(window, HALO, rows, y_halos[phase], change)
        for x_phase in range(2):
            corner = corners[2 * phase + x_phase]
            put_corner(window, corner, reach, upward(along_x, x_phase), up, rows, width, change)


def near_planes(right, width, count):
    return pl.ds(jnp.where(right, width - count, 0), count)


def z_matrix(depth):
    gap = jnp.abs(
        lax.broadcasted_iota(jnp.int32, (depth, depth), 0)
        - lax.broadcasted_iota(jnp.int32, (depth, depth), 1)
    )
    return jnp.where(gap == 1, -16.0, jnp.where(gap == 2, 1.0, 0.0)).astype(jnp.bfloat16)


def sides(source, half, x, count, body):
    def at(dx, dy):
        return source[half, pl.ds(x + dx, count), body.start + dy : body.stop + dy, :]

    near = at(-1, 0) + at(1, 0) + at(0, -1) + at(0, 1)
    far = at(-2, 0) + at(2, 0) + at(0, -2) + at(0, 2)
    return near, far


def z_by_product(values, along_z):
    count, height, _ = values[0].shape
    flat = [v.reshape(count * height, LANES) for v in values]
    high = [v.astype(jnp.bfloat16) for v in flat]
    low = [(v - h.astype(jnp.float32)).astype(jnp.bfloat16) for v, h in zip(flat, high)]
    pieces = jnp.concatenate([jnp.concatenate(high, axis=1), jnp.concatenate(low, axis=1)], axis=0)
    both = jnp.dot(pieces, along_z, preferred_element_type=jnp.float32)
    total = both[: count * height] + both[count * height :]
    return [total[:, h * LANES : (h + 1) * LANES].reshape(values[0].shape) for h in range(2)]


def z_by_rolls(values):
    lane = lax.broadcasted_iota(jnp.int32, values[0].shape, 2)
    zero = jnp.zeros_like(values[0])
    found = []
    for distance in (1, 2):
        back = [pltpu.roll(v, distance, 2) for v in values]
        ahead = [pltpu.roll(v, LANES - distance, 2) for v in values]
        first, last = lane < distance, lane >= LANES - distance
        found.append(
            [
                jnp.where(first, zero, back[0]) + jnp.where(last, ahead[1], ahead[0]),
                jnp.where(first, back[0], back[1]) + jnp.where(last, zero, ahead[1]),
            ]
        )
    return found


def stencil(source, target, local, x, by_product, by_rolls, along_z, first):
    height = source.shape[2] - 2 * PAD
    body = slice(PAD, PAD + height)
    scale = 1.0 if first else 2.0
    results = []
    for start, count, product in ((x, by_product, True), (x + by_product, by_rolls, False)):
        if not count:
            continue
        now = pl.ds(start, count)
        values = [source[half, now, body, :] for half in range(2)]
        if product:
            z_far = z_by_product(values, along_z)
        else:
            z_near, z_far = z_by_rolls(values)
        for half in range(2):
            near, far = sides(source, half, start, count, body)
            far = far + z_far[half]
            if not product:
                near = near + z_near[half]
            result = local[half, now, body, :] * values[half] * scale
            result = result + near * (NEAR * scale) + far * (FAR * scale)
            if not first:
                result = result - target[half, now, body, :]
            results.append((half, now, result))
    for half, now, result in results:
        target[half, now, body, :] = result


def four_steps(a, b, local, along_z):
    extent = a.shape[1]
    height = a.shape[2] - 2 * PAD
    for buffer in (a, b):
        for rows in (slice(0, PAD), slice(PAD + height, PAD + height + PAD)):
            buffer[:, :, rows, :] = jnp.zeros((2, extent, PAD, LANES), jnp.float32)
    outside_is_zero(a)
    buffers = (a, b)
    for step in range(STEPS):
        source, target = buffers[step % 2], buffers[(step + 1) % 2]
        low = 2 * (step + 1)
        together = BY_PRODUCT + BY_ROLLS
        blocks, rest = divmod(extent - 2 * low, together)

        def block(index, carry, source=source, target=target, low=low, step=step):
            x = low + index * together
            stencil(source, target, local, x, BY_PRODUCT, BY_ROLLS, along_z, step == 0)
            return carry

        lax.fori_loop(0, blocks, block, 0, unroll=UNROLL)
        if rest:
            by_rolls = min(BY_ROLLS, rest // 3)
            x = low + blocks * together
            stencil(source, target, local, x, rest - by_rolls, by_rolls, along_z, step == 0)
        if step < STEPS - 1:
            outside_is_zero(target)


def outside_is_zero(window):
    _, chip, along_x = place()
    extent = window.shape[1]

    def clear(where, planes, rows=slice(None)):
        @pl.when(where)
        def _():
            region = window[:, planes, rows, :]
            window[:, planes, rows, :] = jnp.zeros_like(region)

    clear(along_x == 0, slice(0, HALO))
    clear(along_x == lax.axis_size("gx") - 1, slice(extent - HALO, extent))
    if not one_sided():
        clear(chip == 0, slice(None), slice(PAD, PAD + 8))
        clear(chip == lax.axis_size("gy") // 2 - 1, slice(None), slice(PAD + 24, PAD + 32))


def edge_is_own(core, chip, phase):
    return core == jnp.where(upward(chip, phase), 1, 0)


def load_kernel(orbitals, potential, orbitals_out, potential_out, arrived):
    copies = [
        pltpu.make_async_copy(orbitals, orbitals_out, arrived.at[0]),
        pltpu.make_async_copy(potential, potential_out, arrived.at[1]),
    ]
    for copy in copies:
        copy.start()
    for copy in copies:
        copy.wait()


def pack_kernel(orbitals, received, potential, received_potential, *outs):
    core, chip, along_x = place()
    width = potential.shape[0]
    y_out = outs[: len(y_phases())]
    x_out = outs[len(y_phases()) : len(y_phases()) + 2]
    d_out = outs[len(y_phases()) + 2 :]
    tiles = (orbitals.at[core], received.at[core])
    local = (potential, received_potential)
    for x_phase in range(2):
        right = upward(along_x, x_phase)
        for t in range(2):
            x_out[x_phase][t, :HALO] = tiles[t][near_planes(right, width, HALO)]
            x_out[x_phase][t, HALO:] = local[t][near_planes(right, width, HALO - 2)]
    for phase in y_phases():
        own = edge_is_own(core, chip, phase)
        for t, chosen in enumerate((own, jnp.logical_not(own))):

            @pl.when(chosen)
            def _(t=t, phase=phase):
                y_out[phase][...] = tiles[t][...]
                up = upward(chip, phase)
                for x_phase in range(2):
                    right = upward(along_x, x_phase)
                    out = d_out[2 * phase + x_phase]

                    def plane(k, field, right=right):
                        return field[jnp.where(right, width - k, k - 1)]

                    pack_corner(out, functools.partial(plane, field=tiles[t]), HALO, up)
                    rest = out.at[HALO // 2 :]
                    pack_corner(rest, functools.partial(plane, field=local[t]), HALO - 2, up)


def fill_local(window, potential, received_potential, edge, passed, x_halos, corners):
    core, chip, _ = place()

    def change(v):
        return (v - 0.5) / 4.25

    fill(
        window,
        (potential, received_potential),
        [x.at[:, HALO:] for x in x_halos],
        [edge] * len(y_phases()),
        [c.at[HALO // 2 :] for c in corners],
        HALO - 2,
        change,
    )
    for phase in y_phases():
        up = upward(chip, phase)

        @pl.when(core != jnp.where(up, 1, 0))
        def _(up=up):
            put(window, HALO, rows_of(halo_slot(chip, up)), passed, change)


def first_kernel(*refs):
    count = len(y_phases())
    orbitals, received, potential, received_potential, edge, passed = refs[:6]
    halos = refs[6 : 8 + 3 * count]
    own_out, other_out = refs[8 + 3 * count : 10 + 3 * count]
    outs = refs[10 + 3 * count : 12 + 6 * count]
    a, b, local = refs[12 + 6 * count :]
    core, chip, along_x = place()
    width, depth = potential.shape[0], potential.shape[2]
    y_halos, x_halos, corners = halos_of(halos)
    fill(
        a,
        (orbitals.at[core], received.at[core]),
        [x.at[:, :HALO] for x in x_halos],
        y_halos,
        [c.at[: HALO // 2] for c in corners],
        HALO,
    )
    fill_local(local, potential, received_potential, edge, passed, x_halos, corners)
    four_steps(a, b, local, z_matrix(depth))
    y_out, x_out, d_out = outs[:count], outs[count : count + 2], outs[count + 2 :]
    slots = own_slots(core, chip)
    for half in range(2):
        lanes = slice(half * LANES, (half + 1) * LANES)

        def planes(slot, start, size, half=half):
            return a[half, pl.ds(HALO + start, size), rows_of(slot), :]

        def ends(right, size):
            return jnp.where(right, width - size, 0)

        for t, out in enumerate((own_out, other_out)):
            out[:, :, lanes] = planes(slots[t], 0, width)
            for x_phase in range(2):
                start = ends(upward(along_x, x_phase), HALO)
                x_out[x_phase][t, :, :, lanes] = planes(slots[t], start, HALO)
        for phase in y_phases():
            slot = jnp.where(edge_is_own(core, chip, phase), *slots)
            y_out[phase][:, :, lanes] = planes(slot, 0, width)
            for x_phase in range(2):
                right = upward(along_x, x_phase)

                def plane(k, right=right, slot=slot, planes=planes):
                    return planes(slot, jnp.where(right, width - k, k - 1), 1)[0]

                out = d_out[2 * phase + x_phase].at[:, :, lanes]
                pack_corner(out, plane, HALO, upward(chip, phase))


def halos_of(refs):
    count = len(y_phases())
    return refs[:count], refs[count : count + 2], refs[count + 2 :]


def second_kernel(*refs):
    count = len(y_phases())
    orbitals, received, potential, received_potential, edge, passed = refs[:6]
    local_halos = refs[6 : 8 + 3 * count]
    own, other = refs[8 + 3 * count : 10 + 3 * count]
    halos = refs[10 + 3 * count : 12 + 6 * count]
    keep, give = refs[12 + 6 * count : 14 + 6 * count]
    early = refs[14 + 6 * count : -3]
    a, b, local = refs[-3:]
    core, chip, _ = place()
    width, depth = potential.shape[0], potential.shape[2]
    y_halos, x_halos, corners = halos_of(halos)
    fill(a, (own, other), x_halos, y_halos, corners, HALO)
    _, p_x_halos, p_corners = halos_of(local_halos)
    fill_local(local, potential, received_potential, edge, passed, p_x_halos, p_corners)
    four_steps(a, b, local, z_matrix(depth))
    start = (orbitals.at[core], received.at[core])
    outs = (keep, give)
    for t, slot in enumerate(own_slots(core, chip)):
        for half in range(2):
            lanes = slice(half * LANES, (half + 1) * LANES)
            tile = a[half, HALO : HALO + width, rows_of(slot), :]
            outs[t][:, :, lanes] = 2.0 * tile - start[t][:, :, lanes]
    half = width // 2
    for d in range(1, lax.axis_size("band")):
        upper, _ = halves_met(d)
        for out, whole in zip(early[2 * d - 2 : 2 * d], outs):
            out[...] = whole[pl.ds(upper * half, half)]


def halves_met(d):
    bands, band = lax.axis_size("band"), lax.axis_index("band")
    to, source = lax.rem(band + d, bands), lax.rem(band + bands - d, bands)
    return jnp.where(band < to, 1, 0), jnp.where(source < band, 1, 0)


def late_kernel(keep, sibling, *outs):
    half = keep.shape[0] // 2
    for d, out in enumerate(outs, 1):
        upper, _ = halves_met(d)
        for t, whole in enumerate((keep, sibling)):
            out[t] = whole[pl.ds((1 - upper) * half, half)]


def slot_orbitals(bands):
    core, _, _ = place()
    band = lax.axis_index("band")
    names = []
    for d in range(bands):
        group = lax.rem(band + bands - d, bands)
        names += [2 * group + core, 2 * group + 1 - core]
    return names


def correlation_kernel(*refs):
    bands = lax.axis_size("band")
    own, early, out = refs[:2], refs[2:-1], refs[-1]
    names = slot_orbitals(bands)
    row = lax.broadcasted_iota(jnp.int32, (8, LANES), 0)
    column = lax.broadcasted_iota(jnp.int32, (8, LANES), 1)
    pairs = [(0, 0), (0, 1), (1, 1)] + [(i, 2 * d + j) for d in range(1, bands) for i in range(2) for j in range(2)]
    width, height, depth = own[0].shape
    half = width // 2

    def summed_up(value):
        total = jnp.sum(value, axis=0)
        return sum(total[:, k * LANES : (k + 1) * LANES] for k in range(depth // LANES))

    def body(index, totals):
        def planes(ref, upper):
            return ref[pl.ds(upper * half + index * PLANES, PLANES)]

        halves = [[planes(ref, upper) for ref in own] for upper in range(2)]
        found = []
        for (i, j), total in zip(pairs, totals):
            if j < 2:
                total = total + summed_up(halves[0][i] * halves[0][j] + halves[1][i] * halves[1][j])
            else:
                _, upper = halves_met(j // 2)
                total = total + summed_up(planes(own[i], upper) * planes(early[j - 2], 0))
            found.append(total)
        return tuple(found)

    zero = jnp.zeros((height, LANES), jnp.float32)
    totals = lax.fori_loop(0, half // PLANES, body, (zero,) * len(pairs))
    result = jnp.zeros((8, LANES), jnp.float32)
    for (i, j), total in zip(pairs, totals):
        here = ((row == names[i]) & (column == names[j])) | ((row == names[j]) & (column == names[i]))
        result = jnp.where(here, jnp.sum(total), result)
    out[...] = result


def basis_kernel(bands, cells, *refs):
    correlation, order = refs[:2]
    early, late = refs[4 : 2 + 2 * bands], refs[2 + 2 * bands : 1 + 3 * bands]
    out, mixing = refs[1 + 3 * bands : 3 + 3 * bands]
    joined = refs[3 + 3 * bands :]
    slots = list(refs[2:4]) + list(joined)
    for d in range(1, bands):
        _, upper = halves_met(d)
        for t in range(2):
            whole = joined[2 * d - 2 + t]
            half = whole.shape[0] // 2
            whole[pl.ds(upper * half, half)] = early[2 * d - 2 + t][...]
            whole[pl.ds((1 - upper) * half, half)] = late[d - 1][t]
    names = slot_orbitals(bands)
    count = 2 * bands
    band = lax.axis_index("band")

    def splat(value):
        return jnp.full((8, LANES), value, jnp.float32)

    at = [order[p] for p in range(count)]
    mixing[...] = jnp.zeros_like(mixing)
    lower = {}
    inverse_diagonal = []
    for j in range(count):
        for i in range(j, count):
            total = splat(correlation[at[i], at[j]]) * (1.0 / cells)
            for k in range(j):
                total = total - lower[i, k] * lower[j, k]
            if i == j:
                diagonal = jnp.sqrt(total)
                inverse_diagonal.append(1.0 / diagonal)
            else:
                lower[i, j] = total * inverse_diagonal[j]
    inverse = {}
    for j in range(count):
        inverse[j, j] = inverse_diagonal[j]
        for i in range(j + 1, count):
            total = lower[i, j] * inverse[j, j]
            for k in range(j + 1, i):
                total = total + lower[i, k] * inverse[k, j]
            inverse[i, j] = -total * inverse_diagonal[i]
    for (i, j), value in inverse.items():
        mixing[at[i], at[j]] = value
    width, _, depth = slots[0].shape
    for r in range(2):
        factors = [mixing[2 * band + r, name] for name in names]

        def body(x, carry, r=r, factors=factors):
            for half in range(depth // LANES):
                lanes = slice(half * LANES, (half + 1) * LANES)
                total = factors[0] * slots[0][x, :, lanes]
                for factor, slot in zip(factors[1:], slots[1:]):
                    total = total + factor * slot[x, :, lanes]
                out[r, x, :, lanes] = total
            return carry

        lax.fori_loop(0, width, body, 0, unroll=4)


def partner(position, phase, count):
    other = position + 1 if position % 2 == phase else position - 1
    return other if 0 <= other < count else None


def meet(value, x_phase=None, y_phase=None):
    nx, ny = lax.axis_size("gx"), lax.axis_size("gy")
    pairs = []
    for x in range(nx):
        for y in range(ny):
            to_x = x if x_phase is None else partner(x, x_phase, nx)
            chip = y // 2 if y_phase is None else partner(y // 2, y_phase, ny // 2)
            if to_x is None or chip is None:
                pairs.append((x * ny + y, x * ny + (y ^ 1)))
            else:
                pairs.append((x * ny + y, to_x * ny + chip * 2 + y % 2))
    return lax.ppermute(value, ("gx", "gy"), pairs)


def swap(value):
    count = lax.axis_size("gy")
    return lax.ppermute(value, "gy", [(y, y ^ 1) for y in range(count)])


def to_band(value, d, crossed=False):
    bands = lax.axis_size("band")
    pairs = []
    for y in range(lax.axis_size("gy")):
        for band in range(bands):
            pairs.append((y * bands + band, (y ^ crossed) * bands + (band + d) % bands))
    return lax.ppermute(value, ("gy", "band"), pairs)


def face(value):
    count, bands = lax.axis_size("gy"), lax.axis_size("band")
    pairs = []
    for y in range(count):
        for band in range(bands):
            to = partner(y, 1, count)
            if to is not None:
                pairs.append((y * bands + band, to * bands + band))
            elif bands % 2 == 0:
                pairs.append((y * bands + band, y * bands + (band ^ 1)))
    return lax.ppermute(value, ("gy", "band"), pairs)


def exchange(payloads):
    count = len(y_phases())
    halos = [meet(payloads[phase], y_phase=phase) for phase in y_phases()]
    halos += [meet(payloads[count + phase], x_phase=phase) for phase in range(2)]
    for y_phase in y_phases():
        for x_phase in range(2):
            halos.append(meet(payloads[count + 2 + 2 * y_phase + x_phase], x_phase, y_phase))
    return halos


def summed(value, axis):
    count = lax.axis_size(axis)
    if count & (count - 1):
        return lax.psum(value, axis)

    def of(step):
        return lax.ppermute(value, axis, [(i, i ^ step) for i in range(count)])

    if count == 4:
        return (value + of(1)) + (of(2) + of(3))
    step = 1
    while step < count:
        value = value + of(step)
        step *= 2
    return value


def per_device(orbitals, potential, order):
    group, width, height, depth = orbitals.shape
    bands = lax.axis_size("band")
    cells = float(width * lax.axis_size("gx") * height * lax.axis_size("gy") * depth)
    count = len(y_phases())
    window = (2, width + 2 * HALO, 8 * tile_count() + 2 * PAD, LANES)
    scratch = [pltpu.VMEM(window, jnp.float32)] * 3

    received = swap(orbitals)
    received_potential = swap(potential)
    edge = face(potential)
    tile = (width, height, depth)
    orbitals, potential = pl.pallas_call(
        load_kernel,
        out_shape=[struct(*orbitals.shape), struct(*tile)],
        in_specs=[pl.BlockSpec(memory_space=pl.ANY)] * 2,
        out_specs=[VMEM] * 2,
        scratch_shapes=[pltpu.SemaphoreType.DMA((2,))],
        compiler_params=PARAMS,
        name="load",
    )(orbitals, potential)

    def payloads(in_x, in_corner):
        return (
            [struct(*tile)] * count
            + [struct(2, in_x, height, depth)] * 2
            + [struct(in_corner, height, depth)] * (2 * count)
        )

    packed = pl.pallas_call(
        pack_kernel,
        out_shape=payloads(2 * HALO - 2, HALO - 1),
        in_specs=[VMEM] * 4,
        out_specs=[VMEM] * (2 + 3 * count),
        compiler_params=PARAMS,
        name="pack",
    )(orbitals, received, potential, received_potential)
    halos = exchange(packed)
    edge, *_ = lax.optimization_barrier((edge, *halos))
    passed = swap(edge)
    local = (potential, received_potential, edge, passed, *halos)
    own, sibling, *packed = pl.pallas_call(
        first_kernel,
        out_shape=[struct(*tile)] * 2 + payloads(HALO, HALO // 2),
        in_specs=[VMEM] * (8 + 3 * count),
        out_specs=[VMEM] * (4 + 3 * count),
        scratch_shapes=scratch,
        compiler_params=PARAMS,
        name="first_round",
    )(orbitals, received, *local)
    half = (width // 2, height, depth)
    keep, give, *early = pl.pallas_call(
        second_kernel,
        out_shape=[struct(*tile)] * 2 + [struct(*half)] * (2 * bands - 2),
        in_specs=[VMEM] * (12 + 6 * count),
        out_specs=[VMEM] * (2 * bands),
        scratch_shapes=scratch,
        compiler_params=PARAMS,
        name="second_round",
    )(orbitals, received, *local, own, sibling, *exchange(packed))

    early = [to_band(value, 1 + k // 2, crossed=k % 2 == 1) for k, value in enumerate(early)]
    sibling = swap(give)
    late = pl.pallas_call(
        late_kernel,
        out_shape=[struct(2, *half)] * (bands - 1),
        in_specs=[VMEM] * 2,
        out_specs=[VMEM] * (bands - 1),
        compiler_params=PARAMS,
        name="late",
    )(keep, sibling)
    late = [to_band(value, d) for d, value in enumerate(late, 1)]
    partial_value = pl.pallas_call(
        correlation_kernel,
        out_shape=struct(8, LANES),
        in_specs=[VMEM] * (2 * bands),
        out_specs=VMEM,
        compiler_params=PARAMS,
        name="correlation",
    )(keep, sibling, *early)
    correlation = summed(summed(summed(partial_value, "band"), "gy"), "gx")
    return pl.pallas_call(
        functools.partial(basis_kernel, bands, cells),
        out_shape=struct(*orbitals.shape),
        in_specs=[SMEM, SMEM] + [VMEM] * (3 * bands - 1),
        out_specs=VMEM,
        scratch_shapes=[pltpu.VMEM((2 * bands, 2 * bands, 8, LANES), jnp.float32)]
        + [pltpu.VMEM(tile, jnp.float32)] * (2 * bands - 2),
        compiler_params=PARAMS,
        name="basis",
    )(correlation, order, keep, sibling, *early, *late)


def solution(mesh):
    in_specs = (P("band", "gx", "gy", None), P("gx", "gy", None), P())
    out_specs = P("band", "gx", "gy", None)
    return jax.shard_map(
        per_device, mesh=mesh, in_specs=in_specs, out_specs=out_specs, check_vma=False
    )
```

```python
import functools

import jax
import jax.numpy as jnp
from jax import lax
from jax.experimental import pallas as pl
from jax.experimental.pallas import tpu as pltpu
from jax.sharding import PartitionSpec as P

STEPS = 4
HALO = 2 * STEPS
PAD = 8
LANES = 128
PLANES = 4
OWN_ROWS = slice(PAD + 8, PAD + 24)
HALO_ROWS = (slice(PAD, PAD + 8), slice(PAD + 24, PAD + 32))
TOGETHER = {8: (16, 8, 1), 16: (12, 6, 1), 32: (8, 2, 1)}
NEAR = -(2.0 / 3.0) / 4.25
FAR = (1.0 / 24.0) / 4.25
VMEM = pl.BlockSpec(memory_space=pltpu.VMEM)
SMEM = pl.BlockSpec(memory_space=pltpu.SMEM)
PARAMS = pltpu.CompilerParams(vmem_limit_bytes=16 * 1024 * 1024)


def struct(*shape):
    return jax.ShapeDtypeStruct(shape, jnp.float32)


def place():
    along_y = lax.axis_index("gy")
    return along_y % 2, along_y // 2, lax.axis_index("gx")


def one_sided():
    return lax.axis_size("gy") == 4


def y_phases():
    return range(1 if one_sided() else 2)


def upward(position, phase):
    return (position % 2) == phase


def own_slots(core):
    return 1 + core, 2 - core


def halo_slot(up):
    return jnp.where(up, 3, 0)


def rows_of(slot):
    return pl.ds(pl.multiple_of(PAD + 8 * slot, 8), 8)


def put(window, first_plane, rows, planes, change=lambda a: a):
    count = planes.shape[0]
    for half in range(2):
        lanes = slice(half * LANES, (half + 1) * LANES)
        window[half, pl.ds(first_plane, count), rows, :] = change(planes[:, :, lanes])


def halo_start(right, width, count):
    return jnp.where(right, HALO + width, HALO - count)


def corner_plane(right, width, distance):
    return jnp.where(right, HALO + width + distance - 1, HALO - distance)


def put_corner(window, corner, reach, right, up, rows, width, change=lambda a: a):
    for k in range(1, reach // 2 + 1):
        tile = corner[k - 1]
        put(window, corner_plane(right, width, k), rows, tile[None], change)
        if k != reach - k:
            other = jnp.where(up, pltpu.roll(tile, k, 0), pltpu.roll(tile, 8 - k, 0))
            put(window, corner_plane(right, width, reach - k), rows, other[None], change)


def pack_corner(out, plane, reach, up):
    for k in range(1, reach // 2 + 1):
        tile = plane(k)
        if k != reach - k:
            other = plane(reach - k)
            other = jnp.where(up, pltpu.roll(other, k, 0), pltpu.roll(other, 8 - k, 0))
            row = lax.broadcasted_iota(jnp.int32, tile.shape, 0)
            mine = jnp.where(up, row - k, 7 - k - row) >= 0
            tile = jnp.where(mine, tile, other)
        out[k - 1] = tile


def fill_own(window, tiles, x_halos, change=lambda a: a):
    core, _, along_x = place()
    width = tiles[0].shape[0]
    for index, slot in enumerate(own_slots(core)):
        put(window, HALO, rows_of(slot), tiles[index], change)
    fill_x(window, width, x_halos, change)


def fill_x(window, width, x_halos, change=lambda a: a):
    core, _, along_x = place()
    for index, slot in enumerate(own_slots(core)):
        for phase in range(2):
            halo = x_halos[phase].at[index]
            start = halo_start(upward(along_x, phase), width, halo.shape[0])
            put(window, start, rows_of(slot), halo, change)


def fill_y(window, y_halos, corners, reach, change=lambda a: a):
    _, chip, along_x = place()
    width = window.shape[1] - 2 * HALO
    for phase in y_phases():
        up = upward(chip, phase)
        rows = rows_of(halo_slot(up))
        if y_halos is not None:
            put(window, HALO, rows, y_halos[phase], change)
        for x_phase in range(2):
            corner = corners[2 * phase + x_phase]
            put_corner(window, corner, reach, upward(along_x, x_phase), up, rows, width, change)


def near_planes(right, width, count):
    return pl.ds(jnp.where(right, width - count, 0), count)


def z_matrix(depth):
    gap = jnp.abs(
        lax.broadcasted_iota(jnp.int32, (depth, depth), 0)
        - lax.broadcasted_iota(jnp.int32, (depth, depth), 1)
    )
    return jnp.where(gap == 1, -16.0, jnp.where(gap == 2, 1.0, 0.0)).astype(jnp.bfloat16)


def sides(source, half, x, count, body):
    def at(dx, dy):
        return source[half, pl.ds(x + dx, count), body.start + dy : body.stop + dy, :]

    near = at(-1, 0) + at(1, 0) + at(0, -1) + at(0, 1)
    far = at(-2, 0) + at(2, 0) + at(0, -2) + at(0, 2)
    return near, far


def z_by_product(values, along_z):
    count, height, _ = values[0].shape
    flat = [v.reshape(count * height, LANES) for v in values]
    high = [v.astype(jnp.bfloat16) for v in flat]
    low = [(v - h.astype(jnp.float32)).astype(jnp.bfloat16) for v, h in zip(flat, high)]
    pieces = jnp.concatenate([jnp.concatenate(high, axis=1), jnp.concatenate(low, axis=1)], axis=0)
    both = jnp.dot(pieces, along_z, preferred_element_type=jnp.float32)
    total = both[: count * height] + both[count * height :]
    return [total[:, h * LANES : (h + 1) * LANES].reshape(values[0].shape) for h in range(2)]


def z_by_rolls(values):
    lane = lax.broadcasted_iota(jnp.int32, values[0].shape, 2)
    zero = jnp.zeros_like(values[0])
    found = []
    for distance in (1, 2):
        back = [pltpu.roll(v, distance, 2) for v in values]
        ahead = [pltpu.roll(v, LANES - distance, 2) for v in values]
        first, last = lane < distance, lane >= LANES - distance
        found.append(
            [
                jnp.where(first, zero, back[0]) + jnp.where(last, ahead[1], ahead[0]),
                jnp.where(first, back[0], back[1]) + jnp.where(last, zero, ahead[1]),
            ]
        )
    return found


def stencil(source, previous, target, local, x, by_product, by_rolls, along_z, body):
    scale = 1.0 if previous is None else 2.0
    results = []
    for start, count, product in ((x, by_product, True), (x + by_product, by_rolls, False)):
        if not count:
            continue
        now = pl.ds(start, count)
        values = [source[half, now, body, :] for half in range(2)]
        if product:
            z_far = z_by_product(values, along_z)
        else:
            z_near, z_far = z_by_rolls(values)
        for half in range(2):
            near, far = sides(source, half, start, count, body)
            far = far + z_far[half]
            if not product:
                near = near + z_near[half]
            result = local[half, now, body, :] * values[half] * scale
            result = result + near * (NEAR * scale) + far * (FAR * scale)
            if previous is not None:
                result = result - previous[half, now, body, :]
            results.append((half, now, result))
    for half, now, result in results:
        target[half, now, body, :] = result


def four_steps(levels, local, depth, body, last):
    along_z = z_matrix(depth)
    extent = local.shape[1]
    outside_is_zero(levels[0], body)
    for step in range(STEPS):
        rows = last if step == STEPS - 1 else body
        low = 2 * (step + 1)
        by_product, by_rolls, unroll = TOGETHER[rows.stop - rows.start]
        together = by_product + by_rolls
        blocks, rest = divmod(extent - 2 * low, together)
        previous = levels[step - 1] if step else None

        def do(x, by_product, by_rolls, rows=rows, step=step, previous=previous):
            source, target = levels[step], levels[step + 1]
            stencil(source, previous, target, local, x, by_product, by_rolls, along_z, rows)

        def block(index, carry, do=do, low=low, by_product=by_product, by_rolls=by_rolls):
            do(low + index * (by_product + by_rolls), by_product, by_rolls)
            return carry

        lax.fori_loop(0, blocks, block, 0, unroll=min(unroll, blocks))
        if rest:
            rolled = min(by_rolls, rest // 3)
            do(low + blocks * together, rest - rolled, rolled)
        if step < STEPS - 1:
            outside_is_zero(levels[step + 1], body)


def outside_is_zero(window, body):
    _, chip, along_x = place()
    extent = window.shape[1]

    def clear(where, planes, rows):
        @pl.when(where)
        def _():
            region = window[:, planes, rows, :]
            window[:, planes, rows, :] = jnp.zeros_like(region)

    clear(along_x == 0, slice(0, HALO), body)
    clear(along_x == lax.axis_size("gx") - 1, slice(extent - HALO, extent), body)
    if not one_sided():
        clear(chip == 0, slice(None), HALO_ROWS[0])
        clear(chip == lax.axis_size("gy") // 2 - 1, slice(None), HALO_ROWS[1])


def first_part(levels, local, depth):
    if not one_sided():
        return
    _, chip, _ = place()
    for position in range(2):

        @pl.when(chip == position)
        def _(position=position):
            for window in levels[:STEPS]:
                region = window[:, :, HALO_ROWS[position], :]
                window[:, :, HALO_ROWS[position], :] = jnp.zeros_like(region)

    four_steps(levels, local, depth, OWN_ROWS, OWN_ROWS)


def second_part(levels, local, depth):
    if not one_sided():
        four_steps(levels, local, depth, slice(PAD, PAD + 32), OWN_ROWS)
        return
    _, chip, _ = place()
    for position in range(2):
        inner = slice(PAD + 16, PAD + 24) if position == 0 else slice(PAD + 8, PAD + 16)
        body = slice(PAD + 16, PAD + 32) if position == 0 else slice(PAD, PAD + 16)

        @pl.when(chip == position)
        def _(inner=inner, body=body):
            four_steps(levels, local, depth, body, inner)


def edge_is_own(core, chip, phase):
    return core == jnp.where(upward(chip, phase), 1, 0)


def load_kernel(orbitals, potential, orbitals_out, potential_out, arrived):
    copies = [
        pltpu.make_async_copy(orbitals, orbitals_out, arrived.at[0]),
        pltpu.make_async_copy(potential, potential_out, arrived.at[1]),
    ]
    for copy in copies:
        copy.start()
    for copy in copies:
        copy.wait()


def pack_kernel(orbitals, received, potential, received_potential, *outs):
    core, chip, along_x = place()
    width = potential.shape[0]
    y_out = outs[: len(y_phases())]
    x_out = outs[len(y_phases()) : len(y_phases()) + 2]
    d_out = outs[len(y_phases()) + 2 :]
    tiles = (orbitals.at[core], received.at[core])
    local = (potential, received_potential)
    for x_phase in range(2):
        right = upward(along_x, x_phase)
        for t in range(2):
            x_out[x_phase][t, :HALO] = tiles[t][near_planes(right, width, HALO)]
            x_out[x_phase][t, HALO:] = local[t][near_planes(right, width, HALO - 2)]
    for phase in y_phases():
        own = edge_is_own(core, chip, phase)
        for t, chosen in enumerate((own, jnp.logical_not(own))):

            @pl.when(chosen)
            def _(t=t, phase=phase):
                y_out[phase][:width] = tiles[t][...]
                half = width // 2
                y_out[phase][width:] = local[t][pl.ds(core * half, half)]
                up = upward(chip, phase)
                for x_phase in range(2):
                    right = upward(along_x, x_phase)
                    out = d_out[2 * phase + x_phase]

                    def plane(k, field, right=right):
                        return field[jnp.where(right, width - k, k - 1)]

                    pack_corner(out, functools.partial(plane, field=tiles[t]), HALO, up)
                    rest = out.at[HALO // 2 :]
                    pack_corner(rest, functools.partial(plane, field=local[t]), HALO - 2, up)


def halos_of(refs):
    count = len(y_phases())
    return refs[:count], refs[count : count + 2], refs[count + 2 :]


def diagonal(potential):
    return (potential - 0.5) / 4.25


def first_own_kernel(orbitals, received, potential, received_potential, x_a, x_b, *outs):
    levels, local = outs[:-1], outs[-1]
    core, _, _ = place()
    x_halos = (x_a, x_b)
    tiles = (orbitals.at[core], received.at[core])
    fill_own(levels[0], tiles, [x.at[:, :HALO] for x in x_halos])
    tiles = (potential, received_potential)
    fill_own(local, tiles, [x.at[:, HALO:] for x in x_halos], diagonal)
    first_part(levels, local, potential.shape[2])


def first_rest_kernel(*refs):
    count = len(y_phases())
    passed, y_halos = refs[6 : 6 + count], refs[6 + count : 6 + 2 * count]
    corners, outs = refs[6 + 2 * count : 6 + 4 * count], refs[6 + 4 * count :]
    levels, local = outs[: STEPS + 1], outs[STEPS + 1]
    payloads = outs[STEPS + 2 :]
    core, chip, along_x = place()
    width, depth = local.shape[1] - 2 * HALO, 2 * LANES
    fill_y(levels[0], [y.at[:width] for y in y_halos], [c.at[: HALO // 2] for c in corners], HALO)
    fill_y(local, None, [c.at[HALO // 2 :] for c in corners], HALO - 2, diagonal)
    half = width // 2
    for phase in y_phases():
        rows = rows_of(halo_slot(upward(chip, phase)))
        put(local, HALO + core * half, rows, y_halos[phase].at[width:], diagonal)
        put(local, HALO + (1 - core) * half, rows, passed[phase], diagonal)

    second_part(levels, local, depth)
    y_out, x_out, d_out = halos_of(payloads)
    slots = own_slots(core)
    result = levels[STEPS]
    for half in range(2):
        lanes = slice(half * LANES, (half + 1) * LANES)

        def planes(slot, start, size, half=half):
            return result[half, pl.ds(HALO + start, size), rows_of(slot), :]

        for t in range(2):
            for x_phase in range(2):
                start = jnp.where(upward(along_x, x_phase), width - HALO, 0)
                x_out[x_phase][t, :, :, lanes] = planes(slots[t], start, HALO)
        for phase in y_phases():
            slot = jnp.where(edge_is_own(core, chip, phase), *slots)
            y_out[phase][:, :, lanes] = planes(slot, 0, width)
            for x_phase in range(2):
                right = upward(along_x, x_phase)

                def plane(k, right=right, slot=slot, planes=planes):
                    return planes(slot, jnp.where(right, width - k, k - 1), 1)[0]

                out = d_out[2 * phase + x_phase].at[:, :, lanes]
                pack_corner(out, plane, HALO, upward(chip, phase))


def second_own_kernel(before, local, x_a, x_b, *levels):
    width = before.shape[1] - 2 * HALO
    for half in range(2):
        inside = (half, slice(HALO, HALO + width), OWN_ROWS)
        levels[0][inside] = before[inside]
    fill_x(levels[0], width, (x_a, x_b))
    first_part(levels, local, LANES * 2)


def second_rest_kernel(*refs):
    count = len(y_phases())
    local, orbitals, received = refs[STEPS + 1 : STEPS + 4]
    refs = refs[STEPS + 4 :]
    y_halos, corners = refs[:count], refs[count : 3 * count]
    levels, outs = refs[3 * count : 3 * count + STEPS + 1], refs[3 * count + STEPS + 1 :]
    outs, early = outs[:2], outs[2:]
    core, _, _ = place()
    width, depth = orbitals.shape[1], orbitals.shape[3]
    fill_y(levels[0], y_halos, corners, HALO)
    second_part(levels, local, depth)
    start = (orbitals.at[core], received.at[core])
    for t, slot in enumerate(own_slots(core)):
        for half in range(2):
            lanes = slice(half * LANES, (half + 1) * LANES)
            tile = levels[STEPS][half, HALO : HALO + width, rows_of(slot), :]
            outs[t][:, :, lanes] = 2.0 * tile - start[t][:, :, lanes]
    half = width // 2
    for d in range(1, lax.axis_size("band")):
        upper, _ = halves_met(d)
        for out, whole in zip(early[2 * d - 2 : 2 * d], outs):
            out[...] = whole[pl.ds(upper * half, half)]


def halves_met(d):
    bands, band = lax.axis_size("band"), lax.axis_index("band")
    to, source = lax.rem(band + d, bands), lax.rem(band + bands - d, bands)
    return jnp.where(band < to, 1, 0), jnp.where(source < band, 1, 0)


def late_kernel(keep, sibling, *outs):
    half = keep.shape[0] // 2
    for d, out in enumerate(outs, 1):
        upper, _ = halves_met(d)
        for t, whole in enumerate((keep, sibling)):
            out[t] = whole[pl.ds((1 - upper) * half, half)]


def slot_orbitals(bands):
    core, _, _ = place()
    band = lax.axis_index("band")
    names = []
    for d in range(bands):
        group = lax.rem(band + bands - d, bands)
        names += [2 * group + core, 2 * group + 1 - core]
    return names


def correlation_kernel(*refs):
    bands = lax.axis_size("band")
    own, early, out = refs[:2], refs[2:-1], refs[-1]
    names = slot_orbitals(bands)
    row = lax.broadcasted_iota(jnp.int32, (8, LANES), 0)
    column = lax.broadcasted_iota(jnp.int32, (8, LANES), 1)
    pairs = [(0, 0), (0, 1), (1, 1)] + [(i, 2 * d + j) for d in range(1, bands) for i in range(2) for j in range(2)]
    width, height, depth = own[0].shape
    half = width // 2

    def summed_up(value):
        total = jnp.sum(value, axis=0)
        return sum(total[:, k * LANES : (k + 1) * LANES] for k in range(depth // LANES))

    def body(index, totals):
        def planes(ref, upper):
            return ref[pl.ds(upper * half + index * PLANES, PLANES)]

        halves = [[planes(ref, upper) for ref in own] for upper in range(2)]
        found = []
        for (i, j), total in zip(pairs, totals):
            if j < 2:
                total = total + summed_up(halves[0][i] * halves[0][j] + halves[1][i] * halves[1][j])
            else:
                _, upper = halves_met(j // 2)
                total = total + summed_up(planes(own[i], upper) * planes(early[j - 2], 0))
            found.append(total)
        return tuple(found)

    zero = jnp.zeros((height, LANES), jnp.float32)
    totals = lax.fori_loop(0, half // PLANES, body, (zero,) * len(pairs))
    result = jnp.zeros((8, LANES), jnp.float32)
    for (i, j), total in zip(pairs, totals):
        here = ((row == names[i]) & (column == names[j])) | ((row == names[j]) & (column == names[i]))
        result = jnp.where(here, jnp.sum(total), result)
    out[...] = result


def basis_kernel(bands, cells, *refs):
    correlation, order = refs[:2]
    early, late = refs[4 : 2 + 2 * bands], refs[2 + 2 * bands : 1 + 3 * bands]
    out, mixing = refs[1 + 3 * bands : 3 + 3 * bands]
    joined = refs[3 + 3 * bands :]
    slots = list(refs[2:4]) + list(joined)
    for d in range(1, bands):
        _, upper = halves_met(d)
        for t in range(2):
            whole = joined[2 * d - 2 + t]
            half = whole.shape[0] // 2
            whole[pl.ds(upper * half, half)] = early[2 * d - 2 + t][...]
            whole[pl.ds((1 - upper) * half, half)] = late[d - 1][t]
    names = slot_orbitals(bands)
    count = 2 * bands
    band = lax.axis_index("band")

    def splat(value):
        return jnp.full((8, LANES), value, jnp.float32)

    at = [order[p] for p in range(count)]
    mixing[...] = jnp.zeros_like(mixing)
    lower = {}
    inverse_diagonal = []
    for j in range(count):
        for i in range(j, count):
            total = splat(correlation[at[i], at[j]]) * (1.0 / cells)
            for k in range(j):
                total = total - lower[i, k] * lower[j, k]
            if i == j:
                diagonal = jnp.sqrt(total)
                inverse_diagonal.append(1.0 / diagonal)
            else:
                lower[i, j] = total * inverse_diagonal[j]
    inverse = {}
    for j in range(count):
        inverse[j, j] = inverse_diagonal[j]
        for i in range(j + 1, count):
            total = lower[i, j] * inverse[j, j]
            for k in range(j + 1, i):
                total = total + lower[i, k] * inverse[k, j]
            inverse[i, j] = -total * inverse_diagonal[i]
    for (i, j), value in inverse.items():
        mixing[at[i], at[j]] = value
    width, _, depth = slots[0].shape
    for r in range(2):
        factors = [mixing[2 * band + r, name] for name in names]

        def body(x, carry, r=r, factors=factors):
            for half in range(depth // LANES):
                lanes = slice(half * LANES, (half + 1) * LANES)
                total = factors[0] * slots[0][x, :, lanes]
                for factor, slot in zip(factors[1:], slots[1:]):
                    total = total + factor * slot[x, :, lanes]
                out[r, x, :, lanes] = total
            return carry

        lax.fori_loop(0, width, body, 0, unroll=4)


def partner(position, phase, count):
    other = position + 1 if position % 2 == phase else position - 1
    return other if 0 <= other < count else None


def meet(value, x_phase=None, y_phase=None):
    nx, ny = lax.axis_size("gx"), lax.axis_size("gy")
    pairs = []
    for x in range(nx):
        for y in range(ny):
            to_x = x if x_phase is None else partner(x, x_phase, nx)
            chip = y // 2 if y_phase is None else partner(y // 2, y_phase, ny // 2)
            if to_x is None or chip is None:
                pairs.append((x * ny + y, x * ny + (y ^ 1)))
            else:
                pairs.append((x * ny + y, to_x * ny + chip * 2 + y % 2))
    return lax.ppermute(value, ("gx", "gy"), pairs)


def swap(value):
    count = lax.axis_size("gy")
    return lax.ppermute(value, "gy", [(y, y ^ 1) for y in range(count)])


def to_band(value, d, crossed=False):
    bands = lax.axis_size("band")
    pairs = []
    for y in range(lax.axis_size("gy")):
        for band in range(bands):
            pairs.append((y * bands + band, (y ^ crossed) * bands + (band + d) % bands))
    return lax.ppermute(value, ("gy", "band"), pairs)


def exchange(payloads):
    count = len(y_phases())
    halos = [meet(payloads[phase], y_phase=phase) for phase in y_phases()]
    halos += [meet(payloads[count + phase], x_phase=phase) for phase in range(2)]
    for y_phase in y_phases():
        for x_phase in range(2):
            halos.append(meet(payloads[count + 2 + 2 * y_phase + x_phase], x_phase, y_phase))
    return halos


def summed(value, axis):
    count = lax.axis_size(axis)
    if count & (count - 1):
        return lax.psum(value, axis)

    def of(step):
        return lax.ppermute(value, axis, [(i, i ^ step) for i in range(count)])

    if count == 4:
        return (value + of(1)) + (of(2) + of(3))
    step = 1
    while step < count:
        value = value + of(step)
        step *= 2
    return value


def per_device(orbitals, potential, order):
    group, width, height, depth = orbitals.shape
    bands = lax.axis_size("band")
    cells = float(width * lax.axis_size("gx") * height * lax.axis_size("gy") * depth)
    count = len(y_phases())
    window = struct(2, width + 2 * HALO, 32 + 2 * PAD, LANES)
    windows = STEPS + 1

    received = swap(orbitals)
    received_potential = swap(potential)
    tile = (width, height, depth)
    orbitals, potential = pl.pallas_call(
        load_kernel,
        out_shape=[struct(*orbitals.shape), struct(*tile)],
        in_specs=[pl.BlockSpec(memory_space=pl.ANY)] * 2,
        out_specs=[VMEM] * 2,
        scratch_shapes=[pltpu.SemaphoreType.DMA((2,))],
        compiler_params=PARAMS,
        name="load",
    )(orbitals, potential)

    def payloads(in_y, in_x, in_corner):
        return (
            [struct(in_y, height, depth)] * count
            + [struct(2, in_x, height, depth)] * 2
            + [struct(in_corner, height, depth)] * (2 * count)
        )

    packed = pl.pallas_call(
        pack_kernel,
        out_shape=payloads(width + width // 2, 2 * HALO - 2, HALO - 1),
        in_specs=[VMEM] * 4,
        out_specs=[VMEM] * (2 + 3 * count),
        compiler_params=PARAMS,
        name="pack",
    )(orbitals, received, potential, received_potential)
    halos = exchange(packed)
    y_halos, x_halos, corners = halos_of(halos)
    *levels, local = pl.pallas_call(
        first_own_kernel,
        out_shape=[window] * (windows + 1),
        in_specs=[VMEM] * 6,
        out_specs=[VMEM] * (windows + 1),
        compiler_params=PARAMS,
        name="first_own",
    )(orbitals, received, potential, received_potential, *x_halos)
    passed = []
    for phase in y_phases():
        half, *_ = lax.optimization_barrier((y_halos[phase][width:], *y_halos, *corners, *levels))
        passed.append(swap(half))
    outs = pl.pallas_call(
        first_rest_kernel,
        out_shape=[window] * (windows + 1) + payloads(width, HALO, HALO // 2),
        in_specs=[VMEM] * (windows + 1 + 4 * count),
        out_specs=[VMEM] * (windows + 3 + 3 * count),
        input_output_aliases={k: k for k in range(windows + 1)},
        compiler_params=PARAMS,
        name="first_rest",
    )(*levels, local, *passed, *y_halos, *corners)
    levels, local, packed = outs[:windows], outs[windows], outs[windows + 1 :]
    y_halos, x_halos, corners = halos_of(exchange(packed))
    levels = pl.pallas_call(
        second_own_kernel,
        out_shape=[window] * windows,
        in_specs=[VMEM] * 4,
        out_specs=[VMEM] * windows,
        compiler_params=PARAMS,
        name="second_own",
    )(levels[STEPS], local, *x_halos)
    half = (width // 2, height, depth)
    outs = pl.pallas_call(
        second_rest_kernel,
        out_shape=[window] * windows + [struct(*tile)] * 2 + [struct(*half)] * (2 * bands - 2),
        in_specs=[VMEM] * (windows + 3 + 3 * count),
        out_specs=[VMEM] * (windows + 2 * bands),
        input_output_aliases={k: k for k in range(windows)},
        compiler_params=PARAMS,
        name="second_rest",
    )(*levels, local, orbitals, received, *y_halos, *corners)
    keep, give, *early = outs[windows:]

    early = [to_band(value, 1 + k // 2, crossed=k % 2 == 1) for k, value in enumerate(early)]
    sibling = swap(give)
    late = pl.pallas_call(
        late_kernel,
        out_shape=[struct(2, *half)] * (bands - 1),
        in_specs=[VMEM] * 2,
        out_specs=[VMEM] * (bands - 1),
        compiler_params=PARAMS,
        name="late",
    )(keep, sibling)
    late = [to_band(value, d) for d, value in enumerate(late, 1)]
    partial_value = pl.pallas_call(
        correlation_kernel,
        out_shape=struct(8, LANES),
        in_specs=[VMEM] * (2 * bands),
        out_specs=VMEM,
        compiler_params=PARAMS,
        name="correlation",
    )(keep, sibling, *early)
    correlation = summed(summed(summed(partial_value, "band"), "gy"), "gx")
    return pl.pallas_call(
        functools.partial(basis_kernel, bands, cells),
        out_shape=struct(*orbitals.shape),
        in_specs=[SMEM, SMEM] + [VMEM] * (3 * bands - 1),
        out_specs=VMEM,
        scratch_shapes=[pltpu.VMEM((2 * bands, 2 * bands, 8, LANES), jnp.float32)]
        + [pltpu.VMEM(tile, jnp.float32)] * (2 * bands - 2),
        compiler_params=PARAMS,
        name="basis",
    )(correlation, order, keep, sibling, *early, *late)


def solution(mesh):
    in_specs = (P("band", "gx", "gy", None), P("gx", "gy", None), P())
    out_specs = P("band", "gx", "gy", None)
    return jax.shard_map(
        per_device, mesh=mesh, in_specs=in_specs, out_specs=out_specs, check_vma=False
    )
```

```python
import functools

import jax
import jax.numpy as jnp
from jax import lax
from jax.experimental import pallas as pl
from jax.experimental.pallas import tpu as pltpu
from jax.sharding import PartitionSpec as P

STEPS = 4
HALO = 2 * STEPS
PAD = 8
LANES = 128
PLANES = 4
OWN_ROWS = slice(PAD + 8, PAD + 24)
HALO_ROWS = (slice(PAD, PAD + 8), slice(PAD + 24, PAD + 32))
TOGETHER = {8: (32, 0, 1), 16: (8, 4, 2), 32: (8, 2, 1)}
NEAR = -(2.0 / 3.0) / 4.25
FAR = (1.0 / 24.0) / 4.25
VMEM = pl.BlockSpec(memory_space=pltpu.VMEM)
SMEM = pl.BlockSpec(memory_space=pltpu.SMEM)
PARAMS = pltpu.CompilerParams(vmem_limit_bytes=16 * 1024 * 1024)


def struct(*shape):
    return jax.ShapeDtypeStruct(shape, jnp.float32)


def place():
    along_y = lax.axis_index("gy")
    return along_y % 2, along_y // 2, lax.axis_index("gx")


def one_sided():
    return lax.axis_size("gy") == 4


def y_phases():
    return range(1 if one_sided() else 2)


def upward(position, phase):
    return (position % 2) == phase


def own_slots(core):
    return 1 + core, 2 - core


def halo_slot(up):
    return jnp.where(up, 3, 0)


def rows_of(slot):
    return pl.ds(pl.multiple_of(PAD + 8 * slot, 8), 8)


def put(window, first_plane, rows, planes, change=lambda a: a):
    count = planes.shape[0]
    for half in range(2):
        lanes = slice(half * LANES, (half + 1) * LANES)
        window[half, pl.ds(first_plane, count), rows, :] = change(planes[:, :, lanes])


def halo_start(right, width, count):
    return jnp.where(right, HALO + width, HALO - count)


def corner_plane(right, width, distance):
    return jnp.where(right, HALO + width + distance - 1, HALO - distance)


def put_corner(window, corner, reach, right, up, rows, width, change=lambda a: a):
    for k in range(1, reach // 2 + 1):
        tile = corner[k - 1]
        put(window, corner_plane(right, width, k), rows, tile[None], change)
        if k != reach - k:
            other = jnp.where(up, pltpu.roll(tile, k, 0), pltpu.roll(tile, 8 - k, 0))
            put(window, corner_plane(right, width, reach - k), rows, other[None], change)


def pack_corner(out, plane, reach, up):
    for k in range(1, reach // 2 + 1):
        tile = plane(k)
        if k != reach - k:
            other = plane(reach - k)
            other = jnp.where(up, pltpu.roll(other, k, 0), pltpu.roll(other, 8 - k, 0))
            row = lax.broadcasted_iota(jnp.int32, tile.shape, 0)
            mine = jnp.where(up, row - k, 7 - k - row) >= 0
            tile = jnp.where(mine, tile, other)
        out[k - 1] = tile


def fill_own(window, tiles, x_halos, change=lambda a: a):
    core, _, along_x = place()
    width = tiles[0].shape[0]
    for index, slot in enumerate(own_slots(core)):
        put(window, HALO, rows_of(slot), tiles[index], change)
    fill_x(window, width, x_halos, change)


def fill_x(window, width, x_halos, change=lambda a: a):
    core, _, along_x = place()
    for index, slot in enumerate(own_slots(core)):
        for phase in range(2):
            halo = x_halos[phase].at[index]
            start = halo_start(upward(along_x, phase), width, halo.shape[0])
            put(window, start, rows_of(slot), halo, change)


def fill_y(window, y_halos, corners, reach, change=lambda a: a):
    _, chip, along_x = place()
    width = window.shape[1] - 2 * HALO
    for phase in y_phases():
        up = upward(chip, phase)
        rows = rows_of(halo_slot(up))
        if y_halos is not None:
            put(window, HALO, rows, y_halos[phase], change)
        for x_phase in range(2):
            corner = corners[2 * phase + x_phase]
            put_corner(window, corner, reach, upward(along_x, x_phase), up, rows, width, change)


def near_planes(right, width, count):
    return pl.ds(jnp.where(right, width - count, 0), count)


def z_matrix(depth):
    gap = jnp.abs(
        lax.broadcasted_iota(jnp.int32, (depth, depth), 0)
        - lax.broadcasted_iota(jnp.int32, (depth, depth), 1)
    )
    return jnp.where(gap == 1, -16.0, jnp.where(gap == 2, 1.0, 0.0)).astype(jnp.bfloat16)


def sides(source, half, x, count, body):
    def at(dx, dy):
        return source[half, pl.ds(x + dx, count), body.start + dy : body.stop + dy, :]

    near = at(-1, 0) + at(1, 0) + at(0, -1) + at(0, 1)
    far = at(-2, 0) + at(2, 0) + at(0, -2) + at(0, 2)
    return near, far


def z_by_product(values, along_z):
    count, height, _ = values[0].shape
    flat = [v.reshape(count * height, LANES) for v in values]
    high = [v.astype(jnp.bfloat16) for v in flat]
    low = [(v - h.astype(jnp.float32)).astype(jnp.bfloat16) for v, h in zip(flat, high)]
    pieces = jnp.concatenate([jnp.concatenate(high, axis=1), jnp.concatenate(low, axis=1)], axis=0)
    both = jnp.dot(pieces, along_z, preferred_element_type=jnp.float32)
    total = both[: count * height] + both[count * height :]
    return [total[:, h * LANES : (h + 1) * LANES].reshape(values[0].shape) for h in range(2)]


def z_by_rolls(values):
    lane = lax.broadcasted_iota(jnp.int32, values[0].shape, 2)
    zero = jnp.zeros_like(values[0])
    found = []
    for distance in (1, 2):
        back = [pltpu.roll(v, distance, 2) for v in values]
        ahead = [pltpu.roll(v, LANES - distance, 2) for v in values]
        first, last = lane < distance, lane >= LANES - distance
        found.append(
            [
                jnp.where(first, zero, back[0]) + jnp.where(last, ahead[1], ahead[0]),
                jnp.where(first, back[0], back[1]) + jnp.where(last, zero, ahead[1]),
            ]
        )
    return found


def stencil(source, previous, target, local, x, by_product, by_rolls, along_z, body):
    scale = 1.0 if previous is None else 2.0
    results = []
    for start, count, product in ((x, by_product, True), (x + by_product, by_rolls, False)):
        if not count:
            continue
        now = pl.ds(start, count)
        values = [source[half, now, body, :] for half in range(2)]
        if product:
            z_far = z_by_product(values, along_z)
        else:
            z_near, z_far = z_by_rolls(values)
        for half in range(2):
            near, far = sides(source, half, start, count, body)
            far = far + z_far[half]
            if not product:
                near = near + z_near[half]
            result = local[half, now, body, :] * values[half] * scale
            result = result + near * (NEAR * scale) + far * (FAR * scale)
            if previous is not None:
                result = result - previous[half, now, body, :]
            results.append((half, now, result))
    for half, now, result in results:
        target[half, now, body, :] = result


def four_steps(levels, local, depth, body, last):
    along_z = z_matrix(depth)
    extent = local.shape[1]
    outside_is_zero(levels[0], body)
    for step in range(STEPS):
        rows = last if step == STEPS - 1 else body
        low = 2 * (step + 1)
        by_product, by_rolls, unroll = TOGETHER[rows.stop - rows.start]
        together = by_product + by_rolls
        blocks, rest = divmod(extent - 2 * low, together)
        previous = levels[step - 1] if step else None

        def do(x, by_product, by_rolls, rows=rows, step=step, previous=previous):
            source, target = levels[step], levels[step + 1]
            stencil(source, previous, target, local, x, by_product, by_rolls, along_z, rows)

        def block(index, carry, do=do, low=low, by_product=by_product, by_rolls=by_rolls):
            do(low + index * (by_product + by_rolls), by_product, by_rolls)
            return carry

        lax.fori_loop(0, blocks, block, 0, unroll=min(unroll, blocks))
        if rest:
            rolled = min(by_rolls, rest // 3)
            do(low + blocks * together, rest - rolled, rolled)
        if step < STEPS - 1:
            outside_is_zero(levels[step + 1], body)


def outside_is_zero(window, body):
    _, chip, along_x = place()
    extent = window.shape[1]

    def clear(where, planes, rows):
        @pl.when(where)
        def _():
            region = window[:, planes, rows, :]
            window[:, planes, rows, :] = jnp.zeros_like(region)

    clear(along_x == 0, slice(0, HALO), body)
    clear(along_x == lax.axis_size("gx") - 1, slice(extent - HALO, extent), body)
    if not one_sided():
        clear(chip == 0, slice(None), HALO_ROWS[0])
        clear(chip == lax.axis_size("gy") // 2 - 1, slice(None), HALO_ROWS[1])


def first_part(levels, local, depth):
    if not one_sided():
        return
    _, chip, _ = place()
    for position in range(2):

        @pl.when(chip == position)
        def _(position=position):
            for window in levels[:STEPS]:
                region = window[:, :, HALO_ROWS[position], :]
                window[:, :, HALO_ROWS[position], :] = jnp.zeros_like(region)

    four_steps(levels, local, depth, OWN_ROWS, OWN_ROWS)


def second_part(levels, local, depth):
    if not one_sided():
        four_steps(levels, local, depth, slice(PAD, PAD + 32), OWN_ROWS)
        return
    _, chip, _ = place()
    for position in range(2):
        inner = slice(PAD + 16, PAD + 24) if position == 0 else slice(PAD + 8, PAD + 16)
        body = slice(PAD + 16, PAD + 32) if position == 0 else slice(PAD, PAD + 16)

        @pl.when(chip == position)
        def _(inner=inner, body=body):
            four_steps(levels, local, depth, body, inner)


def edge_is_own(core, chip, phase):
    return core == jnp.where(upward(chip, phase), 1, 0)


def load_kernel(orbitals, potential, orbitals_out, potential_out, arrived):
    copies = [
        pltpu.make_async_copy(orbitals, orbitals_out, arrived.at[0]),
        pltpu.make_async_copy(potential, potential_out, arrived.at[1]),
    ]
    for copy in copies:
        copy.start()
    for copy in copies:
        copy.wait()


def pack_kernel(orbitals, received, potential, received_potential, *outs):
    core, chip, along_x = place()
    width = potential.shape[0]
    p_out, outs = outs[: len(y_phases())], outs[len(y_phases()) :]
    y_out, x_out, d_out = halos_of(outs)
    tiles = (orbitals.at[core], received.at[core])
    local = (potential, received_potential)
    for x_phase in range(2):
        right = upward(along_x, x_phase)
        for t in range(2):
            x_out[x_phase][t, :HALO] = tiles[t][near_planes(right, width, HALO)]
            x_out[x_phase][t, HALO:] = local[t][near_planes(right, width, HALO - 2)]
    for phase in y_phases():
        own = edge_is_own(core, chip, phase)
        for t, chosen in enumerate((own, jnp.logical_not(own))):

            @pl.when(chosen)
            def _(t=t, phase=phase):
                y_out[phase][...] = tiles[t][...]
                half = width // 2
                p_out[phase][...] = local[t][pl.ds(core * half, half)]
                up = upward(chip, phase)
                for x_phase in range(2):
                    right = upward(along_x, x_phase)
                    out = d_out[2 * phase + x_phase]

                    def plane(k, field, right=right):
                        return field[jnp.where(right, width - k, k - 1)]

                    pack_corner(out, functools.partial(plane, field=tiles[t]), HALO, up)
                    rest = out.at[HALO // 2 :]
                    pack_corner(rest, functools.partial(plane, field=local[t]), HALO - 2, up)


def halos_of(refs):
    count = len(y_phases())
    return refs[:count], refs[count : count + 2], refs[count + 2 :]


def diagonal(potential):
    return (potential - 0.5) / 4.25


def first_own_kernel(orbitals, received, potential, received_potential, x_a, x_b, *outs):
    levels, local = outs[:-1], outs[-1]
    core, _, _ = place()
    x_halos = (x_a, x_b)
    tiles = (orbitals.at[core], received.at[core])
    fill_own(levels[0], tiles, [x.at[:, :HALO] for x in x_halos])
    tiles = (potential, received_potential)
    fill_own(local, tiles, [x.at[:, HALO:] for x in x_halos], diagonal)
    first_part(levels, local, potential.shape[2])


def first_rest_kernel(*refs):
    count = len(y_phases())
    came, passed = refs[6 : 6 + count], refs[6 + count : 6 + 2 * count]
    y_halos, corners = refs[6 + 2 * count : 6 + 3 * count], refs[6 + 3 * count : 6 + 5 * count]
    outs = refs[6 + 5 * count :]
    levels, local = outs[: STEPS + 1], outs[STEPS + 1]
    payloads = outs[STEPS + 2 :]
    core, chip, along_x = place()
    width, depth = local.shape[1] - 2 * HALO, 2 * LANES
    fill_y(levels[0], y_halos, [c.at[: HALO // 2] for c in corners], HALO)
    fill_y(local, None, [c.at[HALO // 2 :] for c in corners], HALO - 2, diagonal)
    half = width // 2
    for phase in y_phases():
        rows = rows_of(halo_slot(upward(chip, phase)))
        put(local, HALO + core * half, rows, came[phase], diagonal)
        put(local, HALO + (1 - core) * half, rows, passed[phase], diagonal)

    second_part(levels, local, depth)
    y_out, x_out, d_out = halos_of(payloads)
    slots = own_slots(core)
    result = levels[STEPS]
    for half in range(2):
        lanes = slice(half * LANES, (half + 1) * LANES)

        def planes(slot, start, size, half=half):
            return result[half, pl.ds(HALO + start, size), rows_of(slot), :]

        for t in range(2):
            for x_phase in range(2):
                start = jnp.where(upward(along_x, x_phase), width - HALO, 0)
                x_out[x_phase][t, :, :, lanes] = planes(slots[t], start, HALO)
        for phase in y_phases():
            slot = jnp.where(edge_is_own(core, chip, phase), *slots)
            y_out[phase][:, :, lanes] = planes(slot, 0, width)
            for x_phase in range(2):
                right = upward(along_x, x_phase)

                def plane(k, right=right, slot=slot, planes=planes):
                    return planes(slot, jnp.where(right, width - k, k - 1), 1)[0]

                out = d_out[2 * phase + x_phase].at[:, :, lanes]
                pack_corner(out, plane, HALO, upward(chip, phase))


def second_own_kernel(before, local, x_a, x_b, *levels):
    width = before.shape[1] - 2 * HALO
    for half in range(2):
        inside = (half, slice(HALO, HALO + width), OWN_ROWS)
        levels[0][inside] = before[inside]
    fill_x(levels[0], width, (x_a, x_b))
    first_part(levels, local, LANES * 2)


def second_rest_kernel(*refs):
    count = len(y_phases())
    local, orbitals, received = refs[STEPS + 1 : STEPS + 4]
    refs = refs[STEPS + 4 :]
    y_halos, corners = refs[:count], refs[count : 3 * count]
    levels, outs = refs[3 * count : 3 * count + STEPS + 1], refs[3 * count + STEPS + 1 :]
    outs, early = outs[:2], outs[2:]
    core, _, _ = place()
    width, depth = orbitals.shape[1], orbitals.shape[3]
    fill_y(levels[0], y_halos, corners, HALO)
    second_part(levels, local, depth)
    start = (orbitals.at[core], received.at[core])
    for t, slot in enumerate(own_slots(core)):
        for half in range(2):
            lanes = slice(half * LANES, (half + 1) * LANES)
            tile = levels[STEPS][half, HALO : HALO + width, rows_of(slot), :]
            outs[t][:, :, lanes] = 2.0 * tile - start[t][:, :, lanes]
    half = width // 2
    for d in range(1, lax.axis_size("band")):
        upper, _ = halves_met(d)
        for out, whole in zip(early[2 * d - 2 : 2 * d], outs):
            out[...] = whole[pl.ds(upper * half, half)]


def halves_met(d):
    bands, band = lax.axis_size("band"), lax.axis_index("band")
    to, source = lax.rem(band + d, bands), lax.rem(band + bands - d, bands)
    return jnp.where(band < to, 1, 0), jnp.where(source < band, 1, 0)


def late_kernel(keep, sibling, *outs):
    half = keep.shape[0] // 2
    for d, out in enumerate(outs, 1):
        upper, _ = halves_met(d)
        for t, whole in enumerate((keep, sibling)):
            out[t] = whole[pl.ds((1 - upper) * half, half)]


def slot_orbitals(bands):
    core, _, _ = place()
    band = lax.axis_index("band")
    names = []
    for d in range(bands):
        group = lax.rem(band + bands - d, bands)
        names += [2 * group + core, 2 * group + 1 - core]
    return names


def correlation_kernel(*refs):
    bands = lax.axis_size("band")
    own, early, out = refs[:2], refs[2:-1], refs[-1]
    names = slot_orbitals(bands)
    row = lax.broadcasted_iota(jnp.int32, (8, LANES), 0)
    column = lax.broadcasted_iota(jnp.int32, (8, LANES), 1)
    pairs = [(0, 0), (0, 1), (1, 1)] + [(i, 2 * d + j) for d in range(1, bands) for i in range(2) for j in range(2)]
    width, height, depth = own[0].shape
    half = width // 2

    def summed_up(value):
        total = jnp.sum(value, axis=0)
        return sum(total[:, k * LANES : (k + 1) * LANES] for k in range(depth // LANES))

    def body(index, totals):
        def planes(ref, upper):
            return ref[pl.ds(upper * half + index * PLANES, PLANES)]

        halves = [[planes(ref, upper) for ref in own] for upper in range(2)]
        found = []
        for (i, j), total in zip(pairs, totals):
            if j < 2:
                total = total + summed_up(halves[0][i] * halves[0][j] + halves[1][i] * halves[1][j])
            else:
                _, upper = halves_met(j // 2)
                total = total + summed_up(planes(own[i], upper) * planes(early[j - 2], 0))
            found.append(total)
        return tuple(found)

    zero = jnp.zeros((height, LANES), jnp.float32)
    totals = lax.fori_loop(0, half // PLANES, body, (zero,) * len(pairs))
    result = jnp.zeros((8, LANES), jnp.float32)
    for (i, j), total in zip(pairs, totals):
        here = ((row == names[i]) & (column == names[j])) | ((row == names[j]) & (column == names[i]))
        result = jnp.where(here, jnp.sum(total), result)
    out[...] = result


def basis_kernel(bands, cells, *refs):
    correlation, order = refs[:2]
    early, late = refs[4 : 2 + 2 * bands], refs[2 + 2 * bands : 1 + 3 * bands]
    out, mixing = refs[1 + 3 * bands : 3 + 3 * bands]
    joined = refs[3 + 3 * bands :]
    slots = list(refs[2:4]) + list(joined)
    for d in range(1, bands):
        _, upper = halves_met(d)
        for t in range(2):
            whole = joined[2 * d - 2 + t]
            half = whole.shape[0] // 2
            whole[pl.ds(upper * half, half)] = early[2 * d - 2 + t][...]
            whole[pl.ds((1 - upper) * half, half)] = late[d - 1][t]
    names = slot_orbitals(bands)
    count = 2 * bands
    band = lax.axis_index("band")

    def splat(value):
        return jnp.full((8, LANES), value, jnp.float32)

    at = [order[p] for p in range(count)]
    mixing[...] = jnp.zeros_like(mixing)
    lower = {}
    inverse_diagonal = []
    for j in range(count):
        for i in range(j, count):
            total = splat(correlation[at[i], at[j]]) * (1.0 / cells)
            for k in range(j):
                total = total - lower[i, k] * lower[j, k]
            if i == j:
                diagonal = jnp.sqrt(total)
                inverse_diagonal.append(1.0 / diagonal)
            else:
                lower[i, j] = total * inverse_diagonal[j]
    inverse = {}
    for j in range(count):
        inverse[j, j] = inverse_diagonal[j]
        for i in range(j + 1, count):
            total = lower[i, j] * inverse[j, j]
            for k in range(j + 1, i):
                total = total + lower[i, k] * inverse[k, j]
            inverse[i, j] = -total * inverse_diagonal[i]
    for (i, j), value in inverse.items():
        mixing[at[i], at[j]] = value
    width, _, depth = slots[0].shape
    for r in range(2):
        factors = [mixing[2 * band + r, name] for name in names]

        def body(x, carry, r=r, factors=factors):
            for half in range(depth // LANES):
                lanes = slice(half * LANES, (half + 1) * LANES)
                total = factors[0] * slots[0][x, :, lanes]
                for factor, slot in zip(factors[1:], slots[1:]):
                    total = total + factor * slot[x, :, lanes]
                out[r, x, :, lanes] = total
            return carry

        lax.fori_loop(0, width, body, 0, unroll=4)


def partner(position, phase, count):
    other = position + 1 if position % 2 == phase else position - 1
    return other if 0 <= other < count else None


def meet(value, x_phase=None, y_phase=None):
    nx, ny = lax.axis_size("gx"), lax.axis_size("gy")
    pairs = []
    for x in range(nx):
        for y in range(ny):
            to_x = x if x_phase is None else partner(x, x_phase, nx)
            chip = y // 2 if y_phase is None else partner(y // 2, y_phase, ny // 2)
            if to_x is None or chip is None:
                pairs.append((x * ny + y, x * ny + (y ^ 1)))
            else:
                pairs.append((x * ny + y, to_x * ny + chip * 2 + y % 2))
    return lax.ppermute(value, ("gx", "gy"), pairs)


def swap(value):
    count = lax.axis_size("gy")
    return lax.ppermute(value, "gy", [(y, y ^ 1) for y in range(count)])


def to_band(value, d, crossed=False):
    bands = lax.axis_size("band")
    pairs = []
    for y in range(lax.axis_size("gy")):
        for band in range(bands):
            pairs.append((y * bands + band, (y ^ crossed) * bands + (band + d) % bands))
    return lax.ppermute(value, ("gy", "band"), pairs)


def exchange(payloads):
    count = len(y_phases())
    halos = [meet(payloads[phase], y_phase=phase) for phase in y_phases()]
    halos += [meet(payloads[count + phase], x_phase=phase) for phase in range(2)]
    for y_phase in y_phases():
        for x_phase in range(2):
            halos.append(meet(payloads[count + 2 + 2 * y_phase + x_phase], x_phase, y_phase))
    return halos


def summed(value, axis):
    count = lax.axis_size(axis)
    if count & (count - 1):
        return lax.psum(value, axis)

    def of(step):
        return lax.ppermute(value, axis, [(i, i ^ step) for i in range(count)])

    if count == 4:
        return (value + of(1)) + (of(2) + of(3))
    step = 1
    while step < count:
        value = value + of(step)
        step *= 2
    return value


def per_device(orbitals, potential, order):
    group, width, height, depth = orbitals.shape
    bands = lax.axis_size("band")
    cells = float(width * lax.axis_size("gx") * height * lax.axis_size("gy") * depth)
    count = len(y_phases())
    window = struct(2, width + 2 * HALO, 32 + 2 * PAD, LANES)
    windows = STEPS + 1

    received = swap(orbitals)
    received_potential = swap(potential)
    tile = (width, height, depth)
    orbitals, potential = pl.pallas_call(
        load_kernel,
        out_shape=[struct(*orbitals.shape), struct(*tile)],
        in_specs=[pl.BlockSpec(memory_space=pl.ANY)] * 2,
        out_specs=[VMEM] * 2,
        scratch_shapes=[pltpu.SemaphoreType.DMA((2,))],
        compiler_params=PARAMS,
        name="load",
    )(orbitals, potential)

    def payloads(in_x, in_corner):
        return (
            [struct(*tile)] * count
            + [struct(2, in_x, height, depth)] * 2
            + [struct(in_corner, height, depth)] * (2 * count)
        )

    *packed, = pl.pallas_call(
        pack_kernel,
        out_shape=[struct(width // 2, height, depth)] * count + payloads(2 * HALO - 2, HALO - 1),
        in_specs=[VMEM] * 4,
        out_specs=[VMEM] * (2 + 4 * count),
        compiler_params=PARAMS,
        name="pack",
    )(orbitals, received, potential, received_potential)
    came = [meet(packed[phase], y_phase=phase) for phase in y_phases()]
    packed[-1], came = lax.optimization_barrier((packed[-1], came))
    y_halos, x_halos, corners = halos_of(exchange(packed[count:]))
    passed = [swap(value) for value in came]
    *levels, local = pl.pallas_call(
        first_own_kernel,
        out_shape=[window] * (windows + 1),
        in_specs=[VMEM] * 6,
        out_specs=[VMEM] * (windows + 1),
        compiler_params=PARAMS,
        name="first_own",
    )(orbitals, received, potential, received_potential, *x_halos)
    outs = pl.pallas_call(
        first_rest_kernel,
        out_shape=[window] * (windows + 1) + payloads(HALO, HALO // 2),
        in_specs=[VMEM] * (windows + 1 + 5 * count),
        out_specs=[VMEM] * (windows + 3 + 3 * count),
        input_output_aliases={k: k for k in range(windows + 1)},
        compiler_params=PARAMS,
        name="first_rest",
    )(*levels, local, *came, *passed, *y_halos, *corners)
    levels, local, packed = outs[:windows], outs[windows], outs[windows + 1 :]
    y_halos, x_halos, corners = halos_of(exchange(packed))
    levels = pl.pallas_call(
        second_own_kernel,
        out_shape=[window] * windows,
        in_specs=[VMEM] * 4,
        out_specs=[VMEM] * windows,
        compiler_params=PARAMS,
        name="second_own",
    )(levels[STEPS], local, *x_halos)
    half = (width // 2, height, depth)
    outs = pl.pallas_call(
        second_rest_kernel,
        out_shape=[window] * windows + [struct(*tile)] * 2 + [struct(*half)] * (2 * bands - 2),
        in_specs=[VMEM] * (windows + 3 + 3 * count),
        out_specs=[VMEM] * (windows + 2 * bands),
        input_output_aliases={k: k for k in range(windows)},
        compiler_params=PARAMS,
        name="second_rest",
    )(*levels, local, orbitals, received, *y_halos, *corners)
    keep, give, *early = outs[windows:]

    early = [to_band(value, 1 + k // 2, crossed=k % 2 == 1) for k, value in enumerate(early)]
    sibling = swap(give)
    late = pl.pallas_call(
        late_kernel,
        out_shape=[struct(2, *half)] * (bands - 1),
        in_specs=[VMEM] * 2,
        out_specs=[VMEM] * (bands - 1),
        compiler_params=PARAMS,
        name="late",
    )(keep, sibling)
    late = [to_band(value, d) for d, value in enumerate(late, 1)]
    partial_value = pl.pallas_call(
        correlation_kernel,
        out_shape=struct(8, LANES),
        in_specs=[VMEM] * (2 * bands),
        out_specs=VMEM,
        compiler_params=PARAMS,
        name="correlation",
    )(keep, sibling, *early)
    correlation = summed(summed(summed(partial_value, "band"), "gy"), "gx")
    return pl.pallas_call(
        functools.partial(basis_kernel, bands, cells),
        out_shape=struct(*orbitals.shape),
        in_specs=[SMEM, SMEM] + [VMEM] * (3 * bands - 1),
        out_specs=VMEM,
        scratch_shapes=[pltpu.VMEM((2 * bands, 2 * bands, 8, LANES), jnp.float32)]
        + [pltpu.VMEM(tile, jnp.float32)] * (2 * bands - 2),
        compiler_params=PARAMS,
        name="basis",
    )(correlation, order, keep, sibling, *early, *late)


def solution(mesh):
    in_specs = (P("band", "gx", "gy", None), P("gx", "gy", None), P())
    out_specs = P("band", "gx", "gy", None)
    return jax.shard_map(
        per_device, mesh=mesh, in_specs=in_specs, out_specs=out_specs, check_vma=False
    )
```

```python
import functools

import jax
import jax.numpy as jnp
from jax import lax
from jax.experimental import pallas as pl
from jax.experimental.pallas import tpu as pltpu
from jax.sharding import PartitionSpec as P

STEPS = 4
SPLIT = 8
HALO = 2 * STEPS
PAD = 8
LANES = 128
PLANES = 4
OWN_ROWS = slice(PAD + 8, PAD + 24)
HALO_ROWS = (slice(PAD, PAD + 8), slice(PAD + 24, PAD + 32))
TOGETHER = {8: (32, 0, 1), 16: (8, 4, 2), 32: (8, 2, 1)}
NEAR = -(2.0 / 3.0) / 4.25
FAR = (1.0 / 24.0) / 4.25
VMEM = pl.BlockSpec(memory_space=pltpu.VMEM)
SMEM = pl.BlockSpec(memory_space=pltpu.SMEM)
PARAMS = pltpu.CompilerParams(vmem_limit_bytes=16 * 1024 * 1024)


def struct(*shape):
    return jax.ShapeDtypeStruct(shape, jnp.float32)


def place():
    along_y = lax.axis_index("gy")
    return along_y % 2, along_y // 2, lax.axis_index("gx")


def one_sided():
    return lax.axis_size("gy") == 4


def y_phases():
    return range(1 if one_sided() else 2)


def upward(position, phase):
    return (position % 2) == phase


def own_slots(core):
    return 1 + core, 2 - core


def halo_slot(up):
    return jnp.where(up, 3, 0)


def rows_of(slot):
    return pl.ds(pl.multiple_of(PAD + 8 * slot, 8), 8)


def put(window, first_plane, rows, planes, change=lambda a: a):
    count = planes.shape[0]
    for half in range(2):
        lanes = slice(half * LANES, (half + 1) * LANES)
        window[half, pl.ds(first_plane, count), rows, :] = change(planes[:, :, lanes])


def halo_start(right, width, count):
    return jnp.where(right, HALO + width, HALO - count)


def corner_plane(right, width, distance):
    return jnp.where(right, HALO + width + distance - 1, HALO - distance)


def put_corner(window, corner, reach, right, up, rows, width, change=lambda a: a):
    for k in range(1, reach // 2 + 1):
        tile = corner[k - 1]
        put(window, corner_plane(right, width, k), rows, tile[None], change)
        if k != reach - k:
            other = jnp.where(up, pltpu.roll(tile, k, 0), pltpu.roll(tile, 8 - k, 0))
            put(window, corner_plane(right, width, reach - k), rows, other[None], change)


def pack_corner(out, plane, reach, up):
    for k in range(1, reach // 2 + 1):
        tile = plane(k)
        if k != reach - k:
            other = plane(reach - k)
            other = jnp.where(up, pltpu.roll(other, k, 0), pltpu.roll(other, 8 - k, 0))
            row = lax.broadcasted_iota(jnp.int32, tile.shape, 0)
            mine = jnp.where(up, row - k, 7 - k - row) >= 0
            tile = jnp.where(mine, tile, other)
        out[k - 1] = tile


def fill_own(window, tiles, x_halos, change=lambda a: a):
    core, _, along_x = place()
    width = tiles[0].shape[0]
    for index, slot in enumerate(own_slots(core)):
        put(window, HALO, rows_of(slot), tiles[index], change)
    fill_x(window, width, x_halos, change)


def fill_x(window, width, x_halos, change=lambda a: a):
    core, _, along_x = place()
    for index, slot in enumerate(own_slots(core)):
        for phase in range(2):
            halo = x_halos[phase].at[index]
            start = halo_start(upward(along_x, phase), width, halo.shape[0])
            put(window, start, rows_of(slot), halo, change)


def fill_y(window, y_halos, corners, reach, change=lambda a: a):
    _, chip, along_x = place()
    width = window.shape[1] - 2 * HALO
    for phase in y_phases():
        up = upward(chip, phase)
        rows = rows_of(halo_slot(up))
        if y_halos is not None:
            put(window, HALO, rows, y_halos[phase], change)
        for x_phase in range(2):
            corner = corners[2 * phase + x_phase]
            put_corner(window, corner, reach, upward(along_x, x_phase), up, rows, width, change)


def near_planes(right, width, count):
    return pl.ds(jnp.where(right, width - count, 0), count)


def z_matrix(depth):
    gap = jnp.abs(
        lax.broadcasted_iota(jnp.int32, (depth, depth), 0)
        - lax.broadcasted_iota(jnp.int32, (depth, depth), 1)
    )
    return jnp.where(gap == 1, -16.0, jnp.where(gap == 2, 1.0, 0.0)).astype(jnp.bfloat16)


def sides(source, half, x, count, body):
    def at(dx, dy):
        return source[half, pl.ds(x + dx, count), body.start + dy : body.stop + dy, :]

    near = at(-1, 0) + at(1, 0) + at(0, -1) + at(0, 1)
    far = at(-2, 0) + at(2, 0) + at(0, -2) + at(0, 2)
    return near, far


def z_by_product(values, along_z):
    count, height, _ = values[0].shape
    flat = [v.reshape(count * height, LANES) for v in values]
    high = [v.astype(jnp.bfloat16) for v in flat]
    low = [(v - h.astype(jnp.float32)).astype(jnp.bfloat16) for v, h in zip(flat, high)]
    pieces = jnp.concatenate([jnp.concatenate(high, axis=1), jnp.concatenate(low, axis=1)], axis=0)
    both = jnp.dot(pieces, along_z, preferred_element_type=jnp.float32)
    total = both[: count * height] + both[count * height :]
    return [total[:, h * LANES : (h + 1) * LANES].reshape(values[0].shape) for h in range(2)]


def z_by_rolls(values):
    lane = lax.broadcasted_iota(jnp.int32, values[0].shape, 2)
    zero = jnp.zeros_like(values[0])
    found = []
    for distance in (1, 2):
        back = [pltpu.roll(v, distance, 2) for v in values]
        ahead = [pltpu.roll(v, LANES - distance, 2) for v in values]
        first, last = lane < distance, lane >= LANES - distance
        found.append(
            [
                jnp.where(first, zero, back[0]) + jnp.where(last, ahead[1], ahead[0]),
                jnp.where(first, back[0], back[1]) + jnp.where(last, zero, ahead[1]),
            ]
        )
    return found


def stencil(source, previous, target, local, x, by_product, by_rolls, along_z, body):
    scale = 1.0 if previous is None else 2.0
    results = []
    for start, count, product in ((x, by_product, True), (x + by_product, by_rolls, False)):
        if not count:
            continue
        now = pl.ds(start, count)
        values = [source[half, now, body, :] for half in range(2)]
        if product:
            z_far = z_by_product(values, along_z)
        else:
            z_near, z_far = z_by_rolls(values)
        for half in range(2):
            near, far = sides(source, half, start, count, body)
            far = far + z_far[half]
            if not product:
                near = near + z_near[half]
            result = local[half, now, body, :] * values[half] * scale
            result = result + near * (NEAR * scale) + far * (FAR * scale)
            if previous is not None:
                result = result - previous[half, now, body, :]
            results.append((half, now, result))
    for half, now, result in results:
        target[half, now, body, :] = result


def four_steps(levels, local, depth, body, last):
    along_z = z_matrix(depth)
    extent = local.shape[1]
    outside_is_zero(levels[0], body)
    for step in range(STEPS):
        rows = last if step == STEPS - 1 else body
        low = 2 * (step + 1)
        by_product, by_rolls, unroll = TOGETHER[rows.stop - rows.start]
        together = by_product + by_rolls
        blocks, rest = divmod(extent - 2 * low, together)
        previous = levels[step - 1] if step else None

        def do(x, by_product, by_rolls, rows=rows, step=step, previous=previous):
            source, target = levels[step], levels[step + 1]
            stencil(source, previous, target, local, x, by_product, by_rolls, along_z, rows)

        def block(index, carry, do=do, low=low, by_product=by_product, by_rolls=by_rolls):
            do(low + index * (by_product + by_rolls), by_product, by_rolls)
            return carry

        lax.fori_loop(0, blocks, block, 0, unroll=min(unroll, blocks))
        if rest:
            rolled = min(by_rolls, rest // 3)
            do(low + blocks * together, rest - rolled, rolled)
        if step < STEPS - 1:
            outside_is_zero(levels[step + 1], body)


def outside_is_zero(window, body):
    _, chip, along_x = place()
    extent = window.shape[1]

    def clear(where, planes, rows):
        @pl.when(where)
        def _():
            region = window[:, planes, rows, :]
            window[:, planes, rows, :] = jnp.zeros_like(region)

    clear(along_x == 0, slice(0, HALO), body)
    clear(along_x == lax.axis_size("gx") - 1, slice(extent - HALO, extent), body)
    if not one_sided():
        clear(chip == 0, slice(None), HALO_ROWS[0])
        clear(chip == lax.axis_size("gy") // 2 - 1, slice(None), HALO_ROWS[1])


def first_part(levels, local, depth):
    if not one_sided():
        return
    _, chip, _ = place()
    for position in range(2):

        @pl.when(chip == position)
        def _(position=position):
            for window in levels[:STEPS]:
                region = window[:, :, HALO_ROWS[position], :]
                window[:, :, HALO_ROWS[position], :] = jnp.zeros_like(region)

    four_steps(levels, local, depth, OWN_ROWS, OWN_ROWS)


def second_part(levels, local, depth):
    if not one_sided():
        four_steps(levels, local, depth, slice(PAD, PAD + 32), OWN_ROWS)
        return
    _, chip, _ = place()
    for position in range(2):
        inner = slice(PAD + 16, PAD + 24) if position == 0 else slice(PAD + 8, PAD + 16)
        body = slice(PAD + 16, PAD + 32) if position == 0 else slice(PAD, PAD + 16)

        @pl.when(chip == position)
        def _(inner=inner, body=body):
            four_steps(levels, local, depth, body, inner)


def edge_is_own(core, chip, phase):
    return core == jnp.where(upward(chip, phase), 1, 0)


def pack_kernel(fields, received, received_potential, *outs):
    potential = fields.at[fields.shape[0] - 1]
    core, chip, along_x = place()
    width = potential.shape[0]
    p_out, outs = outs[: len(y_phases())], outs[len(y_phases()) :]
    y_out, x_out, d_out = halos_of(outs)
    tiles = (fields.at[core], received.at[core])
    local = (potential, received_potential)
    for x_phase in range(2):
        right = upward(along_x, x_phase)
        for t in range(2):
            x_out[x_phase][t, :HALO] = tiles[t][near_planes(right, width, HALO)]
            x_out[x_phase][t, HALO:] = local[t][near_planes(right, width, HALO - 2)]
    for phase in y_phases():
        own = edge_is_own(core, chip, phase)
        for t, chosen in enumerate((own, jnp.logical_not(own))):

            @pl.when(chosen)
            def _(t=t, phase=phase):
                half, split = width // 2, width // SPLIT
                p_out[phase][:half] = local[t][pl.ds(core * half, half)]
                p_out[phase][half:] = tiles[t][:split]
                y_out[phase][...] = tiles[t][split:]
                up = upward(chip, phase)
                for x_phase in range(2):
                    right = upward(along_x, x_phase)
                    out = d_out[2 * phase + x_phase]

                    def plane(k, field, right=right):
                        return field[jnp.where(right, width - k, k - 1)]

                    pack_corner(out, functools.partial(plane, field=tiles[t]), HALO, up)
                    rest = out.at[HALO // 2 :]
                    pack_corner(rest, functools.partial(plane, field=local[t]), HALO - 2, up)


def halos_of(refs):
    count = len(y_phases())
    return refs[:count], refs[count : count + 2], refs[count + 2 :]


def diagonal(potential):
    return (potential - 0.5) / 4.25


def first_own_kernel(fields, received, received_potential, x_a, x_b, *outs):
    potential = fields.at[fields.shape[0] - 1]
    levels, local = outs[:-1], outs[-1]
    core, _, _ = place()
    x_halos = (x_a, x_b)
    tiles = (fields.at[core], received.at[core])
    fill_own(levels[0], tiles, [x.at[:, :HALO] for x in x_halos])
    tiles = (potential, received_potential)
    fill_own(local, tiles, [x.at[:, HALO:] for x in x_halos], diagonal)
    first_part(levels, local, potential.shape[2])


def first_rest_kernel(*refs):
    count = len(y_phases())
    came, passed = refs[6 : 6 + count], refs[6 + count : 6 + 2 * count]
    y_halos, corners = refs[6 + 2 * count : 6 + 3 * count], refs[6 + 3 * count : 6 + 5 * count]
    outs = refs[6 + 5 * count :]
    levels, local = outs[: STEPS + 1], outs[STEPS + 1]
    payloads = outs[STEPS + 2 :]
    core, chip, along_x = place()
    width, depth = local.shape[1] - 2 * HALO, 2 * LANES
    half, split = width // 2, width // SPLIT
    fill_y(levels[0], None, [c.at[: HALO // 2] for c in corners], HALO)
    for phase in y_phases():
        rows = rows_of(halo_slot(upward(chip, phase)))
        put(levels[0], HALO, rows, came[phase].at[half:])
        put(levels[0], HALO + split, rows, y_halos[phase])
    fill_y(local, None, [c.at[HALO // 2 :] for c in corners], HALO - 2, diagonal)
    for phase in y_phases():
        rows = rows_of(halo_slot(upward(chip, phase)))
        put(local, HALO + core * half, rows, came[phase].at[:half], diagonal)
        put(local, HALO + (1 - core) * half, rows, passed[phase], diagonal)

    second_part(levels, local, depth)
    y_out, x_out, d_out = halos_of(payloads)
    slots = own_slots(core)
    result = levels[STEPS]
    for half in range(2):
        lanes = slice(half * LANES, (half + 1) * LANES)

        def planes(slot, start, size, half=half):
            return result[half, pl.ds(HALO + start, size), rows_of(slot), :]

        for t in range(2):
            for x_phase in range(2):
                start = jnp.where(upward(along_x, x_phase), width - HALO, 0)
                x_out[x_phase][t, :, :, lanes] = planes(slots[t], start, HALO)
        for phase in y_phases():
            slot = jnp.where(edge_is_own(core, chip, phase), *slots)
            y_out[phase][:, :, lanes] = planes(slot, 0, width)
            for x_phase in range(2):
                right = upward(along_x, x_phase)

                def plane(k, right=right, slot=slot, planes=planes):
                    return planes(slot, jnp.where(right, width - k, k - 1), 1)[0]

                out = d_out[2 * phase + x_phase].at[:, :, lanes]
                pack_corner(out, plane, HALO, upward(chip, phase))


def second_own_kernel(before, local, x_a, x_b, *levels):
    width = before.shape[1] - 2 * HALO
    for half in range(2):
        inside = (half, slice(HALO, HALO + width), OWN_ROWS)
        levels[0][inside] = before[inside]
    fill_x(levels[0], width, (x_a, x_b))
    first_part(levels, local, LANES * 2)


def second_rest_kernel(*refs):
    count = len(y_phases())
    local, fields, received = refs[STEPS + 1 : STEPS + 4]
    refs = refs[STEPS + 4 :]
    y_halos, corners = refs[:count], refs[count : 3 * count]
    levels, outs = refs[3 * count : 3 * count + STEPS + 1], refs[3 * count + STEPS + 1 :]
    outs, early = outs[:2], outs[2:]
    core, _, _ = place()
    width, depth = fields.shape[1], fields.shape[3]
    fill_y(levels[0], y_halos, corners, HALO)
    second_part(levels, local, depth)
    start = (fields.at[core], received.at[core])
    for t, slot in enumerate(own_slots(core)):
        for half in range(2):
            lanes = slice(half * LANES, (half + 1) * LANES)
            tile = levels[STEPS][half, HALO : HALO + width, rows_of(slot), :]
            outs[t][:, :, lanes] = 2.0 * tile - start[t][:, :, lanes]
    half = width // 2
    for d in range(1, lax.axis_size("band")):
        upper, _ = halves_met(d)
        for out, whole in zip(early[2 * d - 2 : 2 * d], outs):
            out[...] = whole[pl.ds(upper * half, half)]


def halves_met(d):
    bands, band = lax.axis_size("band"), lax.axis_index("band")
    to, source = lax.rem(band + d, bands), lax.rem(band + bands - d, bands)
    return jnp.where(band < to, 1, 0), jnp.where(source < band, 1, 0)


def late_kernel(keep, sibling, *outs):
    half = keep.shape[0] // 2
    for d, out in enumerate(outs, 1):
        upper, _ = halves_met(d)
        for t, whole in enumerate((keep, sibling)):
            out[t] = whole[pl.ds((1 - upper) * half, half)]


def slot_orbitals(bands):
    core, _, _ = place()
    band = lax.axis_index("band")
    names = []
    for d in range(bands):
        group = lax.rem(band + bands - d, bands)
        names += [2 * group + core, 2 * group + 1 - core]
    return names


def correlation_kernel(*refs):
    bands = lax.axis_size("band")
    own, early, out = refs[:2], refs[2:-1], refs[-1]
    names = slot_orbitals(bands)
    row = lax.broadcasted_iota(jnp.int32, (8, LANES), 0)
    column = lax.broadcasted_iota(jnp.int32, (8, LANES), 1)
    pairs = [(0, 0), (0, 1), (1, 1)] + [(i, 2 * d + j) for d in range(1, bands) for i in range(2) for j in range(2)]
    width, height, depth = own[0].shape
    half = width // 2

    def summed_up(value):
        total = jnp.sum(value, axis=0)
        return sum(total[:, k * LANES : (k + 1) * LANES] for k in range(depth // LANES))

    def body(index, totals):
        def planes(ref, upper):
            return ref[pl.ds(upper * half + index * PLANES, PLANES)]

        halves = [[planes(ref, upper) for ref in own] for upper in range(2)]
        found = []
        for (i, j), total in zip(pairs, totals):
            if j < 2:
                total = total + summed_up(halves[0][i] * halves[0][j] + halves[1][i] * halves[1][j])
            else:
                _, upper = halves_met(j // 2)
                total = total + summed_up(planes(own[i], upper) * planes(early[j - 2], 0))
            found.append(total)
        return tuple(found)

    zero = jnp.zeros((height, LANES), jnp.float32)
    totals = lax.fori_loop(0, half // PLANES, body, (zero,) * len(pairs))
    result = jnp.zeros((8, LANES), jnp.float32)
    for (i, j), total in zip(pairs, totals):
        here = ((row == names[i]) & (column == names[j])) | ((row == names[j]) & (column == names[i]))
        result = jnp.where(here, jnp.sum(total), result)
    out[...] = result


def basis_kernel(bands, cells, *refs):
    correlation, order = refs[:2]
    early, late = refs[4 : 2 + 2 * bands], refs[2 + 2 * bands : 1 + 3 * bands]
    out, mixing = refs[1 + 3 * bands : 3 + 3 * bands]
    joined = refs[3 + 3 * bands :]
    slots = list(refs[2:4]) + list(joined)
    for d in range(1, bands):
        _, upper = halves_met(d)
        for t in range(2):
            whole = joined[2 * d - 2 + t]
            half = whole.shape[0] // 2
            whole[pl.ds(upper * half, half)] = early[2 * d - 2 + t][...]
            whole[pl.ds((1 - upper) * half, half)] = late[d - 1][t]
    names = slot_orbitals(bands)
    count = 2 * bands
    band = lax.axis_index("band")

    def splat(value):
        return jnp.full((8, LANES), value, jnp.float32)

    at = [order[p] for p in range(count)]
    mixing[...] = jnp.zeros_like(mixing)
    lower = {}
    inverse_diagonal = []
    for j in range(count):
        for i in range(j, count):
            total = splat(correlation[at[i], at[j]]) * (1.0 / cells)
            for k in range(j):
                total = total - lower[i, k] * lower[j, k]
            if i == j:
                diagonal = jnp.sqrt(total)
                inverse_diagonal.append(1.0 / diagonal)
            else:
                lower[i, j] = total * inverse_diagonal[j]
    inverse = {}
    for j in range(count):
        inverse[j, j] = inverse_diagonal[j]
        for i in range(j + 1, count):
            total = lower[i, j] * inverse[j, j]
            for k in range(j + 1, i):
                total = total + lower[i, k] * inverse[k, j]
            inverse[i, j] = -total * inverse_diagonal[i]
    for (i, j), value in inverse.items():
        mixing[at[i], at[j]] = value
    width, _, depth = slots[0].shape
    for r in range(2):
        factors = [mixing[2 * band + r, name] for name in names]

        def body(x, carry, r=r, factors=factors):
            for half in range(depth // LANES):
                lanes = slice(half * LANES, (half + 1) * LANES)
                total = factors[0] * slots[0][x, :, lanes]
                for factor, slot in zip(factors[1:], slots[1:]):
                    total = total + factor * slot[x, :, lanes]
                out[r, x, :, lanes] = total
            return carry

        lax.fori_loop(0, width, body, 0, unroll=4)


def partner(position, phase, count):
    other = position + 1 if position % 2 == phase else position - 1
    return other if 0 <= other < count else None


def meet(value, x_phase=None, y_phase=None):
    nx, ny = lax.axis_size("gx"), lax.axis_size("gy")
    pairs = []
    for x in range(nx):
        for y in range(ny):
            to_x = x if x_phase is None else partner(x, x_phase, nx)
            chip = y // 2 if y_phase is None else partner(y // 2, y_phase, ny // 2)
            if to_x is None or chip is None:
                pairs.append((x * ny + y, x * ny + (y ^ 1)))
            else:
                pairs.append((x * ny + y, to_x * ny + chip * 2 + y % 2))
    return lax.ppermute(value, ("gx", "gy"), pairs)


def swap(value):
    count = lax.axis_size("gy")
    return lax.ppermute(value, "gy", [(y, y ^ 1) for y in range(count)])


def to_band(value, d, crossed=False):
    bands = lax.axis_size("band")
    pairs = []
    for y in range(lax.axis_size("gy")):
        for band in range(bands):
            pairs.append((y * bands + band, (y ^ crossed) * bands + (band + d) % bands))
    return lax.ppermute(value, ("gy", "band"), pairs)


def exchange(payloads):
    count = len(y_phases())
    halos = [meet(payloads[phase], y_phase=phase) for phase in y_phases()]
    halos += [meet(payloads[count + phase], x_phase=phase) for phase in range(2)]
    for y_phase in y_phases():
        for x_phase in range(2):
            halos.append(meet(payloads[count + 2 + 2 * y_phase + x_phase], x_phase, y_phase))
    return halos


def summed(value, axis):
    count = lax.axis_size(axis)
    if count & (count - 1):
        return lax.psum(value, axis)

    def of(step):
        return lax.ppermute(value, axis, [(i, i ^ step) for i in range(count)])

    if count == 4:
        return (value + of(1)) + (of(2) + of(3))
    step = 1
    while step < count:
        value = value + of(step)
        step *= 2
    return value


def per_device(orbitals, potential, order):
    group, width, height, depth = orbitals.shape
    bands = lax.axis_size("band")
    cells = float(width * lax.axis_size("gx") * height * lax.axis_size("gy") * depth)
    count = len(y_phases())
    window = struct(2, width + 2 * HALO, 32 + 2 * PAD, LANES)
    windows = STEPS + 1

    received = swap(orbitals)
    received_potential = swap(potential)
    tile = (width, height, depth)
    fields = lax.concatenate([orbitals, potential[None]], 0)

    def payloads(in_y, in_x, in_corner):
        return (
            [struct(in_y, height, depth)] * count
            + [struct(2, in_x, height, depth)] * 2
            + [struct(in_corner, height, depth)] * (2 * count)
        )

    *packed, = pl.pallas_call(
        pack_kernel,
        out_shape=[struct(width // 2 + width // SPLIT, height, depth)] * count
        + payloads(width - width // SPLIT, 2 * HALO - 2, HALO - 1),
        in_specs=[VMEM] * 3,
        out_specs=[VMEM] * (2 + 4 * count),
        compiler_params=PARAMS,
        name="pack",
    )(fields, received, received_potential)
    came = [meet(packed[phase], y_phase=phase) for phase in y_phases()]
    packed[-1], came = lax.optimization_barrier((packed[-1], came))
    y_halos, x_halos, corners = halos_of(exchange(packed[count:]))
    passed = [swap(value[: width // 2]) for value in came]
    *levels, local = pl.pallas_call(
        first_own_kernel,
        out_shape=[window] * (windows + 1),
        in_specs=[VMEM] * 5,
        out_specs=[VMEM] * (windows + 1),
        compiler_params=PARAMS,
        name="first_own",
    )(fields, received, received_potential, *x_halos)
    outs = pl.pallas_call(
        first_rest_kernel,
        out_shape=[window] * (windows + 1) + payloads(width, HALO, HALO // 2),
        in_specs=[VMEM] * (windows + 1 + 5 * count),
        out_specs=[VMEM] * (windows + 3 + 3 * count),
        input_output_aliases={k: k for k in range(windows + 1)},
        compiler_params=PARAMS,
        name="first_rest",
    )(*levels, local, *came, *passed, *y_halos, *corners)
    levels, local, packed = outs[:windows], outs[windows], outs[windows + 1 :]
    y_halos, x_halos, corners = halos_of(exchange(packed))
    levels = pl.pallas_call(
        second_own_kernel,
        out_shape=[window] * windows,
        in_specs=[VMEM] * 4,
        out_specs=[VMEM] * windows,
        compiler_params=PARAMS,
        name="second_own",
    )(levels[STEPS], local, *x_halos)
    half = (width // 2, height, depth)
    outs = pl.pallas_call(
        second_rest_kernel,
        out_shape=[window] * windows + [struct(*tile)] * 2 + [struct(*half)] * (2 * bands - 2),
        in_specs=[VMEM] * (windows + 3 + 3 * count),
        out_specs=[VMEM] * (windows + 2 * bands),
        input_output_aliases={k: k for k in range(windows)},
        compiler_params=PARAMS,
        name="second_rest",
    )(*levels, local, fields, received, *y_halos, *corners)
    keep, give, *early = outs[windows:]

    early = [to_band(value, 1 + k // 2, crossed=k % 2 == 1) for k, value in enumerate(early)]
    sibling = swap(give)
    late = pl.pallas_call(
        late_kernel,
        out_shape=[struct(2, *half)] * (bands - 1),
        in_specs=[VMEM] * 2,
        out_specs=[VMEM] * (bands - 1),
        compiler_params=PARAMS,
        name="late",
    )(keep, sibling)
    late = [to_band(value, d) for d, value in enumerate(late, 1)]
    partial_value = pl.pallas_call(
        correlation_kernel,
        out_shape=struct(8, LANES),
        in_specs=[VMEM] * (2 * bands),
        out_specs=VMEM,
        compiler_params=PARAMS,
        name="correlation",
    )(keep, sibling, *early)
    correlation = summed(summed(summed(partial_value, "band"), "gy"), "gx")
    return pl.pallas_call(
        functools.partial(basis_kernel, bands, cells),
        out_shape=struct(*orbitals.shape),
        in_specs=[SMEM, SMEM] + [VMEM] * (3 * bands - 1),
        out_specs=VMEM,
        scratch_shapes=[pltpu.VMEM((2 * bands, 2 * bands, 8, LANES), jnp.float32)]
        + [pltpu.VMEM(tile, jnp.float32)] * (2 * bands - 2),
        compiler_params=PARAMS,
        name="basis",
    )(correlation, order, keep, sibling, *early, *late)


def solution(mesh):
    in_specs = (P("band", "gx", "gy", None), P("gx", "gy", None), P())
    out_specs = P("band", "gx", "gy", None)
    return jax.shard_map(
        per_device, mesh=mesh, in_specs=in_specs, out_specs=out_specs, check_vma=False
    )
```
